256 devices in a mesh: dp: 8 (over y, x_hi), seq: 32 (over z, x_lo, core).
Axes of the slice: x: 4 (x_hi: 2, x_lo: 2; x = x_hi * 2 + x_lo), y: 4, z: 8, core: 2. Of those that a mesh axis runs over, the one named last changes fastest.
Arguments:
- inputs_x: bfloat16 [8, 4096, 3072], P('dp', 'seq'), may hold values from -0.046875 to 0.046875
- queries: bfloat16 [8, 4096, 4096], P('dp', 'seq'), may hold values from -6 to 6
- keys: bfloat16 [8, 4096, 4096], P('dp', 'seq'), may hold values from -1.25 to 1.25
- values: bfloat16 [8, 4096, 4096], P('dp', 'seq'), may hold values from -1.25 to 1.25
- grad_out: bfloat16 [8, 4096, 4096], P('dp', 'seq'), may hold values from -0.0625 to 0.0625
- decay_exp: int32 [32], P('seq'), may hold values from 0 to 7
- state_in: float32 [8, 32, 128, 128], P('dp', 'seq'), may hold values from -12 to 12
Outputs:
- grad_queries: bfloat16 [8, 4096, 4096], P('dp', 'seq')
- grad_keys: bfloat16 [8, 4096, 4096], P('dp', 'seq')
- grad_values: bfloat16 [8, 4096, 4096], P('dp', 'seq')
- weight_grads: float32 [2, 32, 768, 512], P(None, 'seq', 'dp')
- state_grad: float32 [8, 32, 128, 128], P('dp', 'seq')
The draws below stay inside these ranges and needn't reach their ends.
All inputs are finite; a program needn't handle non-finite values.
Results may differ from the reference program's by a relative error of at most 0.0029.
Values may be sent and summed in bfloat16 or wider, within the bound.
No kernel may reach another device: no remote copies, remote signals or barrier semaphores. Data moves between devices by JAX's collectives and lax.ppermute only.
A program may use at most 128 MiB of HBM per device.

```python
import jax
import jax.numpy as jnp
from jax import lax

D = 3072
HEADS = 32
HEAD_DIM = 128
BLOCK = 256
ROW_GROUPS = 4
LENGTH = 4096
BATCH = 8
ALL_TOKENS = 32768
HD = 4096
COL_GROUPS = 8
N_SEQ = 32


def draw_decay_exp(key, part):
    key = jax.random.fold_in(key, 11)
    first, second, third, fourth = jax.random.split(key, 4)
    slower = jax.random.randint(first, (HEADS,), 0, 2)
    faster = jax.random.randint(second, (HEADS,), 2, 8)
    picked = jax.random.randint(third, (HEADS,), 0, 2)
    result = jnp.where(picked == 0, slower, faster)
    order = jax.random.permutation(fourth, HEADS)
    result = result.at[order[0]].set(7).at[order[1]].set(0)
    return result.astype(jnp.int32)


def strengthened(drawn, own_key, source, target, parts, factor):
    def block_of(position):
        return (jnp.arange(drawn.shape[position]) // (drawn.shape[position] // parts)).reshape((-1,) + (1,) * (drawn.ndim - 1 - position))

    first = jax.random.permutation(own_key, parts)[block_of(target)]
    far = (block_of(target) + parts // 2) % parts
    return jnp.where((block_of(source) == first) | (block_of(source) == far), factor * drawn, drawn)


def block_scale(own_key, shape, cuts, least, largest):
    def one(dim, blocks):
        steps = jax.random.uniform(jax.random.fold_in(jax.random.fold_in(own_key, 6), dim), (blocks,), jnp.float32, least / len(cuts), largest / len(cuts))
        return jnp.repeat(jnp.exp(steps), shape[dim] // blocks).reshape((-1,) + (1,) * (len(shape) - dim - 1))

    loudness = one(*cuts[0])
    for cut in cuts[1:]:
        loudness = loudness * one(*cut)
    return loudness


def bell_draw(stream_key, dims, deviation, limit, cuts=(), kind=jnp.bfloat16):
    factor_of = block_scale(stream_key, dims, cuts, -0.22, 0.18) if cuts else 1.0
    array = jax.random.normal(stream_key, dims, jnp.float32) * deviation * factor_of
    return jnp.minimum(jnp.maximum(array, -limit), limit).astype(kind)


def noise_with(rng, dims, deviation, reach, cuts, heavy, held_as=jnp.bfloat16):
    array = deviation * jax.random.normal(rng, dims, jnp.float32)
    if cuts:
        array = array * block_scale(rng, dims, cuts, -0.22, 0.18)
    return jnp.clip(strengthened(array, jax.random.fold_in(rng, 3), *heavy), -reach, reach).astype(held_as)


def setup_inputs(seed: int = 0) -> dict:
    streams_of = jax.random.split(jax.random.key(seed), 8)
    inputs_x = noise_with(streams_of[0], (BATCH, LENGTH, D), ALL_TOKENS ** -0.5, 0.046875, ((0, 8), (1, 32)), (0, 2, 8, 2.0))
    queries = bell_draw(streams_of[1], (BATCH, LENGTH, HD), 1.0, 6.0, ((0, 8), (1, 32)))
    keys = bell_draw(streams_of[2], (BATCH, LENGTH, HD), 0.2, 1.25, ((0, 8), (1, 32)))
    values = bell_draw(streams_of[3], (BATCH, LENGTH, HD), 0.2, 1.25, ((0, 8), (1, 32)))
    grad_out = bell_draw(streams_of[4], (BATCH, LENGTH, HD), 0.01, 0.0625, ((0, 8), (1, 32)))
    decay_exp = draw_decay_exp(jax.random.fold_in(streams_of[7], 71), 0)
    state_in = bell_draw(streams_of[6], (BATCH, HEADS, HEAD_DIM, HEAD_DIM), 2.0, 12.0, ((0, 8), (1, 32)), jnp.float32)
    return {"inputs_x": inputs_x, "queries": queries, "keys": keys, "values": values, "grad_out": grad_out, "decay_exp": decay_exp, "state_in": state_in}


exact_mode = lax.Precision.HIGHEST


def rates(decay_exp, length):
    return -jnp.power(2.0, decay_exp.astype(jnp.float32)) / length


def head_backward(query_blocks, key_blocks, value_blocks, grad_blocks, log_rate, state_first):
    offsets = jnp.arange(BLOCK, dtype=jnp.float32)
    spread = offsets[:, None] - offsets[None, :]
    lower = jnp.where(spread >= 0.0, jnp.exp(log_rate * jnp.maximum(spread, 0.0)), 0.0)
    whole_decay = jnp.exp(log_rate * BLOCK)
    forward_w = key_blocks * jnp.exp(log_rate * (BLOCK - 1.0 - offsets))[:, None]
    forward_up = jnp.einsum("bia,bic->bac", forward_w, value_blocks, precision=exact_mode)
    reverse_w = query_blocks * jnp.exp(log_rate * offsets)[:, None]
    reverse_up = jnp.einsum("bja,bjc->bac", reverse_w, grad_blocks, precision=exact_mode)

    def advance(state, update):
        return whole_decay * state + update, state

    unused, forward = lax.scan(advance, state_first, forward_up)
    first_state, later = lax.scan(advance, jnp.zeros_like(state_first), reverse_up, reverse=True)
    head_scale = jnp.exp(log_rate * (offsets + 1.0))[:, None]
    tail_scale = jnp.exp(log_rate * (BLOCK - offsets))[:, None]
    grad_scores = jnp.einsum("bja,bia->bji", grad_blocks, value_blocks, precision=exact_mode) * lower
    key_scores = jnp.einsum("bja,bia->bji", query_blocks, key_blocks, precision=exact_mode) * lower
    grad_query = head_scale * jnp.einsum("bja,bca->bjc", grad_blocks, forward, precision=exact_mode)
    grad_query = grad_query + jnp.einsum("bji,bic->bjc", grad_scores, key_blocks, precision=exact_mode)
    grad_key = tail_scale * jnp.einsum("bia,bca->bic", value_blocks, later, precision=exact_mode)
    grad_key = grad_key + jnp.einsum("bji,bjc->bic", grad_scores, query_blocks, precision=exact_mode)
    grad_value = tail_scale * jnp.einsum("bia,bac->bic", key_blocks, later, precision=exact_mode)
    grad_value = grad_value + jnp.einsum("bji,bjc->bic", key_scores, grad_blocks, precision=exact_mode)
    return grad_query, grad_key, grad_value, jnp.exp(log_rate) * first_state


def reference(inputs_x, queries, keys, values, grad_out, decay_exp, state_in):
    length = queries.shape[1]
    head_count = decay_exp.shape[0]
    head_width = queries.shape[2] // head_count
    log_rate = rates(decay_exp, length)

    def split(tensor):
        blocked = tensor.astype(jnp.float32).reshape(length // BLOCK, BLOCK, head_count, head_width)
        return blocked.transpose(2, 0, 1, 3)

    def join(tensor):
        return tensor.transpose(1, 2, 0, 3).reshape(length, head_count * head_width).astype(jnp.bfloat16)

    def one_sequence(members):
        query_seq, key_seq, value_seq, grad_seq, state_seq = members

        def one_head(head_members):
            return head_backward(*head_members)

        grad_query, grad_key, grad_value, state_grad = lax.map(
            one_head, (split(query_seq), split(key_seq), split(value_seq), split(grad_seq), log_rate, state_seq))
        return join(grad_query), join(grad_key), join(grad_value), state_grad

    grad_queries, grad_keys, grad_values, state_grad = lax.map(
        one_sequence, (queries, keys, values, grad_out, state_in))

    def accumulate(total, members):
        x_rows, key_grads, value_grads = members
        first = jnp.dot(x_rows.T, key_grads, preferred_element_type=jnp.float32)
        second = jnp.dot(x_rows.T, value_grads, preferred_element_type=jnp.float32)
        return total + jnp.stack((first, second)), None

    total, unused = lax.scan(accumulate, jnp.zeros((2, D, HD), jnp.float32), (inputs_x, grad_keys, grad_values))
    blocks = total.reshape(2, ROW_GROUPS, D // ROW_GROUPS, COL_GROUPS, HD // COL_GROUPS)
    weight_grads = blocks.transpose(0, 1, 3, 2, 4).reshape(2, N_SEQ, D // ROW_GROUPS, HD // COL_GROUPS)
    return grad_queries, grad_keys, grad_values, weight_grads, state_grad
```

```python
import functools

import jax
import jax.numpy as jnp
from jax import lax
from jax.experimental import pallas as pl
from jax.experimental.pallas import tpu as pltpu
from jax.sharding import Mesh
from jax.sharding import PartitionSpec as P

WIDTH = 128
f32 = jnp.float32
bf16 = jnp.bfloat16
PLANE = ("y", "xh", "xl", "core")
QUAD = ("xl", "core")
CHAIN = ("z", "xl", "core")


def log_rate(exponent, length):
    return -(jnp.left_shift(1, exponent).astype(f32)) * (1.0 / length)


def power_of(rate, steps):
    return jnp.exp(jnp.full((1, WIDTH), rate * steps, f32))


def halves(wide):
    high = wide.astype(bf16)
    return high, (wide - high.astype(f32)).astype(bf16)


def dot(left, right, dims):
    return lax.dot_general(left, right, (dims, ((), ())), preferred_element_type=f32)


def update_kernel(exp_ref, left_ref, right_ref, out_ref, *, reverse, length):
    group = pl.program_id(0)
    span = left_ref.shape[0]
    rows = lax.broadcasted_iota(jnp.int32, (span, WIDTH), 0).astype(f32)
    steps = rows if reverse else (span - 1.0) - rows
    for slot in range(4):
        rate = log_rate(exp_ref[4 * group + slot], length)
        lanes = pl.ds(slot * WIDTH, WIDTH)
        high, low = halves(left_ref[:, lanes].astype(f32) * jnp.exp(rate * steps))
        right = right_ref[:, lanes]
        out_ref[slot, 0] = dot(
            jnp.concatenate((high, low), 0), jnp.concatenate((right, right), 0), ((0,), (0,))
        )


def join_kernel(exp_ref, slot_ref, parts_ref, out_ref, *, reverse, length, span):
    rate = log_rate(exp_ref[4 * pl.program_id(0) + slot_ref[0]], length)
    decay = power_of(rate, span)
    order = (3, 2, 1, 0) if reverse else (0, 1, 2, 3)
    total = parts_ref[order[0], 0]
    for item in order[1:]:
        total = decay * total + parts_ref[item, 0]
    out_ref[0] = total


def scan_forward_kernel(exp_ref, first_ref, parts_ref, out_ref, *, length, span):
    decay = power_of(log_rate(exp_ref[0], length), span)
    state = first_ref[...]
    for item in range(parts_ref.shape[0]):
        out_ref[item] = state
        state = decay * state + parts_ref[item]


def scan_reverse_kernel(exp_ref, parts_ref, out_ref, grad_ref, *, length, span):
    rate = log_rate(exp_ref[0], length)
    decay = power_of(rate, span)
    state = jnp.zeros(parts_ref.shape[1:], f32)
    for item in reversed(range(parts_ref.shape[0])):
        out_ref[item] = state
        state = decay * state + parts_ref[item]
    grad_ref[...] = power_of(rate, 1.0) * state


def spread_kernel(exp_ref, slot_ref, parts_ref, edge_ref, out_ref, *, reverse, length, span):
    rate = log_rate(exp_ref[4 * pl.program_id(0) + slot_ref[0]], length)
    decay = power_of(rate, span)
    state = edge_ref[0]
    for item in (3, 2, 1, 0) if reverse else (0, 1, 2, 3):
        out_ref[item, 0] = state
        state = decay * state + parts_ref[item, 0]


def key_value_kernel(
    exp_ref, query_ref, key_ref, value_ref, grad_ref, later_ref, gk_ref, gv_ref, send_ref, *, length
):
    group = pl.program_id(0)
    span = query_ref.shape[0]
    source = lax.broadcasted_iota(jnp.int32, (span, span), 0)
    target = lax.broadcasted_iota(jnp.int32, (span, span), 1)
    gap = (target - source).astype(f32)
    left = span - lax.broadcasted_iota(jnp.int32, (span, WIDTH), 0).astype(f32)
    for slot in range(4):
        rate = log_rate(exp_ref[4 * group + slot], length)
        lanes = pl.ds(slot * WIDTH, WIDTH)
        query, key = query_ref[:, lanes], key_ref[:, lanes]
        value, grad = value_ref[:, lanes], grad_ref[:, lanes]
        mask = jnp.where(gap >= 0.0, jnp.exp(rate * jnp.maximum(gap, 0.0)), 0.0)
        tail = jnp.exp(rate * left)
        grad_scores = jnp.concatenate(halves(dot(value, grad, ((1,), (1,))) * mask), 1)
        key_scores = jnp.concatenate(halves(dot(key, query, ((1,), (1,))) * mask), 1)
        high, low = halves(later_ref[slot, 0])
        gk = tail * dot(
            jnp.concatenate((value, value), 1), jnp.concatenate((high, low), 1), ((1,), (1,))
        )
        gk = gk + dot(grad_scores, jnp.concatenate((query, query), 0), ((1,), (0,)))
        gv = tail * dot(
            jnp.concatenate((key, key), 1), jnp.concatenate((high, low), 0), ((1,), (0,))
        )
        gv = gv + dot(key_scores, jnp.concatenate((grad, grad), 0), ((1,), (0,)))
        gk_ref[:, lanes] = gk.astype(bf16)
        gv_ref[:, lanes] = gv.astype(bf16)
        send_ref[slot, 0] = gk.astype(bf16)
        send_ref[4 + slot, 0] = gv.astype(bf16)


def query_kernel(exp_ref, key_ref, value_ref, grad_ref, state_ref, gq_ref, *, length):
    group = pl.program_id(0)
    span = key_ref.shape[0]
    target = lax.broadcasted_iota(jnp.int32, (span, span), 0)
    source = lax.broadcasted_iota(jnp.int32, (span, span), 1)
    gap = (target - source).astype(f32)
    done = 1.0 + lax.broadcasted_iota(jnp.int32, (span, WIDTH), 0).astype(f32)
    for slot in range(4):
        rate = log_rate(exp_ref[4 * group + slot], length)
        lanes = pl.ds(slot * WIDTH, WIDTH)
        key, value, grad = key_ref[:, lanes], value_ref[:, lanes], grad_ref[:, lanes]
        mask = jnp.where(gap >= 0.0, jnp.exp(rate * jnp.maximum(gap, 0.0)), 0.0)
        scores = jnp.concatenate(halves(dot(grad, value, ((1,), (1,))) * mask), 1)
        high, low = halves(state_ref[slot, 0])
        gq = jnp.exp(rate * done) * dot(
            jnp.concatenate((grad, grad), 1), jnp.concatenate((high, low), 1), ((1,), (1,))
        )
        gq = gq + dot(scores, jnp.concatenate((key, key), 0), ((1,), (0,)))
        gq_ref[:, lanes] = gq.astype(bf16)


def weight_kernel(cols_ref, rows_ref, out_ref, turned):
    @pl.when(pl.program_id(0) == 0)
    def _():
        turned[...] = cols_ref[...].T

    product = dot(turned[...], rows_ref[...], ((1,), (0,))).T
    out_ref[0] = product[:, :WIDTH]
    out_ref[1] = product[:, WIDTH:]


SMEM = pl.BlockSpec(memory_space=pltpu.SMEM)


def call(kernel, grid, in_specs, out_specs, out_shape, args, scratch=(), name=None):
    return pl.pallas_call(
        kernel,
        grid=grid,
        in_specs=in_specs,
        out_specs=out_specs,
        out_shape=out_shape,
        scratch_shapes=scratch,
        name=name,
        compiler_params=pltpu.CompilerParams(vmem_limit_bytes=48 * 1024 * 1024),
    )(*args)


def per_device(inputs_x, queries, keys, values, grad_out, decay_exp, state_in):
    span = queries.shape[1]
    features = queries.shape[2]
    groups = features // (4 * WIDTH)
    depth = lax.axis_size("z")
    length = span * lax.axis_size(CHAIN)
    tile = (WIDTH, WIDTH)
    query, key, value, grad = queries[0], keys[0], values[0], grad_out[0]
    exps = lax.all_gather(decay_exp, CHAIN, axis=0, tiled=True)
    slot = lax.axis_index(QUAD).astype(jnp.int32)[None]
    rows = lax.all_gather(inputs_x[0], PLANE, axis=0, tiled=True)

    head_cols = pl.BlockSpec((span, 4 * WIDTH), lambda i: (0, i))
    quad_tiles = pl.BlockSpec((4, 1) + tile, lambda i: (0, i, 0, 0))
    one_tile = pl.BlockSpec((1,) + tile, lambda i: (i, 0, 0))
    quad_shape = jax.ShapeDtypeStruct((4, groups) + tile, f32)
    line_shape = jax.ShapeDtypeStruct((groups,) + tile, f32)
    token_shape = jax.ShapeDtypeStruct((span, features), bf16)

    def exchange(array, axes):
        return lax.all_to_all(array, axes, split_axis=0, concat_axis=0, tiled=True)

    def updates(left, right, reverse):
        return call(
            functools.partial(update_kernel, reverse=reverse, length=length),
            (groups,), [SMEM, head_cols, head_cols], quad_tiles, quad_shape, (exps, left, right),
            name="updates",
        )

    def joined(parts, reverse):
        return call(
            functools.partial(join_kernel, reverse=reverse, length=length, span=span),
            (groups,), [SMEM, SMEM, quad_tiles], one_tile, line_shape, (exps, slot, parts),
            name="joined",
        )

    def spread(parts, edge, reverse):
        return call(
            functools.partial(spread_kernel, reverse=reverse, length=length, span=span),
            (groups,), [SMEM, SMEM, quad_tiles, one_tile], quad_tiles, quad_shape,
            (exps, slot, parts, edge), name="spread",
        )

    whole = pl.BlockSpec((depth,) + tile, lambda: (0, 0, 0))
    single = pl.BlockSpec(tile, lambda: (0, 0))

    reverse_parts = exchange(updates(query, grad, True), QUAD)
    reverse_groups = exchange(joined(reverse_parts, True), "z")
    reverse_edges, state_grad = call(
        functools.partial(scan_reverse_kernel, length=length, span=4.0 * span),
        (), [SMEM, whole], [whole, single],
        [line_shape, jax.ShapeDtypeStruct(tile, f32)], (decay_exp, reverse_groups), name="scan",
    )
    reverse_edges = exchange(reverse_edges, "z")
    later = exchange(spread(reverse_parts, reverse_edges, True), QUAD)
    grad_key, grad_value, send = call(
        functools.partial(key_value_kernel, length=length),
        (groups,), [SMEM] + 4 * [head_cols] + [quad_tiles],
        [head_cols, head_cols, pl.BlockSpec((8, 1, span, WIDTH), lambda i: (0, i % 4, 0, i // 4))],
        [token_shape, token_shape, jax.ShapeDtypeStruct((8, 4, span, 2 * WIDTH), bf16)],
        (exps, query, key, value, grad, later), name="key_value",
    )
    cols = exchange(send.reshape(32, span, 2 * WIDTH), PLANE).reshape(32 * span, 2 * WIDTH)

    forward_parts = exchange(updates(key, value, False), QUAD)
    forward_groups = exchange(joined(forward_parts, False), "z")
    forward_edges = call(
        functools.partial(scan_forward_kernel, length=length, span=4.0 * span),
        (), [SMEM, single, whole], whole, line_shape,
        (decay_exp, state_in[0, 0], forward_groups), name="scan",
    )
    forward_edges = exchange(forward_edges, "z")
    states = exchange(spread(forward_parts, forward_edges, False), QUAD)
    grad_query = call(
        functools.partial(query_kernel, length=length),
        (groups,), [SMEM] + 3 * [head_cols] + [quad_tiles], head_cols, token_shape,
        (exps, key, value, grad, states), name="query",
    )

    tokens, width = rows.shape
    block = width // 4
    partial = call(
        weight_kernel, (4,),
        [pl.BlockSpec((tokens, 2 * WIDTH), lambda i: (0, 0)), pl.BlockSpec((tokens, block), lambda i: (0, i))],
        pl.BlockSpec((2, block, WIDTH), lambda i: (i, 0, 0)),
        jax.ShapeDtypeStruct((8, block, WIDTH), f32),
        (cols, rows), scratch=[pltpu.VMEM((2 * WIDTH, tokens), bf16)], name="weight",
    )
    summed = lax.psum_scatter(partial, "z", scatter_dimension=0, tiled=True)
    pieces = exchange(summed.reshape(8, block // 8, WIDTH), ("y", "xh"))
    pieces = pieces.reshape(2, 4, block // 8, WIDTH).transpose(0, 2, 1, 3)
    weight_grads = pieces.reshape(2, 1, block // 8, 4 * WIDTH)
    return (
        grad_query[None], grad_key[None], grad_value[None], weight_grads, state_grad[None, None]
    )


def solution(mesh):
    fine = Mesh(mesh.devices.reshape(4, 2, 8, 2, 2), ("y", "xh", "z", "xl", "core"))
    dp, seq = ("y", "xh"), CHAIN
    tokens = P(dp, seq, None)
    in_specs = (tokens, tokens, tokens, tokens, tokens, P(seq), P(dp, seq, None, None))
    out_specs = (tokens, tokens, tokens, P(None, seq, dp, None), P(dp, seq, None, None))
    return jax.shard_map(
        per_device, mesh=fine, in_specs=in_specs, out_specs=out_specs, check_vma=False
    )
```

```python
import functools

import jax
import jax.numpy as jnp
from jax import lax
from jax.experimental import pallas as pl
from jax.experimental.pallas import tpu as pltpu
from jax.sharding import Mesh
from jax.sharding import PartitionSpec as P

WIDTH = 128
f32 = jnp.float32
bf16 = jnp.bfloat16
PLANE = ("y", "xh", "xl", "core")
QUAD = ("xl", "core")
CHAIN = ("z", "xl", "core")


def log_rate(exponent, length):
    return -(jnp.left_shift(1, exponent).astype(f32)) * (1.0 / length)


def power_of(rate, steps):
    return jnp.exp(jnp.full((1, WIDTH), rate * steps, f32))


def halves(wide):
    high = wide.astype(bf16)
    return high, (wide - high.astype(f32)).astype(bf16)


def dot(left, right, dims):
    return lax.dot_general(left, right, (dims, ((), ())), preferred_element_type=f32)


def update_kernel(here_ref, exp_ref, left_ref, right_ref, keep_ref, send_ref, *, reverse, length):
    group = pl.program_id(0)
    span = left_ref.shape[0]
    rows = lax.broadcasted_iota(jnp.int32, (span, WIDTH), 0).astype(f32)
    steps = rows if reverse else (span - 1.0) - rows
    for slot in range(4):
        rate = log_rate(exp_ref[4 * group + slot], length)
        lanes = pl.ds(slot * WIDTH, WIDTH)
        high, low = halves(left_ref[:, lanes].astype(f32) * jnp.exp(rate * steps))
        right = right_ref[:, lanes]
        update = dot(
            jnp.concatenate((high, low), 0), jnp.concatenate((right, right), 0), ((0,), (0,))
        )
        chip = jnp.bitwise_xor(here_ref[1], slot // 2)

        @pl.when(here_ref[2] == slot % 2)
        def _(update=update, chip=chip):
            keep_ref[0, chip] = update

        @pl.when(here_ref[2] != slot % 2)
        def _(update=update, chip=chip):
            send_ref[0, chip] = update


def weighed(mine, other, position, reverse, rate, span):
    position = position.astype(f32)
    later = position if reverse else 1.0 - position
    return power_of(rate, span * later) * mine + power_of(rate, span * (1.0 - later)) * other


def chip_kernel(
    here_ref, exp_ref, mine_ref, other_ref, after_ref, keep_ref, send_ref,
    *, reverse, length, span
):
    group = pl.program_id(0)
    for chip, out_ref in enumerate((keep_ref, send_ref)):
        head = 4 * group + 2 * jnp.bitwise_xor(here_ref[1], chip) + here_ref[2]
        rate = log_rate(exp_ref[head], length)
        out_ref[0] = weighed(
            mine_ref[0, chip], other_ref[0, chip], here_ref[2], reverse, rate, span
        )


def quad_kernel(here_ref, exp_ref, mine_ref, other_ref, out_ref, *, length, span):
    for group in range(out_ref.shape[0]):
        rate = log_rate(exp_ref[4 * group + 2 * here_ref[1] + here_ref[2]], length)
        out_ref[group] = weighed(
            mine_ref[group], other_ref[group], here_ref[1], True, rate, span
        )


def turn_kernel(
    here_ref, exp_ref, own_ref, parts_ref, mine_ref, other_ref, out_ref, grad_ref, *, length, span
):
    rate = log_rate(own_ref[0], length)
    decay = power_of(rate, 2.0 * span)
    state = jnp.zeros(grad_ref.shape, f32)
    for group in reversed(range(parts_ref.shape[0])):
        out_ref[group, 0] = state
        state = decay * state + parts_ref[group]
    grad_ref[...] = power_of(rate, 1.0) * state
    for group in range(parts_ref.shape[0]):
        rate = log_rate(exp_ref[4 * group + 2 * here_ref[1] + here_ref[2]], length)
        out_ref[group, 1] = weighed(
            mine_ref[group], other_ref[group], here_ref[1], False, rate, span
        )


def scan_kernel(own_ref, parts_ref, first_ref, after_ref, out_ref, *, length, span):
    decay = power_of(log_rate(own_ref[0], length), span)
    state = first_ref[...]
    for group in range(parts_ref.shape[0]):
        out_ref[group, 0] = state
        state = decay * state + parts_ref[group, 0]


def chip_state_kernel(
    here_ref, exp_ref, edge_ref, mine_ref, other_ref, keep_ref, send_ref, *, reverse, length, span
):
    behind = here_ref[1] == (0 if reverse else 1)
    for group in range(edge_ref.shape[0]):
        rate = log_rate(exp_ref[4 * group + 2 * here_ref[1] + here_ref[2]], length)
        edge = edge_ref[group, 0]
        past = power_of(rate, span) * edge
        keep_ref[group] = jnp.where(behind, past + other_ref[group], edge)
        send_ref[group] = jnp.where(behind, edge, past + mine_ref[group])


def core_state_kernel(
    here_ref, exp_ref, mine_edge_ref, other_edge_ref, mine_ref, other_ref, keep_ref, send_ref,
    *, reverse, length, span
):
    group = pl.program_id(0)
    behind = here_ref[2] == (0 if reverse else 1)
    for chip, edge_ref in enumerate((mine_edge_ref, other_edge_ref)):
        head = 4 * group + 2 * jnp.bitwise_xor(here_ref[1], chip) + here_ref[2]
        rate = log_rate(exp_ref[head], length)
        edge = edge_ref[0]
        past = power_of(rate, span) * edge
        keep_ref[0, chip] = jnp.where(behind, past + other_ref[0, chip], edge)
        send_ref[0, chip] = jnp.where(behind, edge, past + mine_ref[0, chip])


def picked(here_ref, mine_ref, other_ref, slot):
    chip = jnp.bitwise_xor(here_ref[1], slot // 2)
    return jnp.where(here_ref[2] == slot % 2, mine_ref[0, chip], other_ref[0, chip])


def key_value_kernel(
    here_ref, exp_ref, query_ref, key_ref, value_ref, grad_ref, mine_ref, other_ref,
    gk_ref, gv_ref, send_ref, *, length
):
    group = pl.program_id(0)
    span = query_ref.shape[0]
    source = lax.broadcasted_iota(jnp.int32, (span, span), 0)
    target = lax.broadcasted_iota(jnp.int32, (span, span), 1)
    gap = (target - source).astype(f32)
    left = span - lax.broadcasted_iota(jnp.int32, (span, WIDTH), 0).astype(f32)
    for slot in range(4):
        rate = log_rate(exp_ref[4 * group + slot], length)
        lanes = pl.ds(slot * WIDTH, WIDTH)
        query, key = query_ref[:, lanes], key_ref[:, lanes]
        value, grad = value_ref[:, lanes], grad_ref[:, lanes]
        mask = jnp.where(gap >= 0.0, jnp.exp(rate * jnp.maximum(gap, 0.0)), 0.0)
        tail = jnp.exp(rate * left)
        grad_scores = jnp.concatenate(halves(dot(value, grad, ((1,), (1,))) * mask), 1)
        key_scores = jnp.concatenate(halves(dot(key, query, ((1,), (1,))) * mask), 1)
        high, low = halves(picked(here_ref, mine_ref, other_ref, slot))
        gk = tail * dot(
            jnp.concatenate((value, value), 1), jnp.concatenate((high, low), 1), ((1,), (1,))
        )
        gk = gk + dot(grad_scores, jnp.concatenate((query, query), 0), ((1,), (0,)))
        gv = tail * dot(
            jnp.concatenate((key, key), 1), jnp.concatenate((high, low), 0), ((1,), (0,))
        )
        gv = gv + dot(key_scores, jnp.concatenate((grad, grad), 0), ((1,), (0,)))
        gk_ref[:, lanes] = gk.astype(bf16)
        gv_ref[:, lanes] = gv.astype(bf16)
        send_ref[slot, 0] = gk.astype(bf16)
        send_ref[4 + slot, 0] = gv.astype(bf16)


def query_kernel(
    here_ref, exp_ref, key_ref, value_ref, grad_ref, mine_ref, other_ref, gq_ref, *, length
):
    group = pl.program_id(0)
    span = key_ref.shape[0]
    target = lax.broadcasted_iota(jnp.int32, (span, span), 0)
    source = lax.broadcasted_iota(jnp.int32, (span, span), 1)
    gap = (target - source).astype(f32)
    done = 1.0 + lax.broadcasted_iota(jnp.int32, (span, WIDTH), 0).astype(f32)
    for slot in range(4):
        rate = log_rate(exp_ref[4 * group + slot], length)
        lanes = pl.ds(slot * WIDTH, WIDTH)
        key, value, grad = key_ref[:, lanes], value_ref[:, lanes], grad_ref[:, lanes]
        mask = jnp.where(gap >= 0.0, jnp.exp(rate * jnp.maximum(gap, 0.0)), 0.0)
        scores = jnp.concatenate(halves(dot(grad, value, ((1,), (1,))) * mask), 1)
        high, low = halves(picked(here_ref, mine_ref, other_ref, slot))
        gq = jnp.exp(rate * done) * dot(
            jnp.concatenate((grad, grad), 1), jnp.concatenate((high, low), 1), ((1,), (1,))
        )
        gq = gq + dot(scores, jnp.concatenate((key, key), 0), ((1,), (0,)))
        gq_ref[:, lanes] = gq.astype(bf16)


def weight_kernel(cols_ref, rows_ref, out_ref, turned):
    @pl.when(pl.program_id(0) == 0)
    def _():
        turned[...] = cols_ref[...].T

    product = dot(turned[...], rows_ref[...], ((1,), (0,))).T
    out_ref[0] = product[:, :WIDTH]
    out_ref[1] = product[:, WIDTH:]


SMEM = pl.BlockSpec(memory_space=pltpu.SMEM)
FREE = pl.BlockSpec(memory_space=pl.ANY)


def call(kernel, grid, in_specs, out_specs, out_shape, args, scratch=(), name=None):
    return pl.pallas_call(
        kernel,
        grid=grid,
        in_specs=in_specs,
        out_specs=out_specs,
        out_shape=out_shape,
        scratch_shapes=scratch,
        name=name,
        compiler_params=pltpu.CompilerParams(vmem_limit_bytes=48 * 1024 * 1024),
    )(*args)


def exchange(array, axes):
    return lax.all_to_all(array, axes, split_axis=0, concat_axis=0, tiled=True)


def per_device(inputs_x, queries, keys, values, grad_out, decay_exp, state_in):
    span = queries.shape[1]
    features = queries.shape[2]
    groups = features // (4 * WIDTH)
    length = span * lax.axis_size(CHAIN)
    tile = (WIDTH, WIDTH)
    query, key, value, grad = queries[0], keys[0], values[0], grad_out[0]
    exps = lax.all_gather(decay_exp, CHAIN, axis=0, tiled=True)
    here = jnp.stack([lax.axis_index(axis) for axis in CHAIN]).astype(jnp.int32)
    rows = lax.all_gather(inputs_x[0], PLANE, axis=0, tiled=True)

    head_cols = pl.BlockSpec((span, 4 * WIDTH), lambda i: (0, i))
    pair_tiles = pl.BlockSpec((1, 2) + tile, lambda i: (i, 0, 0, 0))
    line_tile = pl.BlockSpec((1,) + tile, lambda i: (i, 0, 0))
    line = pl.BlockSpec((groups,) + tile, lambda i: (0, 0, 0))
    single = pl.BlockSpec(tile, lambda i: (0, 0))
    pair_shape = jax.ShapeDtypeStruct((groups, 2) + tile, f32)
    line_shape = jax.ShapeDtypeStruct((groups,) + tile, f32)
    tile_shape = jax.ShapeDtypeStruct(tile, f32)
    token_shape = jax.ShapeDtypeStruct((span, features), bf16)

    def swap(array, axis):
        return lax.ppermute(array, axis, [(0, 1), (1, 0)])

    def run(body, grid, in_specs, out_specs, out_shape, args, after=None, scratch=(), name=None, **sizes):
        if after is not None:
            in_specs, args = in_specs + [FREE], args + (after,)
        return call(
            functools.partial(body, length=length, **sizes), grid, in_specs, out_specs, out_shape,
            args, scratch, name,
        )

    def updates(left, right, reverse):
        return run(
            update_kernel, (groups,), [SMEM, SMEM, head_cols, head_cols], [pair_tiles, pair_tiles],
            [pair_shape, pair_shape], (here, exps, left, right), reverse=reverse, name="updates",
        )

    def chip(mine, other, reverse, after):
        return run(
            chip_kernel, (groups,), [SMEM, SMEM, pair_tiles, pair_tiles], [line_tile, line_tile],
            [line_shape, line_shape], (here, exps, mine, other), after,
            reverse=reverse, span=float(span), name="chip",
        )

    def chip_state(edges, item, mine, other, reverse):
        spec = pl.BlockSpec((groups, 1) + tile, lambda i: (0, item, 0, 0))
        return run(
            chip_state_kernel, (1,), [SMEM, SMEM, spec, line, line], [line, line],
            [line_shape, line_shape], (here, exps, edges, mine, other),
            reverse=reverse, span=2.0 * span, name="chip_state",
        )

    def core_state(mine_edge, other_edge, mine, other, reverse):
        return run(
            core_state_kernel, (groups,),
            [SMEM, SMEM, line_tile, line_tile, pair_tiles, pair_tiles], [pair_tiles, pair_tiles],
            [pair_shape, pair_shape], (here, exps, mine_edge, other_edge, mine, other),
            reverse=reverse, span=float(span), name="core_state",
        )

    r_mine, sent = updates(query, grad, True)
    r_other = swap(sent, "core")
    f_mine, sent = updates(key, value, False)
    f_other = swap(sent, "core")
    r_chip, sent = chip(r_mine, r_other, True, f_mine)
    r_next = swap(sent, "xl")
    r_parts = exchange(run(
        quad_kernel, (1,), [SMEM, SMEM, line, line], line, line_shape,
        (here, exps, r_chip, r_next), span=2.0 * span, name="quad",
    ), "z")
    f_chip, sent = chip(f_mine, f_other, False, r_next)
    f_next = swap(sent, "xl")
    turned, state_grad = run(
        turn_kernel, (1,), [SMEM, SMEM, SMEM, line, line, line],
        [pl.BlockSpec((groups, 2) + tile, lambda i: (0, 0, 0, 0)), single],
        [pair_shape, tile_shape],
        (here, exps, decay_exp, r_parts, f_chip, f_next), span=2.0 * span, name="turn",
    )
    turned = exchange(turned, "z")
    r_edge, sent = chip_state(turned, 0, r_chip, r_next, True)
    r_far = swap(sent, "xl")
    mine, sent = core_state(r_edge, r_far, r_mine, r_other, True)
    other = swap(sent, "core")
    grad_key, grad_value, send = run(
        key_value_kernel, (groups,), [SMEM, SMEM] + 4 * [head_cols] + 2 * [pair_tiles],
        [head_cols, head_cols, pl.BlockSpec((8, 1, span, WIDTH), lambda i: (0, i % 4, 0, i // 4))],
        [token_shape, token_shape, jax.ShapeDtypeStruct((8, 4, span, 2 * WIDTH), bf16)],
        (here, exps, query, key, value, grad, mine, other), name="key_value",
    )
    cols = exchange(send.reshape(32, span, 2 * WIDTH), PLANE).reshape(32 * span, 2 * WIDTH)

    tokens, width = rows.shape
    block = width // 4
    partial = call(
        weight_kernel, (4,),
        [
            pl.BlockSpec((tokens, 2 * WIDTH), lambda i: (0, 0)),
            pl.BlockSpec((tokens, block), lambda i: (0, i)),
        ],
        pl.BlockSpec((2, block, WIDTH), lambda i: (i, 0, 0)),
        jax.ShapeDtypeStruct((8, block, WIDTH), f32),
        (cols, rows), scratch=[pltpu.VMEM((2 * WIDTH, tokens), bf16)], name="weight",
    )
    f_edges = exchange(run(
        scan_kernel, (1,),
        [SMEM, pl.BlockSpec((groups, 1) + tile, lambda i: (0, 1, 0, 0)), single, FREE],
        pl.BlockSpec((groups, 1) + tile, lambda i: (0, 0, 0, 0)),
        jax.ShapeDtypeStruct((groups, 1) + tile, f32),
        (decay_exp, turned, state_in[0, 0], partial), span=4.0 * span, name="scan",
    ), "z")
    f_edge, sent = chip_state(f_edges, 0, f_chip, f_next, False)
    f_far = swap(sent, "xl")
    mine, sent = core_state(f_edge, f_far, f_mine, f_other, False)
    other = swap(sent, "core")
    grad_query = run(
        query_kernel, (groups,), [SMEM, SMEM] + 3 * [head_cols] + 2 * [pair_tiles], head_cols,
        token_shape, (here, exps, key, value, grad, mine, other), name="query",
    )
    summed = lax.psum_scatter(partial, "z", scatter_dimension=0, tiled=True)
    pieces = exchange(summed.reshape(8, block // 8, WIDTH), ("y", "xh"))
    pieces = pieces.reshape(2, 4, block // 8, WIDTH).transpose(0, 2, 1, 3)
    weight_grads = pieces.reshape(2, 1, block // 8, 4 * WIDTH)
    return (
        grad_query[None], grad_key[None], grad_value[None], weight_grads, state_grad[None, None]
    )


def solution(mesh):
    fine = Mesh(mesh.devices.reshape(4, 2, 8, 2, 2), ("y", "xh", "z", "xl", "core"))
    dp, seq = ("y", "xh"), CHAIN
    tokens = P(dp, seq, None)
    in_specs = (tokens, tokens, tokens, tokens, tokens, P(seq), P(dp, seq, None, None))
    out_specs = (tokens, tokens, tokens, P(None, seq, dp, None), P(dp, seq, None, None))
    return jax.shard_map(
        per_device, mesh=fine, in_specs=in_specs, out_specs=out_specs, check_vma=False
    )
```

```python
import functools

import jax
import jax.numpy as jnp
from jax import lax
from jax.experimental import pallas as pl
from jax.experimental.pallas import tpu as pltpu
from jax.sharding import Mesh
from jax.sharding import PartitionSpec as P

WIDTH = 128
f32 = jnp.float32
bf16 = jnp.bfloat16
PLANE = ("y", "xh", "xl", "core")
QUAD = ("xl", "core")
CHAIN = ("z", "xl", "core")


def log_rate(exponent, length):
    return -(jnp.left_shift(1, exponent).astype(f32)) * (1.0 / length)


def power_of(rate, steps):
    return jnp.exp(jnp.full((1, WIDTH), rate * steps, f32))


def halves(wide):
    high = wide.astype(bf16)
    return high, (wide - high.astype(f32)).astype(bf16)


def dot(left, right, dims):
    return lax.dot_general(left, right, (dims, ((), ())), preferred_element_type=f32)


def update_kernel(here_ref, exp_ref, left_ref, right_ref, *refs, reverse, length):
    group = pl.program_id(0)
    span = left_ref.shape[0]
    rows = lax.broadcasted_iota(jnp.int32, (span, WIDTH), 0).astype(f32)
    steps = rows if reverse else (span - 1.0) - rows
    for core, out_ref in enumerate(refs[-2:]):
        for chip in range(2):
            slot = 2 * jnp.bitwise_xor(here_ref[1], chip) + jnp.bitwise_xor(here_ref[2], core)
            rate = log_rate(exp_ref[4 * group + slot], length)
            lanes = pl.ds(pl.multiple_of(slot * WIDTH, WIDTH), WIDTH)
            high, low = halves(left_ref[:, lanes].astype(f32) * jnp.exp(rate * steps))
            right = right_ref[:, lanes]
            out_ref[0, chip] = dot(
                jnp.concatenate((high, low), 0), jnp.concatenate((right, right), 0), ((0,), (0,))
            )


def weighed(mine, other, position, reverse, rate, span):
    position = position.astype(f32)
    later = position if reverse else 1.0 - position
    return power_of(rate, span * later) * mine + power_of(rate, span * (1.0 - later)) * other


def chip_kernel(
    here_ref, exp_ref, mine_ref, other_ref, *refs, reverse, length, span
):
    keep_ref, send_ref = refs[-2:]
    group = pl.program_id(0)
    for chip, out_ref in enumerate((keep_ref, send_ref)):
        head = 4 * group + 2 * jnp.bitwise_xor(here_ref[1], chip) + here_ref[2]
        rate = log_rate(exp_ref[head], length)
        out_ref[0] = weighed(
            mine_ref[0, chip], other_ref[0, chip], here_ref[2], reverse, rate, span
        )


def quad_kernel(here_ref, exp_ref, mine_ref, other_ref, out_ref, *, length, span):
    for group in range(out_ref.shape[0]):
        rate = log_rate(exp_ref[4 * group + 2 * here_ref[1] + here_ref[2]], length)
        out_ref[group] = weighed(
            mine_ref[group], other_ref[group], here_ref[1], True, rate, span
        )


def scan_kernel(own_ref, parts_ref, out_ref, grad_ref, *, length, span):
    rate = log_rate(own_ref[0], length)
    decay = power_of(rate, span)
    state = jnp.zeros(grad_ref.shape, f32)
    for group in reversed(range(parts_ref.shape[0])):
        out_ref[group] = state
        state = decay * state + parts_ref[group]
    grad_ref[...] = power_of(rate, 1.0) * state


def line_kernel(
    here_ref, exp_ref, mine_ref, other_ref, first_ref, after_ref, out_ref, *, length, span
):
    count = mine_ref.shape[0]
    for group in range(count):
        rate = log_rate(exp_ref[4 * group + 2 * here_ref[1] + here_ref[2]], length)
        out_ref[group] = weighed(
            mine_ref[group], other_ref[group], here_ref[1], False, rate, span
        )
    out_ref[count] = first_ref[...]


def edge_kernel(here_ref, exp_ref, parts_ref, first_ref, after_ref, out_ref, *, length, span):
    rate = log_rate(exp_ref[4 * pl.program_id(0) + 2 * here_ref[1] + here_ref[2]], length)
    decay = power_of(rate, span)
    state = first_ref[0, 0]
    for group in range(parts_ref.shape[0] - 1):
        state = jnp.where(here_ref[0] > group, decay * state + parts_ref[group, 0], state)
    out_ref[0] = state


def chip_state_kernel(
    here_ref, exp_ref, edge_ref, mine_ref, other_ref, keep_ref, send_ref, *, reverse, length, span
):
    behind = here_ref[1] == (0 if reverse else 1)
    for group in range(edge_ref.shape[0]):
        rate = log_rate(exp_ref[4 * group + 2 * here_ref[1] + here_ref[2]], length)
        edge = edge_ref[group]
        past = power_of(rate, span) * edge
        keep_ref[group] = jnp.where(behind, past + other_ref[group], edge)
        send_ref[group] = jnp.where(behind, edge, past + mine_ref[group])


def core_state_kernel(
    here_ref, exp_ref, mine_edge_ref, other_edge_ref, mine_ref, other_ref, keep_ref, send_ref,
    *, reverse, length, span
):
    group = pl.program_id(0)
    behind = here_ref[2] == (0 if reverse else 1)
    for chip, edge_ref in enumerate((mine_edge_ref, other_edge_ref)):
        head = 4 * group + 2 * jnp.bitwise_xor(here_ref[1], chip) + here_ref[2]
        rate = log_rate(exp_ref[head], length)
        edge = edge_ref[0]
        past = power_of(rate, span) * edge
        keep_ref[0, chip] = jnp.where(behind, past + other_ref[0, chip], edge)
        send_ref[0, chip] = jnp.where(behind, edge, past + mine_ref[0, chip])


def picked(here_ref, mine_ref, other_ref, slot):
    chip = jnp.bitwise_xor(here_ref[1], slot // 2)
    return jnp.where(here_ref[2] == slot % 2, mine_ref[0, chip], other_ref[0, chip])


def key_value_kernel(
    here_ref, exp_ref, query_ref, key_ref, value_ref, grad_ref, mine_ref, other_ref,
    gk_ref, gv_ref, send_ref, *, length
):
    group = pl.program_id(0)
    span = query_ref.shape[0]
    source = lax.broadcasted_iota(jnp.int32, (span, span), 0)
    target = lax.broadcasted_iota(jnp.int32, (span, span), 1)
    gap = (target - source).astype(f32)
    left = span - lax.broadcasted_iota(jnp.int32, (span, WIDTH), 0).astype(f32)
    for slot in range(4):
        rate = log_rate(exp_ref[4 * group + slot], length)
        lanes = pl.ds(slot * WIDTH, WIDTH)
        query, key = query_ref[:, lanes], key_ref[:, lanes]
        value, grad = value_ref[:, lanes], grad_ref[:, lanes]
        mask = jnp.where(gap >= 0.0, jnp.exp(rate * jnp.maximum(gap, 0.0)), 0.0)
        tail = jnp.exp(rate * left)
        grad_scores = jnp.concatenate(halves(dot(value, grad, ((1,), (1,))) * mask), 1)
        key_scores = jnp.concatenate(halves(dot(key, query, ((1,), (1,))) * mask), 1)
        high, low = halves(picked(here_ref, mine_ref, other_ref, slot))
        gk = tail * dot(
            jnp.concatenate((value, value), 1), jnp.concatenate((high, low), 1), ((1,), (1,))
        )
        gk = gk + dot(grad_scores, jnp.concatenate((query, query), 0), ((1,), (0,)))
        gv = tail * dot(
            jnp.concatenate((key, key), 1), jnp.concatenate((high, low), 0), ((1,), (0,))
        )
        gv = gv + dot(key_scores, jnp.concatenate((grad, grad), 0), ((1,), (0,)))
        gk_ref[:, lanes] = gk.astype(bf16)
        gv_ref[:, lanes] = gv.astype(bf16)
        send_ref[slot, 0] = gk.astype(bf16)
        send_ref[4 + slot, 0] = gv.astype(bf16)


def query_kernel(
    here_ref, exp_ref, key_ref, value_ref, grad_ref, mine_ref, other_ref, gq_ref, *, length
):
    group = pl.program_id(0)
    span = key_ref.shape[0]
    target = lax.broadcasted_iota(jnp.int32, (span, span), 0)
    source = lax.broadcasted_iota(jnp.int32, (span, span), 1)
    gap = (target - source).astype(f32)
    done = 1.0 + lax.broadcasted_iota(jnp.int32, (span, WIDTH), 0).astype(f32)
    for slot in range(4):
        rate = log_rate(exp_ref[4 * group + slot], length)
        lanes = pl.ds(slot * WIDTH, WIDTH)
        key, value, grad = key_ref[:, lanes], value_ref[:, lanes], grad_ref[:, lanes]
        mask = jnp.where(gap >= 0.0, jnp.exp(rate * jnp.maximum(gap, 0.0)), 0.0)
        scores = jnp.concatenate(halves(dot(grad, value, ((1,), (1,))) * mask), 1)
        high, low = halves(picked(here_ref, mine_ref, other_ref, slot))
        gq = jnp.exp(rate * done) * dot(
            jnp.concatenate((grad, grad), 1), jnp.concatenate((high, low), 1), ((1,), (1,))
        )
        gq = gq + dot(scores, jnp.concatenate((key, key), 0), ((1,), (0,)))
        gq_ref[:, lanes] = gq.astype(bf16)


def weight_kernel(cols_ref, rows_ref, out_ref, turned):
    @pl.when(pl.program_id(0) == 0)
    def _():
        turned[...] = cols_ref[...].T

    product = dot(turned[...], rows_ref[...], ((1,), (0,))).T
    out_ref[0] = product[:, :WIDTH]
    out_ref[1] = product[:, WIDTH:]


SMEM = pl.BlockSpec(memory_space=pltpu.SMEM)
FREE = pl.BlockSpec(memory_space=pl.ANY)


def call(kernel, grid, in_specs, out_specs, out_shape, args, scratch=(), name=None):
    return pl.pallas_call(
        kernel,
        grid=grid,
        in_specs=in_specs,
        out_specs=out_specs,
        out_shape=out_shape,
        scratch_shapes=scratch,
        name=name,
        compiler_params=pltpu.CompilerParams(vmem_limit_bytes=48 * 1024 * 1024),
    )(*args)


def exchange(array, axes):
    return lax.all_to_all(array, axes, split_axis=0, concat_axis=0, tiled=True)


def per_device(inputs_x, queries, keys, values, grad_out, decay_exp, state_in):
    span = queries.shape[1]
    features = queries.shape[2]
    groups = features // (4 * WIDTH)
    length = span * lax.axis_size(CHAIN)
    tile = (WIDTH, WIDTH)
    query, key, value, grad = queries[0], keys[0], values[0], grad_out[0]
    exps = lax.all_gather(decay_exp, CHAIN, axis=0, tiled=True)
    here = jnp.stack([lax.axis_index(axis) for axis in CHAIN]).astype(jnp.int32)
    rows = lax.all_gather(inputs_x[0], PLANE, axis=0, tiled=True)

    head_cols = pl.BlockSpec((span, 4 * WIDTH), lambda i: (0, i))
    pair_tiles = pl.BlockSpec((1, 2) + tile, lambda i: (i, 0, 0, 0))
    line_tile = pl.BlockSpec((1,) + tile, lambda i: (i, 0, 0))
    line = pl.BlockSpec((groups,) + tile, lambda i: (0, 0, 0))
    single = pl.BlockSpec(tile, lambda i: (0, 0))
    pair_shape = jax.ShapeDtypeStruct((groups, 2) + tile, f32)
    line_shape = jax.ShapeDtypeStruct((groups,) + tile, f32)
    tile_shape = jax.ShapeDtypeStruct(tile, f32)
    token_shape = jax.ShapeDtypeStruct((span, features), bf16)

    def swap(array, axis):
        return lax.ppermute(array, axis, [(0, 1), (1, 0)])

    def run(body, grid, in_specs, out_specs, out_shape, args, after=None, scratch=(), name=None, **sizes):
        if after is not None:
            in_specs, args = in_specs + [FREE], args + (after,)
        return call(
            functools.partial(body, length=length, **sizes), grid, in_specs, out_specs, out_shape,
            args, scratch, name,
        )

    def updates(left, right, reverse, after=None):
        return run(
            update_kernel, (groups,), [SMEM, SMEM, head_cols, head_cols], [pair_tiles, pair_tiles],
            [pair_shape, pair_shape], (here, exps, left, right), after,
            reverse=reverse, name="updates",
        )

    def chip(mine, other, reverse, after=None):
        return run(
            chip_kernel, (groups,), [SMEM, SMEM, pair_tiles, pair_tiles], [line_tile, line_tile],
            [line_shape, line_shape], (here, exps, mine, other), after,
            reverse=reverse, span=float(span), name="chip",
        )

    def chip_state(edges, mine, other, reverse):
        return run(
            chip_state_kernel, (1,), [SMEM, SMEM, line, line, line], [line, line],
            [line_shape, line_shape], (here, exps, edges, mine, other),
            reverse=reverse, span=2.0 * span, name="chip_state",
        )

    def core_state(mine_edge, other_edge, mine, other, reverse):
        return run(
            core_state_kernel, (groups,),
            [SMEM, SMEM, line_tile, line_tile, pair_tiles, pair_tiles], [pair_tiles, pair_tiles],
            [pair_shape, pair_shape], (here, exps, mine_edge, other_edge, mine, other),
            reverse=reverse, span=float(span), name="core_state",
        )

    r_mine, sent = updates(query, grad, True)
    r_other = swap(sent, "core")
    r_chip, sent = chip(r_mine, r_other, True)
    r_next = swap(sent, "xl")
    f_mine, sent = updates(key, value, False, r_chip)
    f_other = swap(sent, "core")
    r_parts = exchange(run(
        quad_kernel, (1,), [SMEM, SMEM, line, line], line, line_shape,
        (here, exps, r_chip, r_next), span=2.0 * span, name="quad",
    ), "z")
    f_chip, sent = chip(f_mine, f_other, False, r_next)
    f_next = swap(sent, "xl")
    r_edges, state_grad = run(
        scan_kernel, (1,), [SMEM, line], [line, single], [line_shape, tile_shape],
        (decay_exp, r_parts), span=4.0 * span, name="scan",
    )
    r_edges = exchange(r_edges, "z")
    r_edge, sent = chip_state(r_edges, r_chip, r_next, True)
    r_far = swap(sent, "xl")
    f_parts = lax.all_gather(run(
        line_kernel, (1,), [SMEM, SMEM, line, line, single],
        pl.BlockSpec((groups + 1,) + tile, lambda i: (0, 0, 0)),
        jax.ShapeDtypeStruct((groups + 1,) + tile, f32),
        (here, exps, f_chip, f_next, state_in[0, 0]), r_edge, span=2.0 * span, name="line",
    ), "z")
    mine, sent = core_state(r_edge, r_far, r_mine, r_other, True)
    other = swap(sent, "core")
    grad_key, grad_value, send = run(
        key_value_kernel, (groups,), [SMEM, SMEM] + 4 * [head_cols] + 2 * [pair_tiles],
        [head_cols, head_cols, pl.BlockSpec((8, 1, span, WIDTH), lambda i: (0, i % 4, 0, i // 4))],
        [token_shape, token_shape, jax.ShapeDtypeStruct((8, 4, span, 2 * WIDTH), bf16)],
        (here, exps, query, key, value, grad, mine, other), name="key_value",
    )
    cols = exchange(send.reshape(32, span, 2 * WIDTH), PLANE).reshape(32 * span, 2 * WIDTH)

    tokens, width = rows.shape
    block = width // 4
    partial = call(
        weight_kernel, (4,),
        [
            pl.BlockSpec((tokens, 2 * WIDTH), lambda i: (0, 0)),
            pl.BlockSpec((tokens, block), lambda i: (0, i)),
        ],
        pl.BlockSpec((2, block, WIDTH), lambda i: (i, 0, 0)),
        jax.ShapeDtypeStruct((8, block, WIDTH), f32),
        (cols, rows), scratch=[pltpu.VMEM((2 * WIDTH, tokens), bf16)], name="weight",
    )
    f_edges = run(
        edge_kernel, (groups,),
        [
            SMEM, SMEM, pl.BlockSpec((groups, 1) + tile, lambda i: (0, i, 0, 0)),
            pl.BlockSpec((1, 1) + tile, lambda i: (i, groups, 0, 0)),
        ],
        line_tile, line_shape, (here, exps, f_parts, f_parts), partial,
        span=4.0 * span, name="edge",
    )
    f_edge, sent = chip_state(f_edges, f_chip, f_next, False)
    f_far = swap(sent, "xl")
    mine, sent = core_state(f_edge, f_far, f_mine, f_other, False)
    other = swap(sent, "core")
    grad_query = run(
        query_kernel, (groups,), [SMEM, SMEM] + 3 * [head_cols] + 2 * [pair_tiles], head_cols,
        token_shape, (here, exps, key, value, grad, mine, other), name="query",
    )
    summed = lax.psum_scatter(partial, "z", scatter_dimension=0, tiled=True)
    pieces = exchange(summed.reshape(8, block // 8, WIDTH), ("y", "xh"))
    pieces = pieces.reshape(2, 4, block // 8, WIDTH).transpose(0, 2, 1, 3)
    weight_grads = pieces.reshape(2, 1, block // 8, 4 * WIDTH)
    return (
        grad_query[None], grad_key[None], grad_value[None], weight_grads, state_grad[None, None]
    )


def solution(mesh):
    fine = Mesh(mesh.devices.reshape(4, 2, 8, 2, 2), ("y", "xh", "z", "xl", "core"))
    dp, seq = ("y", "xh"), CHAIN
    tokens = P(dp, seq, None)
    in_specs = (tokens, tokens, tokens, tokens, tokens, P(seq), P(dp, seq, None, None))
    out_specs = (tokens, tokens, tokens, P(None, seq, dp, None), P(dp, seq, None, None))
    return jax.shard_map(
        per_device, mesh=fine, in_specs=in_specs, out_specs=out_specs, check_vma=False
    )
```

```python
import functools

import jax
import jax.numpy as jnp
from jax import lax
from jax.experimental import pallas as pl
from jax.experimental.pallas import tpu as pltpu
from jax.sharding import Mesh
from jax.sharding import PartitionSpec as P

WIDTH = 128
f32 = jnp.float32
bf16 = jnp.bfloat16
PLANE = ("y", "xh", "xl", "core")
QUAD = ("xl", "core")
LINE = ("zh", "zl")
CHAIN = ("zh", "zl", "xl", "core")
FINAL = ("y", "xh", "zl")


def log_rate(exponent, length):
    return -(jnp.left_shift(1, exponent).astype(f32)) * (1.0 / length)


def power_of(rate, steps):
    return jnp.exp(jnp.full((1, WIDTH), rate * steps, f32))


def halves(wide):
    high = wide.astype(bf16)
    return high, (wide - high.astype(f32)).astype(bf16)


def dot(left, right, dims):
    return lax.dot_general(left, right, (dims, ((), ())), preferred_element_type=f32)


def update_kernel(here_ref, exp_ref, left_ref, right_ref, *refs, reverse, length):
    group = pl.program_id(0)
    span = left_ref.shape[0]
    rows = lax.broadcasted_iota(jnp.int32, (span, WIDTH), 0).astype(f32)
    steps = rows if reverse else (span - 1.0) - rows
    for core, out_ref in enumerate(refs[-2:]):
        for chip in range(2):
            slot = 2 * jnp.bitwise_xor(here_ref[1], chip) + jnp.bitwise_xor(here_ref[2], core)
            rate = log_rate(exp_ref[4 * group + slot], length)
            lanes = pl.ds(pl.multiple_of(slot * WIDTH, WIDTH), WIDTH)
            high, low = halves(left_ref[:, lanes].astype(f32) * jnp.exp(rate * steps))
            right = right_ref[:, lanes]
            out_ref[0, chip] = dot(
                jnp.concatenate((high, low), 0), jnp.concatenate((right, right), 0), ((0,), (0,))
            )


def weighed(mine, other, position, reverse, rate, span):
    position = position.astype(f32)
    later = position if reverse else 1.0 - position
    return power_of(rate, span * later) * mine + power_of(rate, span * (1.0 - later)) * other


def chip_kernel(
    here_ref, exp_ref, mine_ref, other_ref, *refs, reverse, length, span
):
    keep_ref, send_ref = refs[-2:]
    group = pl.program_id(0)
    for chip, out_ref in enumerate((keep_ref, send_ref)):
        head = 4 * group + 2 * jnp.bitwise_xor(here_ref[1], chip) + here_ref[2]
        rate = log_rate(exp_ref[head], length)
        out_ref[0] = weighed(
            mine_ref[0, chip], other_ref[0, chip], here_ref[2], reverse, rate, span
        )


def quad_kernel(here_ref, exp_ref, mine_ref, other_ref, after_ref, out_ref, *, length, span):
    for group in range(out_ref.shape[0]):
        rate = log_rate(exp_ref[4 * group + 2 * here_ref[1] + here_ref[2]], length)
        out_ref[group] = weighed(
            mine_ref[group], other_ref[group], here_ref[1], True, rate, span
        )


def scan_kernel(own_ref, parts_ref, after_ref, out_ref, grad_ref, *, length, span):
    rate = log_rate(own_ref[0], length)
    decay = power_of(rate, span)
    state = jnp.zeros(grad_ref.shape, f32)
    for group in reversed(range(parts_ref.shape[0])):
        out_ref[group] = state
        state = decay * state + parts_ref[group]
    grad_ref[...] = power_of(rate, 1.0) * state


def line_kernel(
    here_ref, exp_ref, mine_ref, other_ref, first_ref, after_ref, out_ref, *, length, span
):
    count = mine_ref.shape[0]
    for group in range(count):
        rate = log_rate(exp_ref[4 * group + 2 * here_ref[1] + here_ref[2]], length)
        out_ref[group] = weighed(
            mine_ref[group], other_ref[group], here_ref[1], False, rate, span
        )
    out_ref[count] = first_ref[...]


def edge_kernel(here_ref, exp_ref, parts_ref, first_ref, after_ref, out_ref, *, length, span):
    rate = log_rate(exp_ref[4 * pl.program_id(0) + 2 * here_ref[1] + here_ref[2]], length)
    decay = power_of(rate, span)
    state = first_ref[0, 0]
    for group in range(parts_ref.shape[0] - 1):
        state = jnp.where(here_ref[0] > group, decay * state + parts_ref[group, 0], state)
    out_ref[0] = state


def chip_state_kernel(
    here_ref, exp_ref, edge_ref, mine_ref, other_ref, *refs, reverse, length, span
):
    keep_ref, send_ref = refs[-2:]
    behind = here_ref[1] == (0 if reverse else 1)
    for group in range(edge_ref.shape[0]):
        rate = log_rate(exp_ref[4 * group + 2 * here_ref[1] + here_ref[2]], length)
        edge = edge_ref[group]
        past = power_of(rate, span) * edge
        keep_ref[group] = jnp.where(behind, past + other_ref[group], edge)
        send_ref[group] = jnp.where(behind, edge, past + mine_ref[group])


def core_state_kernel(
    here_ref, exp_ref, mine_edge_ref, other_edge_ref, mine_ref, other_ref, *refs,
    reverse, length, span
):
    keep_ref, send_ref = refs[-2:]
    group = pl.program_id(0)
    behind = here_ref[2] == (0 if reverse else 1)
    for chip, edge_ref in enumerate((mine_edge_ref, other_edge_ref)):
        head = 4 * group + 2 * jnp.bitwise_xor(here_ref[1], chip) + here_ref[2]
        rate = log_rate(exp_ref[head], length)
        edge = edge_ref[0]
        past = power_of(rate, span) * edge
        keep_ref[0, chip] = jnp.where(behind, past + other_ref[0, chip], edge)
        send_ref[0, chip] = jnp.where(behind, edge, past + mine_ref[0, chip])


def picked(here_ref, mine_ref, other_ref, slot):
    chip = jnp.bitwise_xor(here_ref[1], slot // 2)
    return jnp.where(here_ref[2] == slot % 2, mine_ref[0, chip], other_ref[0, chip])


def key_value_kernel(
    here_ref, exp_ref, query_ref, key_ref, value_ref, grad_ref, mine_ref, other_ref, *refs,
    length, first
):
    gk_ref, gv_ref, send_ref = refs[-3:]
    group = first + pl.program_id(0)
    span = query_ref.shape[0]
    source = lax.broadcasted_iota(jnp.int32, (span, span), 0)
    target = lax.broadcasted_iota(jnp.int32, (span, span), 1)
    gap = (target - source).astype(f32)
    left = span - lax.broadcasted_iota(jnp.int32, (span, WIDTH), 0).astype(f32)
    for slot in range(4):
        rate = log_rate(exp_ref[4 * group + slot], length)
        lanes = pl.ds(slot * WIDTH, WIDTH)
        query, key = query_ref[:, lanes], key_ref[:, lanes]
        value, grad = value_ref[:, lanes], grad_ref[:, lanes]
        mask = jnp.where(gap >= 0.0, jnp.exp(rate * jnp.maximum(gap, 0.0)), 0.0)
        tail = jnp.exp(rate * left)
        grad_scores = jnp.concatenate(halves(dot(value, grad, ((1,), (1,))) * mask), 1)
        key_scores = jnp.concatenate(halves(dot(key, query, ((1,), (1,))) * mask), 1)
        high, low = halves(picked(here_ref, mine_ref, other_ref, slot))
        gk = tail * dot(
            jnp.concatenate((value, value), 1), jnp.concatenate((high, low), 1), ((1,), (1,))
        )
        gk = gk + dot(grad_scores, jnp.concatenate((query, query), 0), ((1,), (0,)))
        gv = tail * dot(
            jnp.concatenate((key, key), 1), jnp.concatenate((high, low), 0), ((1,), (0,))
        )
        gv = gv + dot(key_scores, jnp.concatenate((grad, grad), 0), ((1,), (0,)))
        gk_ref[:, lanes] = gk.astype(bf16)
        gv_ref[:, lanes] = gv.astype(bf16)
        send_ref[slot, 0] = gk.astype(bf16)
        send_ref[4 + slot, 0] = gv.astype(bf16)


def query_kernel(
    here_ref, exp_ref, key_ref, value_ref, grad_ref, mine_ref, other_ref, gq_ref, *, length
):
    group = pl.program_id(0)
    span = key_ref.shape[0]
    target = lax.broadcasted_iota(jnp.int32, (span, span), 0)
    source = lax.broadcasted_iota(jnp.int32, (span, span), 1)
    gap = (target - source).astype(f32)
    done = 1.0 + lax.broadcasted_iota(jnp.int32, (span, WIDTH), 0).astype(f32)
    for slot in range(4):
        rate = log_rate(exp_ref[4 * group + slot], length)
        lanes = pl.ds(slot * WIDTH, WIDTH)
        key, value, grad = key_ref[:, lanes], value_ref[:, lanes], grad_ref[:, lanes]
        mask = jnp.where(gap >= 0.0, jnp.exp(rate * jnp.maximum(gap, 0.0)), 0.0)
        scores = jnp.concatenate(halves(dot(grad, value, ((1,), (1,))) * mask), 1)
        high, low = halves(picked(here_ref, mine_ref, other_ref, slot))
        gq = jnp.exp(rate * done) * dot(
            jnp.concatenate((grad, grad), 1), jnp.concatenate((high, low), 1), ((1,), (1,))
        )
        gq = gq + dot(scores, jnp.concatenate((key, key), 0), ((1,), (0,)))
        gq_ref[:, lanes] = gq.astype(bf16)


def weight_kernel(cols_ref, rows_ref, *refs):
    out_ref, turned = refs[-2:]

    @pl.when(pl.program_id(0) == 0)
    def _():
        turned[...] = cols_ref[...].T

    product = dot(turned[...], rows_ref[...], ((1,), (0,))).T
    count = product.shape[0] // 16
    for item in range(16):
        out_ref[item % 2, pl.ds(item // 2 * count, count)] = product[
            item * count : (item + 1) * count
        ]


SMEM = pl.BlockSpec(memory_space=pltpu.SMEM)
FREE = pl.BlockSpec(memory_space=pl.ANY)


def call(kernel, grid, in_specs, out_specs, out_shape, args, scratch=(), name=None):
    return pl.pallas_call(
        kernel,
        grid=grid,
        in_specs=in_specs,
        out_specs=out_specs,
        out_shape=out_shape,
        scratch_shapes=scratch,
        name=name,
        compiler_params=pltpu.CompilerParams(vmem_limit_bytes=48 * 1024 * 1024),
    )(*args)


def exchange(array, axes):
    return lax.all_to_all(array, axes, split_axis=0, concat_axis=0, tiled=True)


def per_device(inputs_x, queries, keys, values, grad_out, decay_exp, state_in):
    span = queries.shape[1]
    features = queries.shape[2]
    groups = features // (4 * WIDTH)
    length = span * lax.axis_size(CHAIN)
    tile = (WIDTH, WIDTH)
    query, key, value, grad = queries[0], keys[0], values[0], grad_out[0]
    exps = lax.all_gather(decay_exp, CHAIN, axis=0, tiled=True)
    here = jnp.stack([lax.axis_index(axis) for axis in (LINE, "xl", "core")]).astype(jnp.int32)
    rows = lax.all_gather(inputs_x[0], PLANE, axis=0, tiled=True)

    head_cols = pl.BlockSpec((span, 4 * WIDTH), lambda i: (0, i))
    pair_tiles = pl.BlockSpec((1, 2) + tile, lambda i: (i, 0, 0, 0))
    line_tile = pl.BlockSpec((1,) + tile, lambda i: (i, 0, 0))
    line = pl.BlockSpec((groups,) + tile, lambda i: (0, 0, 0))
    single = pl.BlockSpec(tile, lambda i: (0, 0))
    pair_shape = jax.ShapeDtypeStruct((groups, 2) + tile, f32)
    line_shape = jax.ShapeDtypeStruct((groups,) + tile, f32)
    tile_shape = jax.ShapeDtypeStruct(tile, f32)
    token_shape = jax.ShapeDtypeStruct((span, features), bf16)

    def swap(array, axis):
        return lax.ppermute(array, axis, [(0, 1), (1, 0)])

    def run(body, grid, in_specs, out_specs, out_shape, args, after=None, scratch=(), name=None, **sizes):
        if after is not None:
            in_specs, args = in_specs + [FREE], args + (after,)
        return call(
            functools.partial(body, length=length, **sizes), grid, in_specs, out_specs, out_shape,
            args, scratch, name,
        )

    def updates(left, right, reverse, after=None):
        return run(
            update_kernel, (groups,), [SMEM, SMEM, head_cols, head_cols], [pair_tiles, pair_tiles],
            [pair_shape, pair_shape], (here, exps, left, right), after,
            reverse=reverse, name="updates",
        )

    def chip(mine, other, reverse, after=None):
        return run(
            chip_kernel, (groups,), [SMEM, SMEM, pair_tiles, pair_tiles], [line_tile, line_tile],
            [line_shape, line_shape], (here, exps, mine, other), after,
            reverse=reverse, span=float(span), name="chip",
        )

    def chip_state(edges, mine, other, reverse, after=None):
        return run(
            chip_state_kernel, (1,), [SMEM, SMEM, line, line, line], [line, line],
            [line_shape, line_shape], (here, exps, edges, mine, other), after,
            reverse=reverse, span=2.0 * span, name="chip_state",
        )

    def core_state(mine_edge, other_edge, mine, other, reverse, after=None):
        return run(
            core_state_kernel, (groups,),
            [SMEM, SMEM, line_tile, line_tile, pair_tiles, pair_tiles], [pair_tiles, pair_tiles],
            [pair_shape, pair_shape], (here, exps, mine_edge, other_edge, mine, other), after,
            reverse=reverse, span=float(span), name="core_state",
        )

    r_mine, sent = updates(query, grad, True)
    r_other = swap(sent, "core")
    r_chip, sent = chip(r_mine, r_other, True)
    r_next = swap(sent, "xl")
    f_mine, sent = updates(key, value, False, r_chip)
    f_other = swap(sent, "core")
    r_parts = exchange(run(
        quad_kernel, (1,), [SMEM, SMEM, line, line], line, line_shape,
        (here, exps, r_chip, r_next), f_mine, span=2.0 * span, name="quad",
    ), LINE)
    f_chip, sent = chip(f_mine, f_other, False, r_next)
    f_next = swap(sent, "xl")
    r_edges, state_grad = run(
        scan_kernel, (1,), [SMEM, line], [line, single], [line_shape, tile_shape],
        (decay_exp, r_parts), f_chip, span=4.0 * span, name="scan",
    )
    r_edges = exchange(r_edges, LINE)
    r_edge, sent = chip_state(r_edges, r_chip, r_next, True, f_next)
    r_far = swap(sent, "xl")
    f_parts = lax.all_gather(run(
        line_kernel, (1,), [SMEM, SMEM, line, line, single],
        pl.BlockSpec((groups + 1,) + tile, lambda i: (0, 0, 0)),
        jax.ShapeDtypeStruct((groups + 1,) + tile, f32),
        (here, exps, f_chip, f_next, state_in[0, 0]), r_far, span=2.0 * span, name="line",
    ), LINE)
    mine, sent = core_state(r_edge, r_far, r_mine, r_other, True)
    other = swap(sent, "core")
    rest = here, exps, query, key, value, grad, mine, other
    grads, halves_cols = (), []
    for first in (0, groups // 2):
        columns = pl.BlockSpec((span, 4 * WIDTH), lambda i, first=first: (0, first + i))
        tiles = pl.BlockSpec((1, 2) + tile, lambda i, first=first: (first + i, 0, 0, 0))
        *grads, send = pl.pallas_call(
            functools.partial(key_value_kernel, length=length, first=first),
            grid=(groups // 2,),
            in_specs=[SMEM, SMEM] + 4 * [columns] + 2 * [tiles] + len(grads) * [FREE],
            out_specs=[columns, columns, pl.BlockSpec((8, 1, span, WIDTH), lambda i: (0, i, 0, 0))],
            out_shape=[
                token_shape, token_shape, jax.ShapeDtypeStruct((8, 4, span, WIDTH), bf16)
            ],
            input_output_aliases={8 + item: item for item in range(len(grads))},
            name="key_value",
            compiler_params=pltpu.CompilerParams(vmem_limit_bytes=48 * 1024 * 1024),
        )(*rest, *grads)
        if halves_cols:
            send, halves_cols[0] = lax.optimization_barrier((send, halves_cols[0]))
        halves_cols.append(
            exchange(send.reshape(32, span, WIDTH), PLANE).reshape(32 * span, WIDTH)
        )
    grad_key, grad_value = grads

    tokens, width = rows.shape
    block = width // 4
    def product(cols, after=()):
        return call(
            weight_kernel, (4,),
            [
                pl.BlockSpec((tokens, WIDTH), lambda i: (0, 0)),
                pl.BlockSpec((tokens, block), lambda i: (0, i)),
            ] + len(after) * [FREE],
            pl.BlockSpec((2, block // 2, WIDTH), lambda i: (i, 0, 0)),
            jax.ShapeDtypeStruct((8, block // 2, WIDTH), f32),
            (cols, rows, *after), scratch=[pltpu.VMEM((WIDTH, tokens), bf16)], name="weight",
        )

    def scattered(partial):
        return lax.psum_scatter(partial, LINE, scatter_dimension=0, tiled=True)

    partial = product(halves_cols[0])
    f_edges = run(
        edge_kernel, (groups,),
        [
            SMEM, SMEM, pl.BlockSpec((groups, 1) + tile, lambda i: (0, i, 0, 0)),
            pl.BlockSpec((1, 1) + tile, lambda i: (i, groups, 0, 0)),
        ],
        line_tile, line_shape, (here, exps, f_parts, f_parts), partial,
        span=4.0 * span, name="edge",
    )
    f_edge, sent = chip_state(f_edges, f_chip, f_next, False)
    summed = [scattered(partial), scattered(product(halves_cols[1], (partial, f_edge)))]
    f_far = swap(sent, "xl")
    mine, sent = core_state(f_edge, f_far, f_mine, f_other, False, summed[0])
    other = swap(sent, "core")
    grad_query = run(
        query_kernel, (groups,), [SMEM, SMEM] + 3 * [head_cols] + 2 * [pair_tiles], head_cols,
        token_shape, (here, exps, key, value, grad, mine, other), name="query",
    )
    summed[1], grad_query = lax.optimization_barrier((summed[1], grad_query))
    pieces = jnp.concatenate([part.reshape(8, 1, block // 16, WIDTH) for part in summed], 1)
    pieces = exchange(pieces.reshape(16, block // 16, WIDTH), FINAL)
    pieces = pieces.reshape(2, 4, block // 8, WIDTH).transpose(0, 2, 1, 3)
    weight_grads = pieces.reshape(2, 1, block // 8, 4 * WIDTH)
    return (
        grad_query[None], grad_key[None], grad_value[None], weight_grads, state_grad[None, None]
    )


def solution(mesh):
    fine = Mesh(mesh.devices.reshape(4, 2, 4, 2, 2, 2), ("y", "xh", "zh", "zl", "xl", "core"))
    dp, seq = ("y", "xh"), CHAIN
    tokens = P(dp, seq, None)
    in_specs = (tokens, tokens, tokens, tokens, tokens, P(seq), P(dp, seq, None, None))
    out_specs = (tokens, tokens, tokens, P(None, seq, dp, None), P(dp, seq, None, None))
    return jax.shard_map(
        per_device, mesh=fine, in_specs=in_specs, out_specs=out_specs, check_vma=False
    )
```

```python
import functools

import jax
import jax.numpy as jnp
from jax import lax
from jax.experimental import pallas as pl
from jax.experimental.pallas import tpu as pltpu
from jax.sharding import Mesh
from jax.sharding import PartitionSpec as P

WIDTH = 128
f32 = jnp.float32
bf16 = jnp.bfloat16
PLANE = ("y", "xh", "xl", "core")
QUAD = ("xl", "core")
LINE = ("zh", "zl")
CHAIN = ("zh", "zl", "xl", "core")
FINAL = ("y", "xh", "zl")


def log_rate(exponent, length):
    return -(jnp.left_shift(1, exponent).astype(f32)) * (1.0 / length)


def power_of(rate, steps):
    return jnp.exp(jnp.full((1, WIDTH), rate * steps, f32))


def halves(wide):
    high = wide.astype(bf16)
    return high, (wide - high.astype(f32)).astype(bf16)


def dot(left, right, dims):
    return lax.dot_general(left, right, (dims, ((), ())), preferred_element_type=f32)


def update_kernel(here_ref, exp_ref, left_ref, right_ref, *refs, reverse, length):
    group = pl.program_id(0)
    span = left_ref.shape[0]
    rows = lax.broadcasted_iota(jnp.int32, (span, WIDTH), 0).astype(f32)
    steps = rows if reverse else (span - 1.0) - rows
    for core, out_ref in enumerate(refs[-2:]):
        for chip in range(2):
            slot = 2 * jnp.bitwise_xor(here_ref[1], chip) + jnp.bitwise_xor(here_ref[2], core)
            rate = log_rate(exp_ref[4 * group + slot], length)
            lanes = pl.ds(pl.multiple_of(slot * WIDTH, WIDTH), WIDTH)
            high, low = halves(left_ref[:, lanes].astype(f32) * jnp.exp(rate * steps))
            right = right_ref[:, lanes]
            out_ref[0, chip] = dot(
                jnp.concatenate((high, low), 0), jnp.concatenate((right, right), 0), ((0,), (0,))
            )


def weighed(mine, other, position, reverse, rate, span):
    position = position.astype(f32)
    later = position if reverse else 1.0 - position
    return power_of(rate, span * later) * mine + power_of(rate, span * (1.0 - later)) * other


def chip_kernel(
    here_ref, exp_ref, mine_ref, other_ref, *refs, reverse, length, span
):
    keep_ref, send_ref = refs[-2:]
    group = pl.program_id(0)
    for chip, out_ref in enumerate((keep_ref, send_ref)):
        head = 4 * group + 2 * jnp.bitwise_xor(here_ref[1], chip) + here_ref[2]
        rate = log_rate(exp_ref[head], length)
        out_ref[0] = weighed(
            mine_ref[0, chip], other_ref[0, chip], here_ref[2], reverse, rate, span
        )


def quad_kernel(here_ref, exp_ref, mine_ref, other_ref, after_ref, out_ref, *, length, span):
    for group in range(out_ref.shape[0]):
        rate = log_rate(exp_ref[4 * group + 2 * here_ref[1] + here_ref[2]], length)
        out_ref[group] = weighed(
            mine_ref[group], other_ref[group], here_ref[1], True, rate, span
        )


def scan_kernel(own_ref, parts_ref, after_ref, out_ref, grad_ref, *, length, span):
    rate = log_rate(own_ref[0], length)
    decay = power_of(rate, span)
    state = jnp.zeros(grad_ref.shape, f32)
    for group in reversed(range(parts_ref.shape[0])):
        out_ref[group] = state
        state = decay * state + parts_ref[group]
    grad_ref[...] = power_of(rate, 1.0) * state


def line_kernel(
    here_ref, exp_ref, mine_ref, other_ref, first_ref, after_ref, out_ref, *, length, span
):
    count = mine_ref.shape[0]
    for group in range(count):
        rate = log_rate(exp_ref[4 * group + 2 * here_ref[1] + here_ref[2]], length)
        out_ref[group] = weighed(
            mine_ref[group], other_ref[group], here_ref[1], False, rate, span
        )
    out_ref[count] = first_ref[...]


def edge_kernel(here_ref, exp_ref, parts_ref, first_ref, after_ref, out_ref, *, length, span):
    rate = log_rate(exp_ref[4 * pl.program_id(0) + 2 * here_ref[1] + here_ref[2]], length)
    decay = power_of(rate, span)
    state = first_ref[0, 0]
    for group in range(parts_ref.shape[0] - 1):
        state = jnp.where(here_ref[0] > group, decay * state + parts_ref[group, 0], state)
    out_ref[0] = state


def chip_state_kernel(
    here_ref, exp_ref, edge_ref, mine_ref, other_ref, *refs, reverse, length, span
):
    keep_ref, send_ref = refs[-2:]
    behind = here_ref[1] == (0 if reverse else 1)
    for group in range(edge_ref.shape[0]):
        rate = log_rate(exp_ref[4 * group + 2 * here_ref[1] + here_ref[2]], length)
        edge = edge_ref[group]
        past = power_of(rate, span) * edge
        keep_ref[group] = jnp.where(behind, past + other_ref[group], edge)
        send_ref[group] = jnp.where(behind, edge, past + mine_ref[group])


def core_state_kernel(
    here_ref, exp_ref, mine_edge_ref, other_edge_ref, mine_ref, other_ref, *refs,
    reverse, length, span
):
    keep_ref, send_ref = refs[-2:]
    group = pl.program_id(0)
    behind = here_ref[2] == (0 if reverse else 1)
    for chip, edge_ref in enumerate((mine_edge_ref, other_edge_ref)):
        head = 4 * group + 2 * jnp.bitwise_xor(here_ref[1], chip) + here_ref[2]
        rate = log_rate(exp_ref[head], length)
        edge = edge_ref[0]
        past = power_of(rate, span) * edge
        keep_ref[0, chip] = jnp.where(behind, past + other_ref[0, chip], edge)
        send_ref[0, chip] = jnp.where(behind, edge, past + mine_ref[0, chip])


def picked(here_ref, mine_ref, other_ref, slot):
    chip = jnp.bitwise_xor(here_ref[1], slot // 2)
    return jnp.where(here_ref[2] == slot % 2, mine_ref[0, chip], other_ref[0, chip])


def inner_kernel(
    exp_ref, query_ref, key_ref, value_ref, grad_ref, after_ref, gk_ref, gv_ref, *, length
):
    group = pl.program_id(0)
    span = query_ref.shape[0]
    source = lax.broadcasted_iota(jnp.int32, (span, span), 0)
    target = lax.broadcasted_iota(jnp.int32, (span, span), 1)
    gap = (target - source).astype(f32)
    for slot in range(4):
        rate = log_rate(exp_ref[4 * group + slot], length)
        lanes = pl.ds(slot * WIDTH, WIDTH)
        query, key = query_ref[:, lanes], key_ref[:, lanes]
        value, grad = value_ref[:, lanes], grad_ref[:, lanes]
        mask = jnp.where(gap >= 0.0, jnp.exp(rate * jnp.maximum(gap, 0.0)), 0.0)
        grad_scores = jnp.concatenate(halves(dot(value, grad, ((1,), (1,))) * mask), 1)
        key_scores = jnp.concatenate(halves(dot(key, query, ((1,), (1,))) * mask), 1)
        gk_ref[:, lanes] = dot(grad_scores, jnp.concatenate((query, query), 0), ((1,), (0,)))
        gv_ref[:, lanes] = dot(key_scores, jnp.concatenate((grad, grad), 0), ((1,), (0,)))


def key_value_kernel(
    here_ref, exp_ref, key_ref, value_ref, inner_gk_ref, inner_gv_ref, mine_ref, other_ref,
    gk_ref, gv_ref, send_ref, *, length
):
    group = pl.program_id(0)
    span = key_ref.shape[0]
    left = span - lax.broadcasted_iota(jnp.int32, (span, WIDTH), 0).astype(f32)
    for slot in range(4):
        rate = log_rate(exp_ref[4 * group + slot], length)
        lanes = pl.ds(slot * WIDTH, WIDTH)
        key, value = key_ref[:, lanes], value_ref[:, lanes]
        tail = jnp.exp(rate * left)
        high, low = halves(picked(here_ref, mine_ref, other_ref, slot))
        gk = inner_gk_ref[:, lanes] + tail * dot(
            jnp.concatenate((value, value), 1), jnp.concatenate((high, low), 1), ((1,), (1,))
        )
        gv = inner_gv_ref[:, lanes] + tail * dot(
            jnp.concatenate((key, key), 1), jnp.concatenate((high, low), 0), ((1,), (0,))
        )
        gk_ref[:, lanes] = gk.astype(bf16)
        gv_ref[:, lanes] = gv.astype(bf16)
        send_ref[slot, 0] = gk.astype(bf16)
        send_ref[4 + slot, 0] = gv.astype(bf16)


def query_kernel(
    here_ref, exp_ref, key_ref, value_ref, grad_ref, mine_ref, other_ref, gq_ref, *, length
):
    group = pl.program_id(0)
    span = key_ref.shape[0]
    target = lax.broadcasted_iota(jnp.int32, (span, span), 0)
    source = lax.broadcasted_iota(jnp.int32, (span, span), 1)
    gap = (target - source).astype(f32)
    done = 1.0 + lax.broadcasted_iota(jnp.int32, (span, WIDTH), 0).astype(f32)
    for slot in range(4):
        rate = log_rate(exp_ref[4 * group + slot], length)
        lanes = pl.ds(slot * WIDTH, WIDTH)
        key, value, grad = key_ref[:, lanes], value_ref[:, lanes], grad_ref[:, lanes]
        mask = jnp.where(gap >= 0.0, jnp.exp(rate * jnp.maximum(gap, 0.0)), 0.0)
        scores = jnp.concatenate(halves(dot(grad, value, ((1,), (1,))) * mask), 1)
        high, low = halves(picked(here_ref, mine_ref, other_ref, slot))
        gq = jnp.exp(rate * done) * dot(
            jnp.concatenate((grad, grad), 1), jnp.concatenate((high, low), 1), ((1,), (1,))
        )
        gq = gq + dot(scores, jnp.concatenate((key, key), 0), ((1,), (0,)))
        gq_ref[:, lanes] = gq.astype(bf16)


def turn_kernel(rows_ref, after_ref, out_ref):
    out_ref[...] = rows_ref[...].T


def weight_kernel(cols_ref, turned_ref, out_ref):
    product = dot(turned_ref[...], cols_ref[...], ((1,), (0,)))
    out_ref[0] = product[:, :WIDTH]
    out_ref[1] = product[:, WIDTH:]


SMEM = pl.BlockSpec(memory_space=pltpu.SMEM)
FREE = pl.BlockSpec(memory_space=pl.ANY)


def exchange(array, axes):
    return lax.all_to_all(array, axes, split_axis=0, concat_axis=0, tiled=True)


def swap(array, axis):
    return lax.ppermute(array, axis, [(0, 1), (1, 0)])


def call(
    kernel, grid, in_specs, out_specs, out_shape, args, arrived=(), scratch=(), name=None, vmem=8
):
    args = [
        arg
        if spec is SMEM or any(arg is item for item in arrived)
        else pltpu.with_memory_space_constraint(arg, pltpu.HBM)
        for spec, arg in zip(in_specs, args)
    ]
    out_shape = jax.tree.map(lambda leaf: pltpu.HBM(leaf.shape, leaf.dtype), out_shape)
    return pl.pallas_call(
        kernel,
        grid=grid,
        in_specs=in_specs,
        out_specs=out_specs,
        out_shape=out_shape,
        scratch_shapes=scratch,
        name=name,
        compiler_params=pltpu.CompilerParams(vmem_limit_bytes=vmem * 1024 * 1024),
    )(*args)


def per_device(inputs_x, queries, keys, values, grad_out, decay_exp, state_in):
    span = queries.shape[1]
    features = queries.shape[2]
    groups = features // (4 * WIDTH)
    length = span * lax.axis_size(CHAIN)
    tile = (WIDTH, WIDTH)
    query, key, value, grad = queries[0], keys[0], values[0], grad_out[0]
    exps = lax.all_gather(decay_exp, CHAIN, axis=0, tiled=True)
    here = jnp.stack([lax.axis_index(axis) for axis in (LINE, "xl", "core")]).astype(jnp.int32)
    rows = lax.all_gather(inputs_x[0], PLANE, axis=0, tiled=True)

    head_cols = pl.BlockSpec((span, 4 * WIDTH), lambda i: (0, i))
    pair_tiles = pl.BlockSpec((1, 2) + tile, lambda i: (i, 0, 0, 0))
    line_tile = pl.BlockSpec((1,) + tile, lambda i: (i, 0, 0))
    line = pl.BlockSpec((groups,) + tile, lambda i: (0, 0, 0))
    single = pl.BlockSpec(tile, lambda i: (0, 0))
    pair_shape = jax.ShapeDtypeStruct((groups, 2) + tile, f32)
    line_shape = jax.ShapeDtypeStruct((groups,) + tile, f32)
    tile_shape = jax.ShapeDtypeStruct(tile, f32)
    token_shape = jax.ShapeDtypeStruct((span, features), bf16)

    arrived = []

    def noted(array):
        arrived.append(array)
        return array

    def run(body, grid, in_specs, out_specs, out_shape, args, after=None, name=None, **sizes):
        if after is not None:
            in_specs, args = in_specs + [FREE], args + (after,)
        return call(
            functools.partial(body, length=length, **sizes), grid, in_specs, out_specs, out_shape,
            args, arrived, name=name,
        )

    def updates(left, right, reverse, after=None):
        return run(
            update_kernel, (groups,), [SMEM, SMEM, head_cols, head_cols], [pair_tiles, pair_tiles],
            [pair_shape, pair_shape], (here, exps, left, right), after,
            reverse=reverse, name="updates",
        )

    def chip(mine, other, reverse, after=None):
        return run(
            chip_kernel, (groups,), [SMEM, SMEM, pair_tiles, pair_tiles], [line_tile, line_tile],
            [line_shape, line_shape], (here, exps, mine, other), after,
            reverse=reverse, span=float(span), name="chip",
        )

    def chip_state(edges, mine, other, reverse, after=None):
        return run(
            chip_state_kernel, (1,), [SMEM, SMEM, line, line, line], [line, line],
            [line_shape, line_shape], (here, exps, edges, mine, other), after,
            reverse=reverse, span=2.0 * span, name="chip_state",
        )

    def core_state(mine_edge, other_edge, mine, other, reverse, after=None):
        return run(
            core_state_kernel, (groups,),
            [SMEM, SMEM, line_tile, line_tile, pair_tiles, pair_tiles], [pair_tiles, pair_tiles],
            [pair_shape, pair_shape], (here, exps, mine_edge, other_edge, mine, other), after,
            reverse=reverse, span=float(span), name="core_state",
        )

    r_mine, sent = updates(query, grad, True)
    r_other = noted(swap(sent, "core"))
    r_chip, sent = chip(r_mine, r_other, True)
    r_next = noted(swap(sent, "xl"))
    f_mine, sent = updates(key, value, False, r_mine)
    f_other = noted(swap(sent, "core"))
    r_quad = run(
        quad_kernel, (1,), [SMEM, SMEM, line, line], line, line_shape,
        (here, exps, r_chip, r_next), r_mine, span=2.0 * span, name="quad",
    )
    f_chip, sent = chip(f_mine, f_other, False, r_quad)
    f_next = noted(swap(sent, "xl"))
    r_quad, f_chip = lax.optimization_barrier((r_quad, f_chip))
    r_parts = noted(exchange(r_quad, LINE))
    r_edges, state_grad = run(
        scan_kernel, (1,), [SMEM, line], [line, single], [line_shape, tile_shape],
        (decay_exp, r_parts), f_next, span=4.0 * span, name="scan",
    )
    inner_shape = jax.ShapeDtypeStruct((span, features), f32)
    inner_gk, inner_gv = run(
        inner_kernel, (groups,), [SMEM] + 4 * [head_cols], 2 * [head_cols], 2 * [inner_shape],
        (exps, query, key, value, grad), r_edges, name="inner",
    )
    r_edges = noted(exchange(r_edges, LINE))
    r_edge, sent = chip_state(r_edges, r_chip, r_next, True, inner_gk)
    r_far = noted(swap(sent, "xl"))
    mine, sent = core_state(r_edge, r_far, r_mine, r_other, True)
    other = noted(swap(sent, "core"))
    f_parts = lax.all_gather(run(
        line_kernel, (1,), [SMEM, SMEM, line, line, single],
        pl.BlockSpec((groups + 1,) + tile, lambda i: (0, 0, 0)),
        jax.ShapeDtypeStruct((groups + 1,) + tile, f32),
        (here, exps, f_chip, f_next, state_in[0, 0]), mine, span=2.0 * span, name="line",
    ), LINE)
    grad_key, grad_value, send = run(
        key_value_kernel, (groups,), [SMEM, SMEM] + 4 * [head_cols] + 2 * [pair_tiles],
        [head_cols, head_cols, pl.BlockSpec((8, 1, span, WIDTH), lambda i: (0, i % 4, 0, i // 4))],
        [token_shape, token_shape, jax.ShapeDtypeStruct((8, 4, span, 2 * WIDTH), bf16)],
        (here, exps, key, value, inner_gk, inner_gv, mine, other), name="key_value",
    )
    cols = exchange(send.reshape(32, span, 2 * WIDTH), PLANE)
    cols = noted(cols.reshape(32 * span, 2 * WIDTH))

    tokens, width = rows.shape
    block = width // 4
    turned = call(
        turn_kernel, (width // 256,), [pl.BlockSpec((tokens, 256), lambda i: (0, i)), FREE],
        pl.BlockSpec((256, tokens), lambda i: (i, 0)),
        jax.ShapeDtypeStruct((width, tokens), bf16), (rows, send), name="turn", vmem=16,
    )
    partial = call(
        weight_kernel, (4,),
        [
            pl.BlockSpec((tokens, 2 * WIDTH), lambda i: (0, 0)),
            pl.BlockSpec((block, tokens), lambda i: (i, 0)),
        ],
        pl.BlockSpec((2, block, WIDTH), lambda i: (i, 0, 0)),
        jax.ShapeDtypeStruct((8, block, WIDTH), f32), (cols, turned), arrived, name="weight", vmem=32,
    )
    f_edges = run(
        edge_kernel, (groups,),
        [
            SMEM, SMEM, pl.BlockSpec((groups, 1) + tile, lambda i: (0, i, 0, 0)),
            pl.BlockSpec((1, 1) + tile, lambda i: (i, groups, 0, 0)),
        ],
        line_tile, line_shape, (here, exps, f_parts, f_parts), partial,
        span=4.0 * span, name="edge",
    )
    f_edge, sent = chip_state(f_edges, f_chip, f_next, False)
    f_far = noted(swap(sent, "xl"))
    mine, sent = core_state(f_edge, f_far, f_mine, f_other, False)
    other = noted(swap(sent, "core"))
    grad_query = run(
        query_kernel, (groups,), [SMEM, SMEM] + 3 * [head_cols] + 2 * [pair_tiles], head_cols,
        token_shape, (here, exps, key, value, grad, mine, other), name="query",
    )
    summed = lax.psum_scatter(partial, LINE, scatter_dimension=0, tiled=True)
    summed, grad_query = lax.optimization_barrier((summed, grad_query))
    pieces = exchange(summed.reshape(8, block // 8, WIDTH), ("y", "xh"))
    pieces = pieces.reshape(2, 4, block // 8, WIDTH).transpose(0, 2, 1, 3)
    weight_grads = pieces.reshape(2, 1, block // 8, 4 * WIDTH)
    return (
        grad_query[None], grad_key[None], grad_value[None], weight_grads, state_grad[None, None]
    )


def solution(mesh):
    fine = Mesh(mesh.devices.reshape(4, 2, 4, 2, 2, 2), ("y", "xh", "zh", "zl", "xl", "core"))
    dp, seq = ("y", "xh"), CHAIN
    tokens = P(dp, seq, None)
    in_specs = (tokens, tokens, tokens, tokens, tokens, P(seq), P(dp, seq, None, None))
    out_specs = (tokens, tokens, tokens, P(None, seq, dp, None), P(dp, seq, None, None))
    return jax.shard_map(
        per_device, mesh=fine, in_specs=in_specs, out_specs=out_specs, check_vma=False
    )
```

```python
import functools

import jax
import jax.numpy as jnp
from jax import lax
from jax.experimental import pallas as pl
from jax.experimental.pallas import tpu as pltpu
from jax.sharding import Mesh
from jax.sharding import PartitionSpec as P

WIDTH = 128
f32 = jnp.float32
bf16 = jnp.bfloat16
PLANE = ("y", "xh", "xl", "core")
QUAD = ("xl", "core")
LINE = ("zh", "zl")
CHIPS = ("zh", "zl", "xl")
CHAIN = ("zh", "zl", "xl", "core")
OWNERS = ("y", "xh", "zh", "zl")


def log_rate(exponent, length):
    return -(jnp.left_shift(1, exponent).astype(f32)) * (1.0 / length)


def power_of(rate, steps):
    return jnp.exp(jnp.full((1, WIDTH), rate * steps, f32))


def halves(wide):
    high = wide.astype(bf16)
    return high, (wide - high.astype(f32)).astype(bf16)


def dot(left, right, dims):
    return lax.dot_general(left, right, (dims, ((), ())), preferred_element_type=f32)


def groups_of(ref):
    count = ref.shape[0]
    return [(item, pl.program_id(0) * count + item) for item in range(count)]


def update_kernel(here_ref, exp_ref, left_ref, right_ref, *refs, reverse, length):
    keep_ref, send_ref = refs[-2:]
    span = left_ref.shape[0]
    rows = lax.broadcasted_iota(jnp.int32, (span, WIDTH), 0).astype(f32)
    steps = rows if reverse else (span - 1.0) - rows
    for item, group in groups_of(keep_ref):
        for core, out_ref in enumerate((keep_ref, send_ref)):
            for chip in range(2):
                slot = 2 * jnp.bitwise_xor(here_ref[1], chip) + jnp.bitwise_xor(here_ref[2], core)
                rate = log_rate(exp_ref[4 * group + slot], length)
                start = pl.multiple_of((4 * item + slot) * WIDTH, WIDTH)
                lanes = pl.ds(start, WIDTH)
                high, low = halves(left_ref[:, lanes].astype(f32) * jnp.exp(rate * steps))
                right = right_ref[:, lanes]
                out_ref[item, chip] = dot(
                    jnp.concatenate((high, low), 0), jnp.concatenate((right, right), 0),
                    ((0,), (0,)),
                )


def weighed(mine, other, position, reverse, rate, span):
    position = position.astype(f32)
    later = position if reverse else 1.0 - position
    return power_of(rate, span * later) * mine + power_of(rate, span * (1.0 - later)) * other


def chip_kernel(here_ref, exp_ref, mine_ref, other_ref, *refs, reverse, length, span):
    keep_ref, send_ref = refs[-2:]
    for item, group in groups_of(keep_ref):
        for chip, out_ref in enumerate((keep_ref, send_ref)):
            head = 4 * group + 2 * jnp.bitwise_xor(here_ref[1], chip) + here_ref[2]
            out_ref[item] = weighed(
                mine_ref[item, chip], other_ref[item, chip], here_ref[2], reverse,
                log_rate(exp_ref[head], length), span,
            )


def pair_kernel(here_ref, exp_ref, mine_ref, other_ref, out_ref, *, length, span):
    for item, group in groups_of(out_ref):
        for chip in range(2):
            rate = log_rate(exp_ref[4 * group + 2 * chip + here_ref[2]], length)
            out_ref[item, chip] = weighed(
                mine_ref[item, chip], other_ref[item, chip], here_ref[2], True, rate, span
            )


def scan_kernel(own_ref, parts_ref, after_ref, out_ref, grad_ref, *, length, span):
    rate = log_rate(own_ref[0], length)
    decay = power_of(rate, span)
    state = jnp.zeros(grad_ref.shape, f32)
    for group in reversed(range(parts_ref.shape[0])):
        for chip in (1, 0):
            out_ref[group, chip] = state
            state = decay * state + parts_ref[group, chip]
    grad_ref[...] = power_of(rate, 1.0) * state


def line_kernel(
    here_ref, exp_ref, mine_ref, other_ref, after_ref, keep_ref, send_ref, *, length, span
):
    parity = here_ref[0] % 2
    for half, out_ref in enumerate((keep_ref, send_ref)):
        for item in range(out_ref.shape[0]):
            group = 2 * item + jnp.bitwise_xor(parity, half)
            rate = log_rate(exp_ref[4 * group + 2 * here_ref[1] + here_ref[2]], length)
            out_ref[item] = weighed(
                mine_ref[group], other_ref[group], here_ref[1], False, rate, span
            )


def own_rate(here_ref, exp_ref, item, length):
    group = 2 * item + here_ref[0] % 2
    return log_rate(exp_ref[4 * group + 2 * here_ref[1] + here_ref[2]], length)


def line_pair_kernel(
    here_ref, exp_ref, mine_ref, other_ref, first_ref, out_ref, *, length, span
):
    count = mine_ref.shape[0]
    for item in range(count):
        rate = own_rate(here_ref, exp_ref, item, length)
        out_ref[item] = weighed(
            mine_ref[item], other_ref[item], here_ref[0] % 2, False, rate, span
        )
    out_ref[count] = first_ref[...]


def edge_kernel(
    here_ref, exp_ref, parts_ref, mine_ref, other_ref, after_ref, keep_ref, send_ref,
    *, length, span
):
    count = mine_ref.shape[0]
    behind = here_ref[0] % 2 == 1
    for item in range(count):
        rate = own_rate(here_ref, exp_ref, item, length)
        decay = power_of(rate, 2.0 * span)
        state = parts_ref[item, count]
        for before in range(count - 1):
            update = decay * state + parts_ref[before, item]
            state = jnp.where(here_ref[0] // 2 > before, update, state)
        past = power_of(rate, span) * state
        keep_ref[item] = jnp.where(behind, past + other_ref[item], state)
        send_ref[item] = jnp.where(behind, state, past + mine_ref[item])


def chip_state_kernel(
    here_ref, exp_ref, mine_edge_ref, other_edge_ref, mine_ref, other_ref, keep_ref, send_ref,
    *, length, span
):
    behind = here_ref[1] == 1
    for group in range(keep_ref.shape[0]):
        rate = log_rate(exp_ref[4 * group + 2 * here_ref[1] + here_ref[2]], length)
        edge = jnp.where(
            here_ref[0] % 2 == group % 2, mine_edge_ref[group // 2], other_edge_ref[group // 2]
        )
        past = power_of(rate, span) * edge
        keep_ref[group] = jnp.where(behind, past + other_ref[group], edge)
        send_ref[group] = jnp.where(behind, edge, past + mine_ref[group])


def core_state_kernel(here_ref, exp_ref, mine_ref, other_ref, *refs, reverse, count, length, span):
    edge_refs, (keep_ref, send_ref) = refs[:count], refs[-2:]
    behind = here_ref[2] == (0 if reverse else 1)
    for item, group in groups_of(keep_ref):
        for chip in range(2):
            head = 4 * group + 2 * jnp.bitwise_xor(here_ref[1], chip) + here_ref[2]
            rate = log_rate(exp_ref[head], length)
            edge = edge_refs[0][item, chip] if count == 1 else edge_refs[chip][item]
            past = power_of(rate, span) * edge
            keep_ref[item, chip] = jnp.where(behind, past + other_ref[item, chip], edge)
            send_ref[item, chip] = jnp.where(behind, edge, past + mine_ref[item, chip])


def picked(here_ref, mine_ref, other_ref, item, slot):
    chip = jnp.bitwise_xor(here_ref[1], slot // 2)
    return jnp.where(here_ref[2] == slot % 2, mine_ref[item, chip], other_ref[item, chip])


def heads_of(ref):
    count = ref.shape[1] // (4 * WIDTH)
    first = pl.program_id(0) * count
    return [
        (item, slot, 4 * (first + item) + slot, pl.ds((4 * item + slot) * WIDTH, WIDTH))
        for item in range(count)
        for slot in range(4)
    ]


def inner_kernel(
    exp_ref, query_ref, key_ref, value_ref, grad_ref, after_ref, gk_ref, gv_ref, *, length
):
    span = query_ref.shape[0]
    source = lax.broadcasted_iota(jnp.int32, (span, span), 0)
    target = lax.broadcasted_iota(jnp.int32, (span, span), 1)
    gap = (target - source).astype(f32)
    for item, slot, head, lanes in heads_of(query_ref):
        rate = log_rate(exp_ref[head], length)
        query, key = query_ref[:, lanes], key_ref[:, lanes]
        value, grad = value_ref[:, lanes], grad_ref[:, lanes]
        mask = jnp.where(gap >= 0.0, jnp.exp(rate * jnp.maximum(gap, 0.0)), 0.0)
        grad_scores = jnp.concatenate(halves(dot(value, grad, ((1,), (1,))) * mask), 1)
        key_scores = jnp.concatenate(halves(dot(key, query, ((1,), (1,))) * mask), 1)
        gk_ref[:, lanes] = dot(grad_scores, jnp.concatenate((query, query), 0), ((1,), (0,)))
        gv_ref[:, lanes] = dot(key_scores, jnp.concatenate((grad, grad), 0), ((1,), (0,)))


def key_value_kernel(
    here_ref, exp_ref, key_ref, value_ref, inner_gk_ref, inner_gv_ref, mine_ref, other_ref,
    gk_ref, gv_ref, send_ref, *, length
):
    span = key_ref.shape[0]
    left = span - lax.broadcasted_iota(jnp.int32, (span, WIDTH), 0).astype(f32)
    for item, slot, head, lanes in heads_of(key_ref):
        rate = log_rate(exp_ref[head], length)
        key, value = key_ref[:, lanes], value_ref[:, lanes]
        tail = jnp.exp(rate * left)
        high, low = halves(picked(here_ref, mine_ref, other_ref, item, slot))
        gk = inner_gk_ref[:, lanes] + tail * dot(
            jnp.concatenate((value, value), 1), jnp.concatenate((high, low), 1), ((1,), (1,))
        )
        gv = inner_gv_ref[:, lanes] + tail * dot(
            jnp.concatenate((key, key), 1), jnp.concatenate((high, low), 0), ((1,), (0,))
        )
        gk_ref[:, lanes] = gk.astype(bf16)
        gv_ref[:, lanes] = gv.astype(bf16)
        send_ref[slot, item] = gk.astype(bf16)
        send_ref[4 + slot, item] = gv.astype(bf16)


def query_kernel(
    here_ref, exp_ref, key_ref, value_ref, grad_ref, mine_ref, other_ref, gq_ref, *, length
):
    span = key_ref.shape[0]
    target = lax.broadcasted_iota(jnp.int32, (span, span), 0)
    source = lax.broadcasted_iota(jnp.int32, (span, span), 1)
    gap = (target - source).astype(f32)
    done = 1.0 + lax.broadcasted_iota(jnp.int32, (span, WIDTH), 0).astype(f32)
    for item, slot, head, lanes in heads_of(key_ref):
        rate = log_rate(exp_ref[head], length)
        key, value, grad = key_ref[:, lanes], value_ref[:, lanes], grad_ref[:, lanes]
        mask = jnp.where(gap >= 0.0, jnp.exp(rate * jnp.maximum(gap, 0.0)), 0.0)
        scores = jnp.concatenate(halves(dot(grad, value, ((1,), (1,))) * mask), 1)
        high, low = halves(picked(here_ref, mine_ref, other_ref, item, slot))
        gq = jnp.exp(rate * done) * dot(
            jnp.concatenate((grad, grad), 1), jnp.concatenate((high, low), 1), ((1,), (1,))
        )
        gq = gq + dot(scores, jnp.concatenate((key, key), 0), ((1,), (0,)))
        gq_ref[:, lanes] = gq.astype(bf16)


def weight_kernel(cols_ref, rows_ref, out_ref, turned):
    @pl.when(pl.program_id(0) == 0)
    def _():
        turned[...] = cols_ref[...].T

    product = dot(turned[...], rows_ref[...], ((1,), (0,))).T.astype(bf16)
    count = out_ref.shape[2]
    for item in range(out_ref.shape[0]):
        rows = product[item * count : (item + 1) * count]
        out_ref[item, 0] = rows[:, :WIDTH]
        out_ref[item, 1] = rows[:, WIDTH:]


def total_kernel(parts_ref, out_ref):
    for owner in range(parts_ref.shape[0]):
        total = parts_ref[owner, 0].astype(f32)
        for item in range(1, parts_ref.shape[1]):
            total = total + parts_ref[owner, item].astype(f32)
        out_ref[0, 0, :, owner * WIDTH : (owner + 1) * WIDTH] = total


SMEM = pl.BlockSpec(memory_space=pltpu.SMEM)
FREE = pl.BlockSpec(memory_space=pl.ANY)


def exchange(array, axes):
    return lax.all_to_all(array, axes, split_axis=0, concat_axis=0, tiled=True)


def swap(array, axis):
    return lax.ppermute(array, axis, [(0, 1), (1, 0)])


def far(array):
    return pltpu.with_memory_space_constraint(array, pltpu.HBM)


def call(kernel, grid, in_specs, out_specs, out_shape, args, scratch=(), name=None, vmem=24):
    return pl.pallas_call(
        kernel,
        grid=grid,
        in_specs=in_specs,
        out_specs=out_specs,
        out_shape=out_shape,
        scratch_shapes=scratch,
        name=name,
        compiler_params=pltpu.CompilerParams(vmem_limit_bytes=vmem * 1024 * 1024),
    )(*args)


def per_device(inputs_x, queries, keys, values, grad_out, decay_exp, state_in):
    span = queries.shape[1]
    features = queries.shape[2]
    groups = features // (4 * WIDTH)
    length = span * lax.axis_size(CHAIN)
    tile = (WIDTH, WIDTH)
    query, key, value, grad = queries[0], keys[0], values[0], grad_out[0]
    exps = lax.all_gather(decay_exp, CHAIN, axis=0, tiled=True)
    here = jnp.stack([lax.axis_index(axis) for axis in (LINE, "xl", "core")]).astype(jnp.int32)
    rows = lax.all_gather(inputs_x[0], PLANE, axis=0, tiled=True)

    head_cols = pl.BlockSpec((span, features // 2), lambda i: (0, i))
    pair_tiles = pl.BlockSpec((groups // 2, 2) + tile, lambda i: (i, 0, 0, 0))
    line_tile = pl.BlockSpec((groups // 2,) + tile, lambda i: (i, 0, 0))
    line = pl.BlockSpec((groups,) + tile, lambda i: (0, 0, 0))
    single = pl.BlockSpec(tile, lambda i: (0, 0))
    pair_kept, pair_sent = pltpu.HBM((groups, 2) + tile, f32), pltpu.HBM((groups, 2) + tile, f32)
    line_kept, line_sent = pltpu.HBM((groups,) + tile, f32), pltpu.HBM((groups,) + tile, f32)
    tile_shape = pltpu.HBM(tile, f32)
    token_shape = pltpu.HBM((span, features), bf16)

    arrived = []

    def noted(array):
        arrived.append(array)
        return array

    def run(body, grid, in_specs, out_specs, out_shape, args, after=None, name=None, **sizes):
        if after is not None:
            in_specs, args = in_specs + [FREE], args + (after,)
        args = [
            arg
            if spec is SMEM or any(arg is item for item in arrived)
            else far(arg)
            for spec, arg in zip(in_specs, args)
        ]
        return call(
            functools.partial(body, length=length, **sizes), grid, in_specs, out_specs, out_shape,
            args, name=name,
        )

    def updates(left, right, where, reverse, after=None):
        return run(
            update_kernel, (2,), [SMEM, SMEM, head_cols, head_cols], [pair_tiles, pair_tiles],
            [pair_kept, pair_sent], (where, exps, left, right), after,
            reverse=reverse, name="updates",
        )

    def chip(mine, other, reverse, after=None):
        return run(
            chip_kernel, (2,), [SMEM, SMEM, pair_tiles, pair_tiles], [line_tile, line_tile],
            [line_kept, line_sent], (here, exps, mine, other), after,
            reverse=reverse, span=float(span), name="chip",
        )

    def core_state(edges, mine, other, where, reverse, after=None):
        specs = [pair_tiles] if len(edges) == 1 else [line_tile, line_tile]
        return run(
            core_state_kernel, (2,), [SMEM, SMEM, pair_tiles, pair_tiles] + specs,
            [pair_tiles, pair_tiles], [pair_kept, pair_sent],
            (where, exps, mine, other, *edges), after,
            reverse=reverse, count=len(edges), span=float(span), name="core_state",
        )

    inner_shape = pltpu.HBM((span, features), f32)
    even = here * jnp.array([1, 0, 1], jnp.int32)
    r_mine, sent = updates(query, grad, even, True)
    r_other = noted(swap(sent, "core"))
    r_pair = run(
        pair_kernel, (2,), [SMEM, SMEM, pair_tiles, pair_tiles], pair_tiles, pair_sent,
        (here, exps, r_mine, r_other), span=float(span), name="pair",
    )
    f_mine, sent = updates(key, value, here, False, r_mine)
    f_other = noted(swap(sent, "core"))
    r_parts = exchange(r_pair.reshape((2 * groups,) + tile), CHIPS)
    r_parts = noted(r_parts.reshape((groups, 2) + tile))
    f_chip, sent = chip(f_mine, f_other, False, r_pair)
    f_next = noted(swap(sent, "xl"))
    all_pairs = pl.BlockSpec((groups, 2) + tile, lambda i: (0, 0, 0, 0))
    r_edges, state_grad = run(
        scan_kernel, (1,), [SMEM, all_pairs], [all_pairs, single], [pair_sent, tile_shape],
        (decay_exp, r_parts), f_chip, span=2.0 * span, name="scan",
    )
    inner_gk, inner_gv = run(
        inner_kernel, (2,), [SMEM] + 4 * [head_cols], 2 * [head_cols], 2 * [inner_shape],
        (exps, query, key, value, grad), r_edges, name="inner",
    )
    r_edges = exchange(r_edges.reshape((2 * groups,) + tile), CHIPS)
    r_edges = noted(r_edges.reshape((groups, 2) + tile))
    mine, sent = core_state([r_edges], r_mine, r_other, even, True, inner_gk)
    other = noted(swap(sent, "core"))
    quarter = pl.BlockSpec((4,) + tile, lambda i: (0, 0, 0))
    quarter_shape = pltpu.HBM((4,) + tile, f32)
    f_line, sent = run(
        line_kernel, (1,), [SMEM, SMEM, line, line], [quarter, quarter],
        [quarter_shape, quarter_shape], (here, exps, f_chip, f_next), mine,
        span=2.0 * span, name="line",
    )
    f_beside = noted(swap(sent, "zl"))
    f_parts = lax.all_gather(run(
        line_pair_kernel, (1,), [SMEM, SMEM, quarter, quarter, single],
        pl.BlockSpec((5,) + tile, lambda i: (0, 0, 0)), pltpu.HBM((5,) + tile, f32),
        (here, exps, f_line, f_beside, state_in[0, 0]), span=4.0 * span, name="line_pair",
    ), "zh")
    grad_key, grad_value, send = run(
        key_value_kernel, (2,), [SMEM, SMEM] + 4 * [head_cols] + 2 * [pair_tiles],
        [head_cols, head_cols, pl.BlockSpec((8, 4, span, WIDTH), lambda i: (0, 0, 0, i))],
        [token_shape, token_shape, pltpu.HBM((8, 4, span, 2 * WIDTH), bf16)],
        (even, exps, key, value, inner_gk, inner_gv, mine, other), name="key_value",
    )
    cols = exchange(send.reshape(32, span, 2 * WIDTH), PLANE)
    cols = cols.reshape(32 * span, 2 * WIDTH)

    tokens, width = rows.shape
    block = width // 4
    partial = call(
        weight_kernel, (4,),
        [
            pl.BlockSpec((tokens, 2 * WIDTH), lambda i: (0, 0)),
            pl.BlockSpec((tokens, block), lambda i: (0, i)),
        ],
        pl.BlockSpec((8, 2, block // 8, WIDTH), lambda i: (0, i, 0, 0)),
        pltpu.HBM((8, 8, block // 8, WIDTH), bf16), (cols, far(rows)), scratch=[pltpu.VMEM((2 * WIDTH, tokens), bf16)], name="weight", vmem=40,
    )
    f_edge, sent = run(
        edge_kernel, (1,),
        [SMEM, SMEM, pl.BlockSpec((4, 5) + tile, lambda i: (0, 0, 0, 0)), quarter, quarter],
        [quarter, quarter], [quarter_shape, quarter_shape],
        (here, exps, f_parts, f_line, f_beside), partial, span=4.0 * span, name="edge",
    )
    f_side = noted(swap(sent, "zl"))
    f_edge, sent = run(
        chip_state_kernel, (1,), [SMEM, SMEM, quarter, quarter, line, line], [line, line],
        [line_kept, line_sent], (here, exps, f_edge, f_side, f_chip, f_next),
        span=2.0 * span, name="chip_state",
    )
    f_far = noted(swap(sent, "xl"))
    mine, sent = core_state([f_edge, f_far], f_mine, f_other, here, False)
    other = noted(swap(sent, "core"))
    grad_query = run(
        query_kernel, (2,), [SMEM, SMEM] + 3 * [head_cols] + 2 * [pair_tiles], head_cols,
        token_shape, (here, exps, key, value, grad, mine, other), name="query",
    )
    share = block // 8
    pieces = exchange(partial.reshape(64, share, WIDTH), OWNERS).reshape(8, 8, share, WIDTH)
    weight_grads = call(
        total_kernel, (2,), [pl.BlockSpec((4, 8, share, WIDTH), lambda i: (i, 0, 0, 0))],
        pl.BlockSpec((1, 1, share, 4 * WIDTH), lambda i: (i, 0, 0, 0)),
        pltpu.HBM((2, 1, share, 4 * WIDTH), f32), (pieces,), name="total",
    )
    return (
        grad_query[None], grad_key[None], grad_value[None], weight_grads, state_grad[None, None]
    )


def solution(mesh):
    fine = Mesh(mesh.devices.reshape(4, 2, 4, 2, 2, 2), ("y", "xh", "zh", "zl", "xl", "core"))
    dp, seq = ("y", "xh"), CHAIN
    tokens = P(dp, seq, None)
    in_specs = (tokens, tokens, tokens, tokens, tokens, P(seq), P(dp, seq, None, None))
    out_specs = (tokens, tokens, tokens, P(None, seq, dp, None), P(dp, seq, None, None))
    return jax.shard_map(
        per_device, mesh=fine, in_specs=in_specs, out_specs=out_specs, check_vma=False
    )
```

```python
import functools

import jax
import jax.numpy as jnp
from jax import lax
from jax.experimental import pallas as pl
from jax.experimental.pallas import tpu as pltpu
from jax.sharding import Mesh
from jax.sharding import PartitionSpec as P

WIDTH = 128
f32 = jnp.float32
bf16 = jnp.bfloat16
PLANE = ("y", "xh", "xl", "core")
QUAD = ("xl", "core")
LINE = ("zh", "zl")
CHIPS = ("zh", "zl", "xl")
CHAIN = ("zh", "zl", "xl", "core")
OWNERS = ("y", "xh", "zh", "zl")


def log_rate(exponent, length):
    return -(jnp.left_shift(1, exponent).astype(f32)) * (1.0 / length)


def power_of(rate, steps):
    return jnp.exp(jnp.full((1, WIDTH), rate * steps, f32))


def halves(wide):
    high = wide.astype(bf16)
    return high, (wide - high.astype(f32)).astype(bf16)


def dot(left, right, dims):
    return lax.dot_general(left, right, (dims, ((), ())), preferred_element_type=f32)


def groups_of(ref):
    count = ref.shape[0]
    return [(item, pl.program_id(0) * count + item) for item in range(count)]


def update_kernel(here_ref, exp_ref, left_ref, right_ref, *refs, reverse, length):
    keep_ref, send_ref = refs[-2:]
    span = left_ref.shape[0]
    rows = lax.broadcasted_iota(jnp.int32, (span, WIDTH), 0).astype(f32)
    steps = rows if reverse else (span - 1.0) - rows
    for item, group in groups_of(keep_ref):
        for core, out_ref in enumerate((keep_ref, send_ref)):
            for chip in range(2):
                slot = 2 * jnp.bitwise_xor(here_ref[1], chip) + jnp.bitwise_xor(here_ref[2], core)
                rate = log_rate(exp_ref[4 * group + slot], length)
                start = pl.multiple_of((4 * item + slot) * WIDTH, WIDTH)
                lanes = pl.ds(start, WIDTH)
                high, low = halves(left_ref[:, lanes].astype(f32) * jnp.exp(rate * steps))
                right = right_ref[:, lanes]
                out_ref[item, chip] = dot(
                    jnp.concatenate((high, low), 0), jnp.concatenate((right, right), 0),
                    ((0,), (0,)),
                )


def weighed(mine, other, position, reverse, rate, span):
    position = position.astype(f32)
    later = position if reverse else 1.0 - position
    return power_of(rate, span * later) * mine + power_of(rate, span * (1.0 - later)) * other


def chip_kernel(here_ref, exp_ref, mine_ref, other_ref, *refs, reverse, length, span):
    keep_ref, send_ref = refs[-2:]
    for item, group in groups_of(keep_ref):
        for chip, out_ref in enumerate((keep_ref, send_ref)):
            head = 4 * group + 2 * jnp.bitwise_xor(here_ref[1], chip) + here_ref[2]
            out_ref[item] = weighed(
                mine_ref[item, chip], other_ref[item, chip], here_ref[2], reverse,
                log_rate(exp_ref[head], length), span,
            )


def pair_kernel(here_ref, exp_ref, mine_ref, other_ref, out_ref, *, length, span):
    for item, group in groups_of(out_ref):
        for chip in range(2):
            rate = log_rate(exp_ref[4 * group + 2 * chip + here_ref[2]], length)
            out_ref[item, chip] = weighed(
                mine_ref[item, chip], other_ref[item, chip], here_ref[2], True, rate, span
            )


def scan_kernel(own_ref, parts_ref, after_ref, out_ref, grad_ref, *, length, span):
    rate = log_rate(own_ref[0], length)
    decay = power_of(rate, span)
    state = jnp.zeros(grad_ref.shape, f32)
    for group in reversed(range(parts_ref.shape[0])):
        for chip in (1, 0):
            out_ref[group, chip] = state
            state = decay * state + parts_ref[group, chip]
    grad_ref[...] = power_of(rate, 1.0) * state


def line_kernel(
    here_ref, exp_ref, mine_ref, other_ref, after_ref, keep_ref, send_ref, *, length, span
):
    parity = here_ref[0] % 2
    for half, out_ref in enumerate((keep_ref, send_ref)):
        for item in range(out_ref.shape[0]):
            group = 2 * item + jnp.bitwise_xor(parity, half)
            rate = log_rate(exp_ref[4 * group + 2 * here_ref[1] + here_ref[2]], length)
            out_ref[item] = weighed(
                mine_ref[group], other_ref[group], here_ref[1], False, rate, span
            )


def own_rate(here_ref, exp_ref, item, length):
    group = 2 * item + here_ref[0] % 2
    return log_rate(exp_ref[4 * group + 2 * here_ref[1] + here_ref[2]], length)


def line_pair_kernel(
    here_ref, exp_ref, mine_ref, other_ref, first_ref, *refs, length, span
):
    out_ref = refs[-1]
    count = mine_ref.shape[0]
    for item in range(count):
        rate = own_rate(here_ref, exp_ref, item, length)
        out_ref[item] = weighed(
            mine_ref[item], other_ref[item], here_ref[0] % 2, False, rate, span
        )
    out_ref[count] = first_ref[...]


def edge_kernel(
    here_ref, exp_ref, parts_ref, mine_ref, other_ref, after_ref, keep_ref, send_ref,
    *, length, span
):
    count = mine_ref.shape[0]
    behind = here_ref[0] % 2 == 1
    for item in range(count):
        rate = own_rate(here_ref, exp_ref, item, length)
        decay = power_of(rate, 2.0 * span)
        state = parts_ref[item, count]
        for before in range(count - 1):
            update = decay * state + parts_ref[before, item]
            state = jnp.where(here_ref[0] // 2 > before, update, state)
        past = power_of(rate, span) * state
        keep_ref[item] = jnp.where(behind, past + other_ref[item], state)
        send_ref[item] = jnp.where(behind, state, past + mine_ref[item])


def chip_state_kernel(
    here_ref, exp_ref, mine_edge_ref, other_edge_ref, mine_ref, other_ref, keep_ref, send_ref,
    *, length, span
):
    behind = here_ref[1] == 1
    for group in range(keep_ref.shape[0]):
        rate = log_rate(exp_ref[4 * group + 2 * here_ref[1] + here_ref[2]], length)
        edge = jnp.where(
            here_ref[0] % 2 == group % 2, mine_edge_ref[group // 2], other_edge_ref[group // 2]
        )
        past = power_of(rate, span) * edge
        keep_ref[group] = jnp.where(behind, past + other_ref[group], edge)
        send_ref[group] = jnp.where(behind, edge, past + mine_ref[group])


def core_state_kernel(here_ref, exp_ref, mine_ref, other_ref, *refs, reverse, count, length, span):
    edge_refs, (keep_ref, send_ref) = refs[:count], refs[-2:]
    behind = here_ref[2] == (0 if reverse else 1)
    for item, group in groups_of(keep_ref):
        for chip in range(2):
            head = 4 * group + 2 * jnp.bitwise_xor(here_ref[1], chip) + here_ref[2]
            rate = log_rate(exp_ref[head], length)
            edge = edge_refs[0][item, chip] if count == 1 else edge_refs[chip][item]
            past = power_of(rate, span) * edge
            keep_ref[item, chip] = jnp.where(behind, past + other_ref[item, chip], edge)
            send_ref[item, chip] = jnp.where(behind, edge, past + mine_ref[item, chip])


def picked(here_ref, mine_ref, other_ref, item, slot):
    chip = jnp.bitwise_xor(here_ref[1], slot // 2)
    return jnp.where(here_ref[2] == slot % 2, mine_ref[item, chip], other_ref[item, chip])


def heads_of(ref):
    count = ref.shape[1] // (4 * WIDTH)
    first = pl.program_id(0) * count
    return [
        (item, slot, 4 * (first + item) + slot, pl.ds((4 * item + slot) * WIDTH, WIDTH))
        for item in range(count)
        for slot in range(4)
    ]


def inner_kernel(
    exp_ref, query_ref, key_ref, value_ref, grad_ref, after_ref, gk_ref, gv_ref, *, length
):
    span = query_ref.shape[0]
    source = lax.broadcasted_iota(jnp.int32, (span, span), 0)
    target = lax.broadcasted_iota(jnp.int32, (span, span), 1)
    gap = (target - source).astype(f32)
    for item, slot, head, lanes in heads_of(query_ref):
        rate = log_rate(exp_ref[head], length)
        query, key = query_ref[:, lanes], key_ref[:, lanes]
        value, grad = value_ref[:, lanes], grad_ref[:, lanes]
        mask = jnp.where(gap >= 0.0, jnp.exp(rate * jnp.maximum(gap, 0.0)), 0.0)
        grad_scores = jnp.concatenate(halves(dot(value, grad, ((1,), (1,))) * mask), 1)
        key_scores = jnp.concatenate(halves(dot(key, query, ((1,), (1,))) * mask), 1)
        gk_ref[:, lanes] = dot(grad_scores, jnp.concatenate((query, query), 0), ((1,), (0,)))
        gv_ref[:, lanes] = dot(key_scores, jnp.concatenate((grad, grad), 0), ((1,), (0,)))


def key_value_kernel(
    here_ref, exp_ref, key_ref, value_ref, inner_gk_ref, inner_gv_ref, mine_ref, other_ref,
    gk_ref, gv_ref, send_ref, *, length
):
    span = key_ref.shape[0]
    left = span - lax.broadcasted_iota(jnp.int32, (span, WIDTH), 0).astype(f32)
    for item, slot, head, lanes in heads_of(key_ref):
        rate = log_rate(exp_ref[head], length)
        key, value = key_ref[:, lanes], value_ref[:, lanes]
        tail = jnp.exp(rate * left)
        high, low = halves(picked(here_ref, mine_ref, other_ref, item, slot))
        gk = inner_gk_ref[:, lanes] + tail * dot(
            jnp.concatenate((value, value), 1), jnp.concatenate((high, low), 1), ((1,), (1,))
        )
        gv = inner_gv_ref[:, lanes] + tail * dot(
            jnp.concatenate((key, key), 1), jnp.concatenate((high, low), 0), ((1,), (0,))
        )
        gk_ref[:, lanes] = gk.astype(bf16)
        gv_ref[:, lanes] = gv.astype(bf16)
        send_ref[slot, item] = gk.astype(bf16)
        send_ref[4 + slot, item] = gv.astype(bf16)


def query_kernel(
    here_ref, exp_ref, key_ref, value_ref, grad_ref, mine_ref, other_ref, gq_ref, *, length
):
    span = key_ref.shape[0]
    target = lax.broadcasted_iota(jnp.int32, (span, span), 0)
    source = lax.broadcasted_iota(jnp.int32, (span, span), 1)
    gap = (target - source).astype(f32)
    done = 1.0 + lax.broadcasted_iota(jnp.int32, (span, WIDTH), 0).astype(f32)
    for item, slot, head, lanes in heads_of(key_ref):
        rate = log_rate(exp_ref[head], length)
        key, value, grad = key_ref[:, lanes], value_ref[:, lanes], grad_ref[:, lanes]
        mask = jnp.where(gap >= 0.0, jnp.exp(rate * jnp.maximum(gap, 0.0)), 0.0)
        scores = jnp.concatenate(halves(dot(grad, value, ((1,), (1,))) * mask), 1)
        high, low = halves(picked(here_ref, mine_ref, other_ref, item, slot))
        gq = jnp.exp(rate * done) * dot(
            jnp.concatenate((grad, grad), 1), jnp.concatenate((high, low), 1), ((1,), (1,))
        )
        gq = gq + dot(scores, jnp.concatenate((key, key), 0), ((1,), (0,)))
        gq_ref[:, lanes] = gq.astype(bf16)


def weight_kernel(cols_ref, rows_ref, out_ref, turned):
    @pl.when(pl.program_id(0) == 0)
    def _():
        turned[...] = cols_ref[...].T

    product = dot(turned[...], rows_ref[...], ((1,), (0,))).T.astype(bf16)
    count = out_ref.shape[2]
    for item in range(out_ref.shape[0]):
        rows = product[item * count : (item + 1) * count]
        out_ref[item, 0] = rows[:, :WIDTH]
        out_ref[item, 1] = rows[:, WIDTH:]


def total_kernel(parts_ref, out_ref):
    for owner in range(parts_ref.shape[0]):
        total = parts_ref[owner, 0].astype(f32)
        for item in range(1, parts_ref.shape[1]):
            total = total + parts_ref[owner, item].astype(f32)
        out_ref[0, 0, :, owner * WIDTH : (owner + 1) * WIDTH] = total


SMEM = pl.BlockSpec(memory_space=pltpu.SMEM)
FREE = pl.BlockSpec(memory_space=pl.ANY)


def exchange(array, axes):
    return lax.all_to_all(array, axes, split_axis=0, concat_axis=0, tiled=True)


def swap(array, axis):
    return lax.ppermute(array, axis, [(0, 1), (1, 0)])


def far(array):
    return pltpu.with_memory_space_constraint(array, pltpu.HBM)


def call(kernel, grid, in_specs, out_specs, out_shape, args, scratch=(), name=None, vmem=24):
    return pl.pallas_call(
        kernel,
        grid=grid,
        in_specs=in_specs,
        out_specs=out_specs,
        out_shape=out_shape,
        scratch_shapes=scratch,
        name=name,
        compiler_params=pltpu.CompilerParams(vmem_limit_bytes=vmem * 1024 * 1024),
    )(*args)


def per_device(inputs_x, queries, keys, values, grad_out, decay_exp, state_in):
    span = queries.shape[1]
    features = queries.shape[2]
    groups = features // (4 * WIDTH)
    length = span * lax.axis_size(CHAIN)
    tile = (WIDTH, WIDTH)
    query, key, value, grad = queries[0], keys[0], values[0], grad_out[0]
    exps = lax.all_gather(decay_exp, CHAIN, axis=0, tiled=True)
    here = jnp.stack([lax.axis_index(axis) for axis in (LINE, "xl", "core")]).astype(jnp.int32)
    rows = lax.all_gather(inputs_x[0], PLANE, axis=0, tiled=True)

    head_cols = pl.BlockSpec((span, features // 2), lambda i: (0, i))
    pair_tiles = pl.BlockSpec((groups // 2, 2) + tile, lambda i: (i, 0, 0, 0))
    line_tile = pl.BlockSpec((groups // 2,) + tile, lambda i: (i, 0, 0))
    line = pl.BlockSpec((groups,) + tile, lambda i: (0, 0, 0))
    single = pl.BlockSpec(tile, lambda i: (0, 0))
    pair_kept, pair_sent = pltpu.HBM((groups, 2) + tile, f32), pltpu.HBM((groups, 2) + tile, f32)
    line_kept, line_sent = pltpu.HBM((groups,) + tile, f32), pltpu.HBM((groups,) + tile, f32)
    tile_shape = pltpu.HBM(tile, f32)
    token_shape = pltpu.HBM((span, features), bf16)

    arrived = []

    def noted(array):
        arrived.append(array)
        return array

    def run(body, grid, in_specs, out_specs, out_shape, args, after=None, name=None, **sizes):
        if after is not None:
            in_specs, args = in_specs + [FREE], args + (after,)
        args = [
            arg
            if spec is SMEM or any(arg is item for item in arrived)
            else far(arg)
            for spec, arg in zip(in_specs, args)
        ]
        return call(
            functools.partial(body, length=length, **sizes), grid, in_specs, out_specs, out_shape,
            args, name=name,
        )

    def updates(left, right, where, reverse, after=None):
        return run(
            update_kernel, (2,), [SMEM, SMEM, head_cols, head_cols], [pair_tiles, pair_tiles],
            [pair_kept, pair_sent], (where, exps, left, right), after,
            reverse=reverse, name="updates",
        )

    def chip(mine, other, reverse, after=None):
        return run(
            chip_kernel, (2,), [SMEM, SMEM, pair_tiles, pair_tiles], [line_tile, line_tile],
            [line_kept, line_sent], (here, exps, mine, other), after,
            reverse=reverse, span=float(span), name="chip",
        )

    def core_state(edges, mine, other, where, reverse, after=None):
        specs = [pair_tiles] if len(edges) == 1 else [line_tile, line_tile]
        return run(
            core_state_kernel, (2,), [SMEM, SMEM, pair_tiles, pair_tiles] + specs,
            [pair_tiles, pair_tiles], [pair_kept, pair_sent],
            (where, exps, mine, other, *edges), after,
            reverse=reverse, count=len(edges), span=float(span), name="core_state",
        )

    inner_shape = pltpu.HBM((span, features), f32)
    even = here * jnp.array([1, 0, 1], jnp.int32)
    r_mine, sent = updates(query, grad, even, True)
    r_other = noted(swap(sent, "core"))
    r_pair = run(
        pair_kernel, (2,), [SMEM, SMEM, pair_tiles, pair_tiles], pair_tiles, pair_sent,
        (here, exps, r_mine, r_other), span=float(span), name="pair",
    )
    f_mine, sent = updates(key, value, here, False, r_mine)
    f_other = noted(swap(sent, "core"))
    r_parts = exchange(r_pair.reshape((2 * groups,) + tile), CHIPS)
    r_parts = noted(r_parts.reshape((groups, 2) + tile))
    f_chip, sent = chip(f_mine, f_other, False, r_pair)
    f_next = noted(swap(sent, "xl"))
    all_pairs = pl.BlockSpec((groups, 2) + tile, lambda i: (0, 0, 0, 0))
    r_edges, state_grad = run(
        scan_kernel, (1,), [SMEM, all_pairs], [all_pairs, single], [pair_sent, tile_shape],
        (decay_exp, r_parts), f_next, span=2.0 * span, name="scan",
    )
    quarter = pl.BlockSpec((4,) + tile, lambda i: (0, 0, 0))
    quarter_shape = pltpu.HBM((4,) + tile, f32)
    f_line, sent = run(
        line_kernel, (1,), [SMEM, SMEM, line, line], [quarter, quarter],
        [quarter_shape, quarter_shape], (here, exps, f_chip, f_next), r_edges,
        span=2.0 * span, name="line",
    )
    f_beside = noted(swap(sent, "zl"))
    inner_gk, inner_gv = run(
        inner_kernel, (2,), [SMEM] + 4 * [head_cols], 2 * [head_cols], 2 * [inner_shape],
        (exps, query, key, value, grad), r_edges, name="inner",
    )
    r_edges = exchange(r_edges.reshape((2 * groups,) + tile), CHIPS)
    r_edges = noted(r_edges.reshape((groups, 2) + tile))
    mine, sent = core_state([r_edges], r_mine, r_other, even, True, inner_gk)
    other = noted(swap(sent, "core"))
    grad_key, grad_value, send = run(
        key_value_kernel, (2,), [SMEM, SMEM] + 4 * [head_cols] + 2 * [pair_tiles],
        [head_cols, head_cols, pl.BlockSpec((8, 4, span, WIDTH), lambda i: (0, 0, 0, i))],
        [token_shape, token_shape, pltpu.HBM((8, 4, span, 2 * WIDTH), bf16)],
        (even, exps, key, value, inner_gk, inner_gv, mine, other), name="key_value",
    )
    cols = exchange(send.reshape(32, span, 2 * WIDTH), PLANE)
    cols = cols.reshape(32 * span, 2 * WIDTH)

    f_lines = run(
        line_pair_kernel, (1,), [SMEM, SMEM, quarter, quarter, single, FREE],
        pl.BlockSpec((5,) + tile, lambda i: (0, 0, 0)), pltpu.HBM((5,) + tile, f32),
        (here, exps, f_line, f_beside, state_in[0, 0], rows), send, span=4.0 * span,
        name="line_pair",
    )
    f_parts = lax.all_gather(f_lines, "zh")
    tokens, width = rows.shape
    block = width // 4
    partial = call(
        weight_kernel, (4,),
        [
            pl.BlockSpec((tokens, 2 * WIDTH), lambda i: (0, 0)),
            pl.BlockSpec((tokens, block), lambda i: (0, i)),
        ],
        pl.BlockSpec((8, 2, block // 8, WIDTH), lambda i: (0, i, 0, 0)),
        pltpu.HBM((8, 8, block // 8, WIDTH), bf16), (cols, far(rows)), scratch=[pltpu.VMEM((2 * WIDTH, tokens), bf16)], name="weight", vmem=40,
    )
    f_edge, f_sent = run(
        edge_kernel, (1,),
        [SMEM, SMEM, pl.BlockSpec((4, 5) + tile, lambda i: (0, 0, 0, 0)), quarter, quarter],
        [quarter, quarter], [quarter_shape, quarter_shape],
        (here, exps, f_parts, f_line, f_beside), partial, span=4.0 * span, name="edge",
    )
    partial, f_sent = lax.optimization_barrier((partial, f_sent))
    f_side = noted(swap(f_sent, "zl"))
    f_edge, sent = run(
        chip_state_kernel, (1,), [SMEM, SMEM, quarter, quarter, line, line], [line, line],
        [line_kept, line_sent], (here, exps, f_edge, f_side, f_chip, f_next),
        span=2.0 * span, name="chip_state",
    )
    f_far = noted(swap(sent, "xl"))
    mine, sent = core_state([f_edge, f_far], f_mine, f_other, here, False)
    other = noted(swap(sent, "core"))
    grad_query = run(
        query_kernel, (2,), [SMEM, SMEM] + 3 * [head_cols] + 2 * [pair_tiles], head_cols,
        token_shape, (here, exps, key, value, grad, mine, other), name="query",
    )
    share = block // 8
    pieces = exchange(partial.reshape(64, share, WIDTH), OWNERS).reshape(8, 8, share, WIDTH)
    weight_grads = call(
        total_kernel, (2,), [pl.BlockSpec((4, 8, share, WIDTH), lambda i: (i, 0, 0, 0))],
        pl.BlockSpec((1, 1, share, 4 * WIDTH), lambda i: (i, 0, 0, 0)),
        pltpu.HBM((2, 1, share, 4 * WIDTH), f32), (pieces,), name="total",
    )
    return (
        grad_query[None], grad_key[None], grad_value[None], weight_grads, state_grad[None, None]
    )


def solution(mesh):
    fine = Mesh(mesh.devices.reshape(4, 2, 4, 2, 2, 2), ("y", "xh", "zh", "zl", "xl", "core"))
    dp, seq = ("y", "xh"), CHAIN
    tokens = P(dp, seq, None)
    in_specs = (tokens, tokens, tokens, tokens, tokens, P(seq), P(dp, seq, None, None))
    out_specs = (tokens, tokens, tokens, P(None, seq, dp, None), P(dp, seq, None, None))
    return jax.shard_map(
        per_device, mesh=fine, in_specs=in_specs, out_specs=out_specs, check_vma=False
    )
```

```python
import functools

import jax
import jax.numpy as jnp
from jax import lax
from jax.experimental import pallas as pl
from jax.experimental.pallas import tpu as pltpu
from jax.sharding import Mesh
from jax.sharding import PartitionSpec as P

WIDTH = 128
f32 = jnp.float32
bf16 = jnp.bfloat16
PLANE = ("y", "xh", "xl", "core")
QUAD = ("xl", "core")
LINE = ("zh", "zl")
CHIPS = ("zh", "zl", "xl")
CHAIN = ("zh", "zl", "xl", "core")
OWNERS = ("y", "xh", "zh", "zl")


def log_rate(exponent, length):
    return -(jnp.left_shift(1, exponent).astype(f32)) * (1.0 / length)


def power_of(rate, steps):
    return jnp.exp(jnp.full((1, WIDTH), rate * steps, f32))


def halves(wide):
    high = wide.astype(bf16)
    return high, (wide - high.astype(f32)).astype(bf16)


def dot(left, right, dims):
    return lax.dot_general(left, right, (dims, ((), ())), preferred_element_type=f32)


def groups_of(ref):
    count = ref.shape[0]
    return [(item, pl.program_id(0) * count + item) for item in range(count)]


def update_kernel(here_ref, exp_ref, left_ref, right_ref, *refs, reverse, length):
    keep_ref, send_ref = refs[-2:]
    span = left_ref.shape[0]
    rows = lax.broadcasted_iota(jnp.int32, (span, WIDTH), 0).astype(f32)
    steps = rows if reverse else (span - 1.0) - rows
    for item, group in groups_of(keep_ref):
        for core, out_ref in enumerate((keep_ref, send_ref)):
            for chip in range(2):
                slot = 2 * jnp.bitwise_xor(here_ref[1], chip) + jnp.bitwise_xor(here_ref[2], core)
                rate = log_rate(exp_ref[4 * group + slot], length)
                start = pl.multiple_of((4 * item + slot) * WIDTH, WIDTH)
                lanes = pl.ds(start, WIDTH)
                high, low = halves(left_ref[:, lanes].astype(f32) * jnp.exp(rate * steps))
                right = right_ref[:, lanes]
                out_ref[item, chip] = dot(
                    jnp.concatenate((high, low), 0), jnp.concatenate((right, right), 0),
                    ((0,), (0,)),
                )


def weighed(mine, other, position, reverse, rate, span):
    position = position.astype(f32)
    later = position if reverse else 1.0 - position
    return power_of(rate, span * later) * mine + power_of(rate, span * (1.0 - later)) * other


def chip_kernel(here_ref, exp_ref, mine_ref, other_ref, *refs, reverse, length, span):
    keep_ref, send_ref = refs[-2:]
    for item, group in groups_of(keep_ref):
        for chip, out_ref in enumerate((keep_ref, send_ref)):
            head = 4 * group + 2 * jnp.bitwise_xor(here_ref[1], chip) + here_ref[2]
            out_ref[item] = weighed(
                mine_ref[item, chip], other_ref[item, chip], here_ref[2], reverse,
                log_rate(exp_ref[head], length), span,
            )


def pair_kernel(here_ref, exp_ref, mine_ref, other_ref, out_ref, *, length, span):
    for item, group in groups_of(out_ref):
        for chip in range(2):
            rate = log_rate(exp_ref[4 * group + 2 * chip + here_ref[2]], length)
            out_ref[item, chip] = weighed(
                mine_ref[item, chip], other_ref[item, chip], here_ref[2], True, rate, span
            )


def scan_kernel(own_ref, parts_ref, after_ref, out_ref, grad_ref, *, length, span):
    rate = log_rate(own_ref[0], length)
    decay = power_of(rate, span)
    state = jnp.zeros(grad_ref.shape, f32)
    for group in reversed(range(parts_ref.shape[0])):
        for chip in (1, 0):
            out_ref[group, chip] = state
            state = decay * state + parts_ref[group, chip]
    grad_ref[...] = power_of(rate, 1.0) * state


def group_rate(here_ref, exp_ref, group, length):
    return log_rate(exp_ref[4 * group + 2 * here_ref[1] + here_ref[2]], length)


def line_kernel(
    here_ref, exp_ref, mine_ref, other_ref, first_ref, after_ref, out_ref, *, length, span
):
    count = mine_ref.shape[0]
    for group in range(count):
        rate = group_rate(here_ref, exp_ref, group, length)
        out_ref[group] = weighed(
            mine_ref[group], other_ref[group], here_ref[1], False, rate, span
        )
    out_ref[count] = first_ref[...]


def line_pair_kernel(here_ref, exp_ref, mine_ref, other_ref, *refs, length, span):
    out_ref = refs[-1]
    count = mine_ref.shape[0] - 1
    for group in range(count):
        rate = group_rate(here_ref, exp_ref, group, length)
        out_ref[group] = weighed(
            mine_ref[group], other_ref[group], here_ref[0] % 2, False, rate, span
        )
    out_ref[count] = mine_ref[count]
    out_ref[count + 1] = other_ref[count]


def edge_kernel(
    here_ref, exp_ref, parts_ref, beside_ref, mine_ref, other_ref, after_ref, keep_ref, send_ref,
    *, length, span
):
    count = mine_ref.shape[0]
    for group in range(count):
        rate = group_rate(here_ref, exp_ref, group, length)
        decay = power_of(rate, 4.0 * span)
        state = jnp.where(
            here_ref[0] % 2 == group % 2,
            parts_ref[group // 2, count],
            parts_ref[group // 2, count + 1],
        )
        for before in range(parts_ref.shape[0] - 1):
            update = decay * state + parts_ref[before, group]
            state = jnp.where(here_ref[0] // 2 > before, update, state)
        update = power_of(rate, 2.0 * span) * state + beside_ref[group]
        state = jnp.where(here_ref[0] % 2 == 1, update, state)
        past = power_of(rate, span) * state
        behind = here_ref[1] == 1
        keep_ref[group] = jnp.where(behind, past + other_ref[group], state)
        send_ref[group] = jnp.where(behind, state, past + mine_ref[group])


def core_state_kernel(here_ref, exp_ref, mine_ref, other_ref, *refs, reverse, count, length, span):
    edge_refs, (keep_ref, send_ref) = refs[:count], refs[-2:]
    behind = here_ref[2] == (0 if reverse else 1)
    for item, group in groups_of(keep_ref):
        for chip in range(2):
            head = 4 * group + 2 * jnp.bitwise_xor(here_ref[1], chip) + here_ref[2]
            rate = log_rate(exp_ref[head], length)
            edge = edge_refs[0][item, chip] if count == 1 else edge_refs[chip][item]
            past = power_of(rate, span) * edge
            keep_ref[item, chip] = jnp.where(behind, past + other_ref[item, chip], edge)
            send_ref[item, chip] = jnp.where(behind, edge, past + mine_ref[item, chip])


def picked(here_ref, mine_ref, other_ref, item, slot):
    chip = jnp.bitwise_xor(here_ref[1], slot // 2)
    return jnp.where(here_ref[2] == slot % 2, mine_ref[item, chip], other_ref[item, chip])


def heads_of(ref):
    count = ref.shape[1] // (4 * WIDTH)
    first = pl.program_id(0) * count
    return [
        (item, slot, 4 * (first + item) + slot, pl.ds((4 * item + slot) * WIDTH, WIDTH))
        for item in range(count)
        for slot in range(4)
    ]


def inner_kernel(
    exp_ref, query_ref, key_ref, value_ref, grad_ref, after_ref, gk_ref, gv_ref, *, length
):
    span = query_ref.shape[0]
    source = lax.broadcasted_iota(jnp.int32, (span, span), 0)
    target = lax.broadcasted_iota(jnp.int32, (span, span), 1)
    gap = (target - source).astype(f32)
    for item, slot, head, lanes in heads_of(query_ref):
        rate = log_rate(exp_ref[head], length)
        query, key = query_ref[:, lanes], key_ref[:, lanes]
        value, grad = value_ref[:, lanes], grad_ref[:, lanes]
        mask = jnp.where(gap >= 0.0, jnp.exp(rate * jnp.maximum(gap, 0.0)), 0.0)
        grad_scores = jnp.concatenate(halves(dot(value, grad, ((1,), (1,))) * mask), 1)
        key_scores = jnp.concatenate(halves(dot(key, query, ((1,), (1,))) * mask), 1)
        gk_ref[:, lanes] = dot(grad_scores, jnp.concatenate((query, query), 0), ((1,), (0,)))
        gv_ref[:, lanes] = dot(key_scores, jnp.concatenate((grad, grad), 0), ((1,), (0,)))


def key_value_kernel(
    here_ref, exp_ref, key_ref, value_ref, inner_gk_ref, inner_gv_ref, mine_ref, other_ref,
    after_ref, gk_ref, gv_ref, send_ref, *, length
):
    span = key_ref.shape[0]
    left = span - lax.broadcasted_iota(jnp.int32, (span, WIDTH), 0).astype(f32)
    for item, slot, head, lanes in heads_of(key_ref):
        rate = log_rate(exp_ref[head], length)
        key, value = key_ref[:, lanes], value_ref[:, lanes]
        tail = jnp.exp(rate * left)
        high, low = halves(picked(here_ref, mine_ref, other_ref, item, slot))
        gk = inner_gk_ref[:, lanes] + tail * dot(
            jnp.concatenate((value, value), 1), jnp.concatenate((high, low), 1), ((1,), (1,))
        )
        gv = inner_gv_ref[:, lanes] + tail * dot(
            jnp.concatenate((key, key), 1), jnp.concatenate((high, low), 0), ((1,), (0,))
        )
        gk_ref[:, lanes] = gk.astype(bf16)
        gv_ref[:, lanes] = gv.astype(bf16)
        send_ref[slot, item] = gk.astype(bf16)
        send_ref[4 + slot, item] = gv.astype(bf16)


def query_kernel(
    here_ref, exp_ref, key_ref, value_ref, grad_ref, mine_ref, other_ref, gq_ref, *, length
):
    span = key_ref.shape[0]
    target = lax.broadcasted_iota(jnp.int32, (span, span), 0)
    source = lax.broadcasted_iota(jnp.int32, (span, span), 1)
    gap = (target - source).astype(f32)
    done = 1.0 + lax.broadcasted_iota(jnp.int32, (span, WIDTH), 0).astype(f32)
    for item, slot, head, lanes in heads_of(key_ref):
        rate = log_rate(exp_ref[head], length)
        key, value, grad = key_ref[:, lanes], value_ref[:, lanes], grad_ref[:, lanes]
        mask = jnp.where(gap >= 0.0, jnp.exp(rate * jnp.maximum(gap, 0.0)), 0.0)
        scores = jnp.concatenate(halves(dot(grad, value, ((1,), (1,))) * mask), 1)
        high, low = halves(picked(here_ref, mine_ref, other_ref, item, slot))
        gq = jnp.exp(rate * done) * dot(
            jnp.concatenate((grad, grad), 1), jnp.concatenate((high, low), 1), ((1,), (1,))
        )
        gq = gq + dot(scores, jnp.concatenate((key, key), 0), ((1,), (0,)))
        gq_ref[:, lanes] = gq.astype(bf16)


def weight_kernel(cols_ref, rows_ref, out_ref, turned):
    @pl.when(pl.program_id(0) == 0)
    def _():
        turned[...] = cols_ref[...].T

    product = dot(turned[...], rows_ref[...], ((1,), (0,))).T.astype(bf16)
    count = out_ref.shape[2]
    for item in range(out_ref.shape[0]):
        rows = product[item * count : (item + 1) * count]
        out_ref[item, 0] = rows[:, :WIDTH]
        out_ref[item, 1] = rows[:, WIDTH:]


def total_kernel(parts_ref, out_ref):
    for owner in range(parts_ref.shape[0]):
        total = parts_ref[owner, 0].astype(f32)
        for item in range(1, parts_ref.shape[1]):
            total = total + parts_ref[owner, item].astype(f32)
        out_ref[0, 0, :, owner * WIDTH : (owner + 1) * WIDTH] = total


SMEM = pl.BlockSpec(memory_space=pltpu.SMEM)
FREE = pl.BlockSpec(memory_space=pl.ANY)


def exchange(array, axes):
    return lax.all_to_all(array, axes, split_axis=0, concat_axis=0, tiled=True)


def swap(array, axis):
    return lax.ppermute(array, axis, [(0, 1), (1, 0)])


def far(array):
    return pltpu.with_memory_space_constraint(array, pltpu.HBM)


def call(kernel, grid, in_specs, out_specs, out_shape, args, scratch=(), name=None, vmem=24):
    return pl.pallas_call(
        kernel,
        grid=grid,
        in_specs=in_specs,
        out_specs=out_specs,
        out_shape=out_shape,
        scratch_shapes=scratch,
        name=name,
        compiler_params=pltpu.CompilerParams(vmem_limit_bytes=vmem * 1024 * 1024),
    )(*args)


def per_device(inputs_x, queries, keys, values, grad_out, decay_exp, state_in):
    span = queries.shape[1]
    features = queries.shape[2]
    groups = features // (4 * WIDTH)
    length = span * lax.axis_size(CHAIN)
    tile = (WIDTH, WIDTH)
    query, key, value, grad = queries[0], keys[0], values[0], grad_out[0]
    exps = lax.all_gather(decay_exp, CHAIN, axis=0, tiled=True)
    here = jnp.stack([lax.axis_index(axis) for axis in (LINE, "xl", "core")]).astype(jnp.int32)
    rows = lax.all_gather(inputs_x[0], PLANE, axis=0, tiled=True)

    head_cols = pl.BlockSpec((span, features // 2), lambda i: (0, i))
    pair_tiles = pl.BlockSpec((groups // 2, 2) + tile, lambda i: (i, 0, 0, 0))
    line_tile = pl.BlockSpec((groups // 2,) + tile, lambda i: (i, 0, 0))
    line = pl.BlockSpec((groups,) + tile, lambda i: (0, 0, 0))
    single = pl.BlockSpec(tile, lambda i: (0, 0))
    pair_kept, pair_sent = pltpu.HBM((groups, 2) + tile, f32), pltpu.HBM((groups, 2) + tile, f32)
    line_kept, line_sent = pltpu.HBM((groups,) + tile, f32), pltpu.HBM((groups,) + tile, f32)
    tile_shape = pltpu.HBM(tile, f32)
    token_shape = pltpu.HBM((span, features), bf16)

    arrived = []

    def noted(array):
        arrived.append(array)
        return array

    def run(body, grid, in_specs, out_specs, out_shape, args, after=None, name=None, **sizes):
        if after is not None:
            in_specs, args = in_specs + [FREE], args + (after,)
        args = [
            arg
            if spec is SMEM or any(arg is item for item in arrived)
            else far(arg)
            for spec, arg in zip(in_specs, args)
        ]
        return call(
            functools.partial(body, length=length, **sizes), grid, in_specs, out_specs, out_shape,
            args, name=name,
        )

    def updates(left, right, where, reverse, after=None):
        return run(
            update_kernel, (2,), [SMEM, SMEM, head_cols, head_cols], [pair_tiles, pair_tiles],
            [pair_kept, pair_sent], (where, exps, left, right), after,
            reverse=reverse, name="updates",
        )

    def chip(mine, other, reverse, after=None):
        return run(
            chip_kernel, (2,), [SMEM, SMEM, pair_tiles, pair_tiles], [line_tile, line_tile],
            [line_kept, line_sent], (here, exps, mine, other), after,
            reverse=reverse, span=float(span), name="chip",
        )

    def core_state(edges, mine, other, where, reverse, after=None):
        specs = [pair_tiles] if len(edges) == 1 else [line_tile, line_tile]
        return run(
            core_state_kernel, (2,), [SMEM, SMEM, pair_tiles, pair_tiles] + specs,
            [pair_tiles, pair_tiles], [pair_kept, pair_sent],
            (where, exps, mine, other, *edges), after,
            reverse=reverse, count=len(edges), span=float(span), name="core_state",
        )

    inner_shape = pltpu.HBM((span, features), f32)
    even = here * jnp.array([1, 0, 1], jnp.int32)
    r_mine, sent = updates(query, grad, even, True)
    r_other = noted(swap(sent, "core"))
    r_pair = run(
        pair_kernel, (2,), [SMEM, SMEM, pair_tiles, pair_tiles], pair_tiles, pair_sent,
        (here, exps, r_mine, r_other), span=float(span), name="pair",
    )
    f_mine, sent = updates(key, value, here, False, r_mine)
    f_other = noted(swap(sent, "core"))
    r_parts = exchange(r_pair.reshape((2 * groups,) + tile), CHIPS)
    r_parts = noted(r_parts.reshape((groups, 2) + tile))
    f_chip, sent = chip(f_mine, f_other, False, r_pair)
    f_next = noted(swap(sent, "xl"))
    all_pairs = pl.BlockSpec((groups, 2) + tile, lambda i: (0, 0, 0, 0))
    r_edges, state_grad = run(
        scan_kernel, (1,), [SMEM, all_pairs], [all_pairs, single], [pair_sent, tile_shape],
        (decay_exp, r_parts), f_chip, span=2.0 * span, name="scan",
    )
    nine = pl.BlockSpec((groups + 1,) + tile, lambda i: (0, 0, 0))
    f_line = run(
        line_kernel, (1,), [SMEM, SMEM, line, line, single], nine,
        pltpu.HBM((groups + 1,) + tile, f32), (here, exps, f_chip, f_next, state_in[0, 0]), r_edges,
        span=2.0 * span, name="line",
    )
    f_beside = noted(swap(f_line, "zl"))
    inner_gk, inner_gv = run(
        inner_kernel, (2,), [SMEM] + 4 * [head_cols], 2 * [head_cols], 2 * [inner_shape],
        (exps, query, key, value, grad), r_edges, name="inner",
    )
    r_edges = exchange(r_edges.reshape((2 * groups,) + tile), CHIPS)
    r_edges = noted(r_edges.reshape((groups, 2) + tile))
    mine, sent = core_state([r_edges], r_mine, r_other, even, True, inner_gk)
    other = noted(swap(sent, "core"))
    grad_key, grad_value, send = run(
        key_value_kernel, (2,), [SMEM, SMEM] + 4 * [head_cols] + 2 * [pair_tiles],
        [head_cols, head_cols, pl.BlockSpec((8, 4, span, WIDTH), lambda i: (0, 0, 0, i))],
        [token_shape, token_shape, pltpu.HBM((8, 4, span, 2 * WIDTH), bf16)],
        (even, exps, key, value, inner_gk, inner_gv, mine, other), f_line, name="key_value",
    )
    cols = exchange(send.reshape(32, span, 2 * WIDTH), PLANE)
    cols = cols.reshape(32 * span, 2 * WIDTH)

    f_lines = run(
        line_pair_kernel, (1,), [SMEM, SMEM, nine, nine],
        pl.BlockSpec((groups + 2,) + tile, lambda i: (0, 0, 0)),
        pltpu.HBM((groups + 2,) + tile, f32), (here, exps, f_line, f_beside), send,
        span=4.0 * span, name="line_pair",
    )
    f_parts = lax.all_gather(f_lines, "zh")
    tokens, width = rows.shape
    block = width // 4
    partial = call(
        weight_kernel, (4,),
        [
            pl.BlockSpec((tokens, 2 * WIDTH), lambda i: (0, 0)),
            pl.BlockSpec((tokens, block), lambda i: (0, i)),
        ],
        pl.BlockSpec((8, 2, block // 8, WIDTH), lambda i: (0, i, 0, 0)),
        pltpu.HBM((8, 8, block // 8, WIDTH), bf16), (cols, far(rows)), scratch=[pltpu.VMEM((2 * WIDTH, tokens), bf16)], name="weight", vmem=40,
    )
    f_edge, sent = run(
        edge_kernel, (1,),
        [
            SMEM, SMEM, pl.BlockSpec((4, groups + 2) + tile, lambda i: (0, 0, 0, 0)), nine, line,
            line,
        ],
        [line, line], [line_kept, line_sent], (here, exps, f_parts, f_beside, f_chip, f_next),
        partial, span=2.0 * span, name="edge",
    )
    f_far = noted(swap(sent, "xl"))
    mine, sent = core_state([f_edge, f_far], f_mine, f_other, here, False)
    other = noted(swap(sent, "core"))
    grad_query = run(
        query_kernel, (2,), [SMEM, SMEM] + 3 * [head_cols] + 2 * [pair_tiles], head_cols,
        token_shape, (here, exps, key, value, grad, mine, other), name="query",
    )
    share = block // 8
    pieces = exchange(partial.reshape(64, share, WIDTH), OWNERS).reshape(8, 8, share, WIDTH)
    weight_grads = call(
        total_kernel, (2,), [pl.BlockSpec((4, 8, share, WIDTH), lambda i: (i, 0, 0, 0))],
        pl.BlockSpec((1, 1, share, 4 * WIDTH), lambda i: (i, 0, 0, 0)),
        pltpu.HBM((2, 1, share, 4 * WIDTH), f32), (pieces,), name="total",
    )
    return (
        grad_query[None], grad_key[None], grad_value[None], weight_grads, state_grad[None, None]
    )


def solution(mesh):
    fine = Mesh(mesh.devices.reshape(4, 2, 4, 2, 2, 2), ("y", "xh", "zh", "zl", "xl", "core"))
    dp, seq = ("y", "xh"), CHAIN
    tokens = P(dp, seq, None)
    in_specs = (tokens, tokens, tokens, tokens, tokens, P(seq), P(dp, seq, None, None))
    out_specs = (tokens, tokens, tokens, P(None, seq, dp, None), P(dp, seq, None, None))
    return jax.shard_map(
        per_device, mesh=fine, in_specs=in_specs, out_specs=out_specs, check_vma=False
    )
```

```python
import functools

import jax
import jax.numpy as jnp
from jax import lax
from jax.experimental import pallas as pl
from jax.experimental.pallas import tpu as pltpu
from jax.sharding import Mesh
from jax.sharding import PartitionSpec as P

WIDTH = 128
f32 = jnp.float32
bf16 = jnp.bfloat16
PLANE = ("y", "xh", "xl", "core")
QUAD = ("xl", "core")
LINE = ("zh", "zl")
CHIPS = ("zh", "zl", "xl")
CHAIN = ("zh", "zl", "xl", "core")
OWNERS = ("y", "xh", "zh", "zl")


def log_rate(exponent, length):
    return -(jnp.left_shift(1, exponent).astype(f32)) * (1.0 / length)


def power_of(rate, steps):
    return jnp.exp(jnp.full((1, WIDTH), rate * steps, f32))


def halves(wide):
    high = wide.astype(bf16)
    return high, (wide - high.astype(f32)).astype(bf16)


def dot(left, right, dims):
    return lax.dot_general(left, right, (dims, ((), ())), preferred_element_type=f32)


def groups_of(ref):
    count = ref.shape[0]
    return [(item, pl.program_id(0) * count + item) for item in range(count)]


def update_kernel(here_ref, exp_ref, left_ref, right_ref, *refs, reverse, length):
    keep_ref, send_ref = refs[-2:]
    span = left_ref.shape[0]
    rows = lax.broadcasted_iota(jnp.int32, (span, WIDTH), 0).astype(f32)
    steps = rows if reverse else (span - 1.0) - rows
    for item, group in groups_of(keep_ref):
        for core, out_ref in enumerate((keep_ref, send_ref)):
            for chip in range(2):
                slot = 2 * jnp.bitwise_xor(here_ref[1], chip) + jnp.bitwise_xor(here_ref[2], core)
                rate = log_rate(exp_ref[4 * group + slot], length)
                start = pl.multiple_of((4 * item + slot) * WIDTH, WIDTH)
                lanes = pl.ds(start, WIDTH)
                high, low = halves(left_ref[:, lanes].astype(f32) * jnp.exp(rate * steps))
                right = right_ref[:, lanes]
                out_ref[item, chip] = dot(
                    jnp.concatenate((high, low), 0), jnp.concatenate((right, right), 0),
                    ((0,), (0,)),
                )


def weighed(mine, other, position, reverse, rate, span):
    position = position.astype(f32)
    later = position if reverse else 1.0 - position
    return power_of(rate, span * later) * mine + power_of(rate, span * (1.0 - later)) * other


def chip_kernel(here_ref, exp_ref, mine_ref, other_ref, *refs, reverse, length, span):
    keep_ref, send_ref = refs[-2:]
    for item, group in groups_of(keep_ref):
        for chip, out_ref in enumerate((keep_ref, send_ref)):
            head = 4 * group + 2 * jnp.bitwise_xor(here_ref[1], chip) + here_ref[2]
            out_ref[item] = weighed(
                mine_ref[item, chip], other_ref[item, chip], here_ref[2], reverse,
                log_rate(exp_ref[head], length), span,
            )


def pair_kernel(here_ref, exp_ref, mine_ref, other_ref, out_ref, *, length, span):
    for item, group in groups_of(out_ref):
        for chip in range(2):
            rate = log_rate(exp_ref[4 * group + 2 * chip + here_ref[2]], length)
            out_ref[item, chip] = weighed(
                mine_ref[item, chip], other_ref[item, chip], here_ref[2], True, rate, span
            )


def scan_kernel(own_ref, parts_ref, after_ref, out_ref, grad_ref, *, length, span):
    rate = log_rate(own_ref[0], length)
    decay = power_of(rate, span)
    state = jnp.zeros(grad_ref.shape, f32)
    for group in reversed(range(parts_ref.shape[0])):
        for chip in (1, 0):
            out_ref[group, chip] = state
            state = decay * state + parts_ref[group, chip]
    grad_ref[...] = power_of(rate, 1.0) * state


def line_kernel(
    here_ref, exp_ref, mine_ref, other_ref, after_ref, keep_ref, send_ref, *, length, span
):
    parity = here_ref[0] % 2
    for half, out_ref in enumerate((keep_ref, send_ref)):
        for item in range(out_ref.shape[0]):
            group = 2 * item + jnp.bitwise_xor(parity, half)
            rate = log_rate(exp_ref[4 * group + 2 * here_ref[1] + here_ref[2]], length)
            out_ref[item] = weighed(
                mine_ref[group], other_ref[group], here_ref[1], False, rate, span
            )


def own_rate(here_ref, exp_ref, item, length):
    group = 2 * item + here_ref[0] % 2
    return log_rate(exp_ref[4 * group + 2 * here_ref[1] + here_ref[2]], length)


def line_pair_kernel(
    here_ref, exp_ref, mine_ref, other_ref, first_ref, *refs, length, span
):
    out_ref = refs[-1]
    count = mine_ref.shape[0]
    for item in range(count):
        rate = own_rate(here_ref, exp_ref, item, length)
        out_ref[item] = weighed(
            mine_ref[item], other_ref[item], here_ref[0] % 2, False, rate, span
        )
    out_ref[count] = first_ref[...]


def edge_kernel(
    here_ref, exp_ref, parts_ref, mine_ref, other_ref, after_ref, keep_ref, send_ref,
    *, length, span
):
    count = mine_ref.shape[0]
    behind = here_ref[0] % 2 == 1
    for item in range(count):
        rate = own_rate(here_ref, exp_ref, item, length)
        decay = power_of(rate, 2.0 * span)
        state = parts_ref[item, count]
        for before in range(count - 1):
            update = decay * state + parts_ref[before, item]
            state = jnp.where(here_ref[0] // 2 > before, update, state)
        past = power_of(rate, span) * state
        keep_ref[item] = jnp.where(behind, past + other_ref[item], state)
        send_ref[item] = jnp.where(behind, state, past + mine_ref[item])


def chip_state_kernel(
    here_ref, exp_ref, mine_edge_ref, other_edge_ref, mine_ref, other_ref, keep_ref, send_ref,
    *, length, span
):
    behind = here_ref[1] == 1
    for group in range(keep_ref.shape[0]):
        rate = log_rate(exp_ref[4 * group + 2 * here_ref[1] + here_ref[2]], length)
        edge = jnp.where(
            here_ref[0] % 2 == group % 2, mine_edge_ref[group // 2], other_edge_ref[group // 2]
        )
        past = power_of(rate, span) * edge
        keep_ref[group] = jnp.where(behind, past + other_ref[group], edge)
        send_ref[group] = jnp.where(behind, edge, past + mine_ref[group])


def core_state_kernel(here_ref, exp_ref, mine_ref, other_ref, *refs, reverse, count, length, span):
    edge_refs, (keep_ref, send_ref) = refs[:count], refs[-2:]
    behind = here_ref[2] == (0 if reverse else 1)
    for item, group in groups_of(keep_ref):
        for chip in range(2):
            head = 4 * group + 2 * jnp.bitwise_xor(here_ref[1], chip) + here_ref[2]
            rate = log_rate(exp_ref[head], length)
            edge = edge_refs[0][item, chip] if count == 1 else edge_refs[chip][item]
            past = power_of(rate, span) * edge
            keep_ref[item, chip] = jnp.where(behind, past + other_ref[item, chip], edge)
            send_ref[item, chip] = jnp.where(behind, edge, past + mine_ref[item, chip])


def picked(here_ref, mine_ref, other_ref, item, slot):
    chip = jnp.bitwise_xor(here_ref[1], slot // 2)
    return jnp.where(here_ref[2] == slot % 2, mine_ref[item, chip], other_ref[item, chip])


def heads_of(ref):
    count = ref.shape[1] // (4 * WIDTH)
    first = pl.program_id(0) * count
    return [
        (item, slot, 4 * (first + item) + slot, pl.ds((4 * item + slot) * WIDTH, WIDTH))
        for item in range(count)
        for slot in range(4)
    ]


def inner_kernel(
    exp_ref, query_ref, key_ref, value_ref, grad_ref, after_ref, gk_ref, gv_ref, *, length
):
    span = query_ref.shape[0]
    source = lax.broadcasted_iota(jnp.int32, (span, span), 0)
    target = lax.broadcasted_iota(jnp.int32, (span, span), 1)
    gap = (target - source).astype(f32)
    for item, slot, head, lanes in heads_of(query_ref):
        rate = log_rate(exp_ref[head], length)
        query, key = query_ref[:, lanes], key_ref[:, lanes]
        value, grad = value_ref[:, lanes], grad_ref[:, lanes]
        mask = jnp.where(gap >= 0.0, jnp.exp(rate * jnp.maximum(gap, 0.0)), 0.0)
        grad_scores = jnp.concatenate(halves(dot(value, grad, ((1,), (1,))) * mask), 1)
        key_scores = jnp.concatenate(halves(dot(key, query, ((1,), (1,))) * mask), 1)
        gk_ref[:, lanes] = dot(grad_scores, jnp.concatenate((query, query), 0), ((1,), (0,)))
        gv_ref[:, lanes] = dot(key_scores, jnp.concatenate((grad, grad), 0), ((1,), (0,)))


def key_value_kernel(
    here_ref, exp_ref, key_ref, value_ref, inner_gk_ref, inner_gv_ref, mine_ref, other_ref,
    after_ref, gk_ref, gv_ref, send_ref, *, length
):
    span = key_ref.shape[0]
    left = span - lax.broadcasted_iota(jnp.int32, (span, WIDTH), 0).astype(f32)
    for item, slot, head, lanes in heads_of(key_ref):
        rate = log_rate(exp_ref[head], length)
        key, value = key_ref[:, lanes], value_ref[:, lanes]
        tail = jnp.exp(rate * left)
        high, low = halves(picked(here_ref, mine_ref, other_ref, item, slot))
        gk = inner_gk_ref[:, lanes] + tail * dot(
            jnp.concatenate((value, value), 1), jnp.concatenate((high, low), 1), ((1,), (1,))
        )
        gv = inner_gv_ref[:, lanes] + tail * dot(
            jnp.concatenate((key, key), 1), jnp.concatenate((high, low), 0), ((1,), (0,))
        )
        gk_ref[:, lanes] = gk.astype(bf16)
        gv_ref[:, lanes] = gv.astype(bf16)
        send_ref[slot, item] = gk.astype(bf16)
        send_ref[4 + slot, item] = gv.astype(bf16)


def query_kernel(
    here_ref, exp_ref, key_ref, value_ref, grad_ref, mine_ref, other_ref, gq_ref, *, length
):
    span = key_ref.shape[0]
    target = lax.broadcasted_iota(jnp.int32, (span, span), 0)
    source = lax.broadcasted_iota(jnp.int32, (span, span), 1)
    gap = (target - source).astype(f32)
    done = 1.0 + lax.broadcasted_iota(jnp.int32, (span, WIDTH), 0).astype(f32)
    for item, slot, head, lanes in heads_of(key_ref):
        rate = log_rate(exp_ref[head], length)
        key, value, grad = key_ref[:, lanes], value_ref[:, lanes], grad_ref[:, lanes]
        mask = jnp.where(gap >= 0.0, jnp.exp(rate * jnp.maximum(gap, 0.0)), 0.0)
        scores = jnp.concatenate(halves(dot(grad, value, ((1,), (1,))) * mask), 1)
        high, low = halves(picked(here_ref, mine_ref, other_ref, item, slot))
        gq = jnp.exp(rate * done) * dot(
            jnp.concatenate((grad, grad), 1), jnp.concatenate((high, low), 1), ((1,), (1,))
        )
        gq = gq + dot(scores, jnp.concatenate((key, key), 0), ((1,), (0,)))
        gq_ref[:, lanes] = gq.astype(bf16)


def weight_kernel(cols_ref, rows_ref, out_ref, turned):
    @pl.when(pl.program_id(0) == 0)
    def _():
        turned[...] = cols_ref[...].T

    product = dot(turned[...], rows_ref[...], ((1,), (0,))).T.astype(bf16)
    count = out_ref.shape[2]
    for item in range(out_ref.shape[0]):
        rows = product[item * count : (item + 1) * count]
        out_ref[item, 0] = rows[:, :WIDTH]
        out_ref[item, 1] = rows[:, WIDTH:]


def total_kernel(parts_ref, out_ref):
    for owner in range(parts_ref.shape[0]):
        total = parts_ref[owner, 0].astype(f32)
        for item in range(1, parts_ref.shape[1]):
            total = total + parts_ref[owner, item].astype(f32)
        out_ref[0, 0, :, owner * WIDTH : (owner + 1) * WIDTH] = total


SMEM = pl.BlockSpec(memory_space=pltpu.SMEM)
FREE = pl.BlockSpec(memory_space=pl.ANY)


def exchange(array, axes):
    return lax.all_to_all(array, axes, split_axis=0, concat_axis=0, tiled=True)


def swap(array, axis):
    return lax.ppermute(array, axis, [(0, 1), (1, 0)])


def far(array):
    return pltpu.with_memory_space_constraint(array, pltpu.HBM)


def call(kernel, grid, in_specs, out_specs, out_shape, args, scratch=(), name=None, vmem=24):
    return pl.pallas_call(
        kernel,
        grid=grid,
        in_specs=in_specs,
        out_specs=out_specs,
        out_shape=out_shape,
        scratch_shapes=scratch,
        name=name,
        compiler_params=pltpu.CompilerParams(vmem_limit_bytes=vmem * 1024 * 1024),
    )(*args)


def per_device(inputs_x, queries, keys, values, grad_out, decay_exp, state_in):
    span = queries.shape[1]
    features = queries.shape[2]
    groups = features // (4 * WIDTH)
    length = span * lax.axis_size(CHAIN)
    tile = (WIDTH, WIDTH)
    query, key, value, grad = queries[0], keys[0], values[0], grad_out[0]
    exps = lax.all_gather(decay_exp, CHAIN, axis=0, tiled=True)
    here = jnp.stack([lax.axis_index(axis) for axis in (LINE, "xl", "core")]).astype(jnp.int32)
    rows = lax.all_gather(inputs_x[0], PLANE, axis=0, tiled=True)

    head_cols = pl.BlockSpec((span, features // 2), lambda i: (0, i))
    pair_tiles = pl.BlockSpec((groups // 2, 2) + tile, lambda i: (i, 0, 0, 0))
    line_tile = pl.BlockSpec((groups // 2,) + tile, lambda i: (i, 0, 0))
    line = pl.BlockSpec((groups,) + tile, lambda i: (0, 0, 0))
    single = pl.BlockSpec(tile, lambda i: (0, 0))
    pair_kept, pair_sent = pltpu.HBM((groups, 2) + tile, f32), pltpu.HBM((groups, 2) + tile, f32)
    line_kept, line_sent = pltpu.HBM((groups,) + tile, f32), pltpu.HBM((groups,) + tile, f32)
    tile_shape = pltpu.HBM(tile, f32)
    token_shape = pltpu.HBM((span, features), bf16)

    arrived = []

    def noted(array):
        arrived.append(array)
        return array

    def run(body, grid, in_specs, out_specs, out_shape, args, after=None, name=None, **sizes):
        if after is not None:
            in_specs, args = in_specs + [FREE], args + (after,)
        args = [
            arg
            if spec is SMEM or any(arg is item for item in arrived)
            else far(arg)
            for spec, arg in zip(in_specs, args)
        ]
        return call(
            functools.partial(body, length=length, **sizes), grid, in_specs, out_specs, out_shape,
            args, name=name,
        )

    def updates(left, right, where, reverse, after=None):
        return run(
            update_kernel, (2,), [SMEM, SMEM, head_cols, head_cols], [pair_tiles, pair_tiles],
            [pair_kept, pair_sent], (where, exps, left, right), after,
            reverse=reverse, name="updates",
        )

    def chip(mine, other, reverse, after=None):
        return run(
            chip_kernel, (2,), [SMEM, SMEM, pair_tiles, pair_tiles], [line_tile, line_tile],
            [line_kept, line_sent], (here, exps, mine, other), after,
            reverse=reverse, span=float(span), name="chip",
        )

    def core_state(edges, mine, other, where, reverse, after=None):
        specs = [pair_tiles] if len(edges) == 1 else [line_tile, line_tile]
        return run(
            core_state_kernel, (2,), [SMEM, SMEM, pair_tiles, pair_tiles] + specs,
            [pair_tiles, pair_tiles], [pair_kept, pair_sent],
            (where, exps, mine, other, *edges), after,
            reverse=reverse, count=len(edges), span=float(span), name="core_state",
        )

    inner_shape = pltpu.HBM((span, features), f32)
    even = here * jnp.array([1, 0, 1], jnp.int32)
    r_mine, sent = updates(query, grad, even, True)
    r_other = noted(swap(sent, "core"))
    r_pair = run(
        pair_kernel, (2,), [SMEM, SMEM, pair_tiles, pair_tiles], pair_tiles, pair_sent,
        (here, exps, r_mine, r_other), span=float(span), name="pair",
    )
    f_mine, sent = updates(key, value, here, False, r_mine)
    f_other = noted(swap(sent, "core"))
    r_parts = exchange(r_pair.reshape((2 * groups,) + tile), CHIPS)
    r_parts = noted(r_parts.reshape((groups, 2) + tile))
    f_chip, sent = chip(f_mine, f_other, False, r_pair)
    f_next = noted(swap(sent, "xl"))
    all_pairs = pl.BlockSpec((groups, 2) + tile, lambda i: (0, 0, 0, 0))
    r_edges, state_grad = run(
        scan_kernel, (1,), [SMEM, all_pairs], [all_pairs, single], [pair_sent, tile_shape],
        (decay_exp, r_parts), f_chip, span=2.0 * span, name="scan",
    )
    quarter = pl.BlockSpec((4,) + tile, lambda i: (0, 0, 0))
    quarter_shape = pltpu.HBM((4,) + tile, f32)
    f_line, sent = run(
        line_kernel, (1,), [SMEM, SMEM, line, line], [quarter, quarter],
        [quarter_shape, quarter_shape], (here, exps, f_chip, f_next), r_edges,
        span=2.0 * span, name="line",
    )
    f_beside = noted(swap(sent, "zl"))
    inner_gk, inner_gv = run(
        inner_kernel, (2,), [SMEM] + 4 * [head_cols], 2 * [head_cols], 2 * [inner_shape],
        (exps, query, key, value, grad), r_edges, name="inner",
    )
    r_edges = exchange(r_edges.reshape((2 * groups,) + tile), CHIPS)
    r_edges = noted(r_edges.reshape((groups, 2) + tile))
    mine, sent = core_state([r_edges], r_mine, r_other, even, True, inner_gk)
    other = noted(swap(sent, "core"))
    grad_key, grad_value, send = run(
        key_value_kernel, (2,), [SMEM, SMEM] + 4 * [head_cols] + 2 * [pair_tiles],
        [head_cols, head_cols, pl.BlockSpec((8, 4, span, WIDTH), lambda i: (0, 0, 0, i))],
        [token_shape, token_shape, pltpu.HBM((8, 4, span, 2 * WIDTH), bf16)],
        (even, exps, key, value, inner_gk, inner_gv, mine, other), f_line, name="key_value",
    )
    cols = exchange(send.reshape(32, span, 2 * WIDTH), PLANE)
    cols = cols.reshape(32 * span, 2 * WIDTH)

    f_lines = run(
        line_pair_kernel, (1,), [SMEM, SMEM, quarter, quarter, single],
        pl.BlockSpec((5,) + tile, lambda i: (0, 0, 0)), pltpu.HBM((5,) + tile, f32),
        (here, exps, f_line, f_beside, state_in[0, 0]), send, span=4.0 * span,
        name="line_pair",
    )
    f_parts = lax.all_gather(f_lines, "zh")
    tokens, width = rows.shape
    block = width // 4
    partial = call(
        weight_kernel, (4,),
        [
            pl.BlockSpec((tokens, 2 * WIDTH), lambda i: (0, 0)),
            pl.BlockSpec((tokens, block), lambda i: (0, i)),
        ],
        pl.BlockSpec((8, 2, block // 8, WIDTH), lambda i: (0, i, 0, 0)),
        pltpu.HBM((8, 8, block // 8, WIDTH), bf16), (cols, far(rows)), scratch=[pltpu.VMEM((2 * WIDTH, tokens), bf16)], name="weight", vmem=40,
    )
    f_edge, f_sent = run(
        edge_kernel, (1,),
        [SMEM, SMEM, pl.BlockSpec((4, 5) + tile, lambda i: (0, 0, 0, 0)), quarter, quarter],
        [quarter, quarter], [quarter_shape, quarter_shape],
        (here, exps, f_parts, f_line, f_beside), partial, span=4.0 * span, name="edge",
    )
    f_side = noted(swap(f_sent, "zl"))
    f_edge, sent = run(
        chip_state_kernel, (1,), [SMEM, SMEM, quarter, quarter, line, line], [line, line],
        [line_kept, line_sent], (here, exps, f_edge, f_side, f_chip, f_next),
        span=2.0 * span, name="chip_state",
    )
    partial, sent = lax.optimization_barrier((partial, sent))
    f_far = noted(swap(sent, "xl"))
    mine, sent = core_state([f_edge, f_far], f_mine, f_other, here, False)
    other = noted(swap(sent, "core"))
    grad_query = run(
        query_kernel, (2,), [SMEM, SMEM] + 3 * [head_cols] + 2 * [pair_tiles], head_cols,
        token_shape, (here, exps, key, value, grad, mine, other), name="query",
    )
    share = block // 8
    pieces = exchange(partial.reshape(64, share, WIDTH), OWNERS).reshape(8, 8, share, WIDTH)
    weight_grads = call(
        total_kernel, (2,), [pl.BlockSpec((4, 8, share, WIDTH), lambda i: (i, 0, 0, 0))],
        pl.BlockSpec((1, 1, share, 4 * WIDTH), lambda i: (i, 0, 0, 0)),
        pltpu.HBM((2, 1, share, 4 * WIDTH), f32), (pieces,), name="total",
    )
    return (
        grad_query[None], grad_key[None], grad_value[None], weight_grads, state_grad[None, None]
    )


def solution(mesh):
    fine = Mesh(mesh.devices.reshape(4, 2, 4, 2, 2, 2), ("y", "xh", "zh", "zl", "xl", "core"))
    dp, seq = ("y", "xh"), CHAIN
    tokens = P(dp, seq, None)
    in_specs = (tokens, tokens, tokens, tokens, tokens, P(seq), P(dp, seq, None, None))
    out_specs = (tokens, tokens, tokens, P(None, seq, dp, None), P(dp, seq, None, None))
    return jax.shard_map(
        per_device, mesh=fine, in_specs=in_specs, out_specs=out_specs, check_vma=False
    )
```

```python
import functools

import jax
import jax.numpy as jnp
from jax import lax
from jax.experimental import pallas as pl
from jax.experimental.pallas import tpu as pltpu
from jax.sharding import Mesh
from jax.sharding import PartitionSpec as P

WIDTH = 128
f32 = jnp.float32
bf16 = jnp.bfloat16
PLANE = ("y", "xh", "xl", "core")
QUAD = ("xl", "core")
LINE = ("zh", "zl")
CHIPS = ("zh", "zl", "xl")
CHAIN = ("zh", "zl", "xl", "core")
OWNERS = ("y", "xh", "zh", "zl")


def log_rate(exponent, length):
    return -(jnp.left_shift(1, exponent).astype(f32)) * (1.0 / length)


def power_of(rate, steps):
    return jnp.exp(jnp.full((1, WIDTH), rate * steps, f32))


def halves(wide):
    high = wide.astype(bf16)
    return high, (wide - high.astype(f32)).astype(bf16)


def dot(left, right, dims):
    return lax.dot_general(left, right, (dims, ((), ())), preferred_element_type=f32)


def groups_of(ref):
    count = ref.shape[0]
    return [(item, pl.program_id(0) * count + item) for item in range(count)]


def update_kernel(here_ref, exp_ref, left_ref, right_ref, *refs, reverse, length):
    keep_ref, send_ref = refs[-2:]
    span = left_ref.shape[0]
    rows = lax.broadcasted_iota(jnp.int32, (span, WIDTH), 0).astype(f32)
    steps = rows if reverse else (span - 1.0) - rows
    for item, group in groups_of(keep_ref):
        for core, out_ref in enumerate((keep_ref, send_ref)):
            for chip in range(2):
                slot = 2 * jnp.bitwise_xor(here_ref[1], chip) + jnp.bitwise_xor(here_ref[2], core)
                rate = log_rate(exp_ref[4 * group + slot], length)
                start = pl.multiple_of((4 * item + slot) * WIDTH, WIDTH)
                lanes = pl.ds(start, WIDTH)
                high, low = halves(left_ref[:, lanes].astype(f32) * jnp.exp(rate * steps))
                right = right_ref[:, lanes]
                out_ref[item, chip] = dot(
                    jnp.concatenate((high, low), 0), jnp.concatenate((right, right), 0),
                    ((0,), (0,)),
                )


def weighed(mine, other, position, reverse, rate, span):
    position = position.astype(f32)
    later = position if reverse else 1.0 - position
    return power_of(rate, span * later) * mine + power_of(rate, span * (1.0 - later)) * other


def chip_kernel(here_ref, exp_ref, mine_ref, other_ref, *refs, reverse, length, span):
    keep_ref, send_ref = refs[-2:]
    for item, group in groups_of(keep_ref):
        for chip, out_ref in enumerate((keep_ref, send_ref)):
            head = 4 * group + 2 * jnp.bitwise_xor(here_ref[1], chip) + here_ref[2]
            out_ref[item] = weighed(
                mine_ref[item, chip], other_ref[item, chip], here_ref[2], reverse,
                log_rate(exp_ref[head], length), span,
            )


def pair_kernel(here_ref, exp_ref, mine_ref, other_ref, out_ref, *, length, span):
    for item, group in groups_of(out_ref):
        for chip in range(2):
            rate = log_rate(exp_ref[4 * group + 2 * chip + here_ref[2]], length)
            out_ref[item, chip] = weighed(
                mine_ref[item, chip], other_ref[item, chip], here_ref[2], True, rate, span
            )


def scan_kernel(own_ref, parts_ref, after_ref, out_ref, grad_ref, *, length, span):
    rate = log_rate(own_ref[0], length)
    decay = power_of(rate, span)
    state = jnp.zeros(grad_ref.shape, f32)
    for group in reversed(range(parts_ref.shape[0])):
        for chip in (1, 0):
            out_ref[group, chip] = state
            state = decay * state + parts_ref[group, chip]
    grad_ref[...] = power_of(rate, 1.0) * state


def line_kernel(
    here_ref, exp_ref, mine_ref, other_ref, after_ref, keep_ref, send_ref, *, length, span
):
    parity = here_ref[0] % 2
    for half, out_ref in enumerate((keep_ref, send_ref)):
        for item in range(out_ref.shape[0]):
            group = 2 * item + jnp.bitwise_xor(parity, half)
            rate = log_rate(exp_ref[4 * group + 2 * here_ref[1] + here_ref[2]], length)
            out_ref[item] = weighed(
                mine_ref[group], other_ref[group], here_ref[1], False, rate, span
            )


def own_rate(here_ref, exp_ref, item, length):
    group = 2 * item + here_ref[0] % 2
    return log_rate(exp_ref[4 * group + 2 * here_ref[1] + here_ref[2]], length)


def line_pair_kernel(
    here_ref, exp_ref, mine_ref, other_ref, first_ref, *refs, length, span
):
    out_ref = refs[-1]
    count = mine_ref.shape[0]
    for item in range(count):
        rate = own_rate(here_ref, exp_ref, item, length)
        out_ref[item] = weighed(
            mine_ref[item], other_ref[item], here_ref[0] % 2, False, rate, span
        )
    out_ref[count] = first_ref[...]


def edge_kernel(
    here_ref, exp_ref, parts_ref, mine_ref, other_ref, after_ref, keep_ref, send_ref,
    *, length, span
):
    count = mine_ref.shape[0]
    behind = here_ref[0] % 2 == 1
    for item in range(count):
        rate = own_rate(here_ref, exp_ref, item, length)
        decay = power_of(rate, 2.0 * span)
        state = parts_ref[item, count]
        for before in range(count - 1):
            update = decay * state + parts_ref[before, item]
            state = jnp.where(here_ref[0] // 2 > before, update, state)
        past = power_of(rate, span) * state
        keep_ref[item] = jnp.where(behind, past + other_ref[item], state)
        send_ref[item] = jnp.where(behind, state, past + mine_ref[item])


def chip_state_kernel(
    here_ref, exp_ref, mine_edge_ref, other_edge_ref, mine_ref, other_ref, keep_ref, send_ref,
    *, length, span
):
    behind = here_ref[1] == 1
    for group in range(keep_ref.shape[0]):
        rate = log_rate(exp_ref[4 * group + 2 * here_ref[1] + here_ref[2]], length)
        edge = jnp.where(
            here_ref[0] % 2 == group % 2, mine_edge_ref[group // 2], other_edge_ref[group // 2]
        )
        past = power_of(rate, span) * edge
        keep_ref[group] = jnp.where(behind, past + other_ref[group], edge)
        send_ref[group] = jnp.where(behind, edge, past + mine_ref[group])


def core_state_kernel(here_ref, exp_ref, mine_ref, other_ref, *refs, reverse, count, length, span):
    edge_refs, (keep_ref, send_ref) = refs[:count], refs[-2:]
    behind = here_ref[2] == (0 if reverse else 1)
    for item, group in groups_of(keep_ref):
        for chip in range(2):
            head = 4 * group + 2 * jnp.bitwise_xor(here_ref[1], chip) + here_ref[2]
            rate = log_rate(exp_ref[head], length)
            edge = edge_refs[0][item, chip] if count == 1 else edge_refs[chip][item]
            past = power_of(rate, span) * edge
            keep_ref[item, chip] = jnp.where(behind, past + other_ref[item, chip], edge)
            send_ref[item, chip] = jnp.where(behind, edge, past + mine_ref[item, chip])


def picked(here_ref, mine_ref, other_ref, item, slot):
    chip = jnp.bitwise_xor(here_ref[1], slot // 2)
    return jnp.where(here_ref[2] == slot % 2, mine_ref[item, chip], other_ref[item, chip])


def heads_of(ref):
    count = ref.shape[1] // (4 * WIDTH)
    first = pl.program_id(0) * count
    return [
        (item, slot, 4 * (first + item) + slot, pl.ds((4 * item + slot) * WIDTH, WIDTH))
        for item in range(count)
        for slot in range(4)
    ]


def inner_kernel(
    exp_ref, query_ref, key_ref, value_ref, grad_ref, next_ref, after_ref, gk_ref, gv_ref,
    *, length
):
    span = query_ref.shape[0]
    source = lax.broadcasted_iota(jnp.int32, (span, span), 0)
    target = lax.broadcasted_iota(jnp.int32, (span, span), 1)
    gap = (target - source).astype(f32)
    for item, slot, head, lanes in heads_of(query_ref):
        rate = log_rate(exp_ref[head], length)
        query, key = query_ref[:, lanes], key_ref[:, lanes]
        value, grad = value_ref[:, lanes], grad_ref[:, lanes]
        mask = jnp.where(gap >= 0.0, jnp.exp(rate * jnp.maximum(gap, 0.0)), 0.0)
        grad_scores = jnp.concatenate(halves(dot(value, grad, ((1,), (1,))) * mask), 1)
        key_scores = jnp.concatenate(halves(dot(key, query, ((1,), (1,))) * mask), 1)
        gk_ref[:, lanes] = dot(grad_scores, jnp.concatenate((query, query), 0), ((1,), (0,)))
        gv_ref[:, lanes] = dot(key_scores, jnp.concatenate((grad, grad), 0), ((1,), (0,)))


def key_value_kernel(
    here_ref, exp_ref, key_ref, value_ref, inner_gk_ref, inner_gv_ref, mine_ref, other_ref,
    after_ref, gk_ref, gv_ref, send_ref, *, length
):
    span = key_ref.shape[0]
    left = span - lax.broadcasted_iota(jnp.int32, (span, WIDTH), 0).astype(f32)
    for item, slot, head, lanes in heads_of(key_ref):
        rate = log_rate(exp_ref[head], length)
        key, value = key_ref[:, lanes], value_ref[:, lanes]
        tail = jnp.exp(rate * left)
        high, low = halves(picked(here_ref, mine_ref, other_ref, item, slot))
        gk = inner_gk_ref[:, lanes] + tail * dot(
            jnp.concatenate((value, value), 1), jnp.concatenate((high, low), 1), ((1,), (1,))
        )
        gv = inner_gv_ref[:, lanes] + tail * dot(
            jnp.concatenate((key, key), 1), jnp.concatenate((high, low), 0), ((1,), (0,))
        )
        gk_ref[:, lanes] = gk.astype(bf16)
        gv_ref[:, lanes] = gv.astype(bf16)
        send_ref[slot, item] = gk.astype(bf16)
        send_ref[4 + slot, item] = gv.astype(bf16)


def query_kernel(
    here_ref, exp_ref, key_ref, value_ref, grad_ref, mine_ref, other_ref, gq_ref, *, length
):
    span = key_ref.shape[0]
    target = lax.broadcasted_iota(jnp.int32, (span, span), 0)
    source = lax.broadcasted_iota(jnp.int32, (span, span), 1)
    gap = (target - source).astype(f32)
    done = 1.0 + lax.broadcasted_iota(jnp.int32, (span, WIDTH), 0).astype(f32)
    for item, slot, head, lanes in heads_of(key_ref):
        rate = log_rate(exp_ref[head], length)
        key, value, grad = key_ref[:, lanes], value_ref[:, lanes], grad_ref[:, lanes]
        mask = jnp.where(gap >= 0.0, jnp.exp(rate * jnp.maximum(gap, 0.0)), 0.0)
        scores = jnp.concatenate(halves(dot(grad, value, ((1,), (1,))) * mask), 1)
        high, low = halves(picked(here_ref, mine_ref, other_ref, item, slot))
        gq = jnp.exp(rate * done) * dot(
            jnp.concatenate((grad, grad), 1), jnp.concatenate((high, low), 1), ((1,), (1,))
        )
        gq = gq + dot(scores, jnp.concatenate((key, key), 0), ((1,), (0,)))
        gq_ref[:, lanes] = gq.astype(bf16)


def weight_kernel(cols_ref, rows_ref, out_ref, turned):
    @pl.when(pl.program_id(0) == 0)
    def _():
        turned[...] = cols_ref[...].T

    product = dot(turned[...], rows_ref[...], ((1,), (0,))).T.astype(bf16)
    count = out_ref.shape[2]
    for item in range(out_ref.shape[0]):
        rows = product[item * count : (item + 1) * count]
        out_ref[item, 0] = rows[:, :WIDTH]
        out_ref[item, 1] = rows[:, WIDTH:]


def total_kernel(parts_ref, out_ref):
    for owner in range(parts_ref.shape[0]):
        total = parts_ref[owner, 0].astype(f32)
        for item in range(1, parts_ref.shape[1]):
            total = total + parts_ref[owner, item].astype(f32)
        out_ref[0, 0, :, owner * WIDTH : (owner + 1) * WIDTH] = total


SMEM = pl.BlockSpec(memory_space=pltpu.SMEM)
FREE = pl.BlockSpec(memory_space=pl.ANY)


def exchange(array, axes):
    return lax.all_to_all(array, axes, split_axis=0, concat_axis=0, tiled=True)


def swap(array, axis):
    return lax.ppermute(array, axis, [(0, 1), (1, 0)])


def far(array):
    return pltpu.with_memory_space_constraint(array, pltpu.HBM)


def call(kernel, grid, in_specs, out_specs, out_shape, args, scratch=(), name=None, vmem=24):
    return pl.pallas_call(
        kernel,
        grid=grid,
        in_specs=in_specs,
        out_specs=out_specs,
        out_shape=out_shape,
        scratch_shapes=scratch,
        name=name,
        compiler_params=pltpu.CompilerParams(vmem_limit_bytes=vmem * 1024 * 1024),
    )(*args)


def per_device(inputs_x, queries, keys, values, grad_out, decay_exp, state_in):
    span = queries.shape[1]
    features = queries.shape[2]
    groups = features // (4 * WIDTH)
    length = span * lax.axis_size(CHAIN)
    tile = (WIDTH, WIDTH)
    query, key, value, grad = queries[0], keys[0], values[0], grad_out[0]
    exps = lax.all_gather(decay_exp, CHAIN, axis=0, tiled=True)
    here = jnp.stack([lax.axis_index(axis) for axis in (LINE, "xl", "core")]).astype(jnp.int32)
    rows = lax.all_gather(inputs_x[0], PLANE, axis=0, tiled=True)

    head_cols = pl.BlockSpec((span, features // 2), lambda i: (0, i))
    pair_tiles = pl.BlockSpec((groups // 2, 2) + tile, lambda i: (i, 0, 0, 0))
    line_tile = pl.BlockSpec((groups // 2,) + tile, lambda i: (i, 0, 0))
    line = pl.BlockSpec((groups,) + tile, lambda i: (0, 0, 0))
    single = pl.BlockSpec(tile, lambda i: (0, 0))
    pair_kept, pair_sent = pltpu.HBM((groups, 2) + tile, f32), pltpu.HBM((groups, 2) + tile, f32)
    line_kept, line_sent = pltpu.HBM((groups,) + tile, f32), pltpu.HBM((groups,) + tile, f32)
    tile_shape = pltpu.HBM(tile, f32)
    token_shape = pltpu.HBM((span, features), bf16)

    arrived = []

    def noted(array):
        arrived.append(array)
        return array

    def run(body, grid, in_specs, out_specs, out_shape, args, after=None, name=None, **sizes):
        if after is not None:
            in_specs, args = in_specs + [FREE], args + (after,)
        args = [
            arg
            if spec is SMEM or any(arg is item for item in arrived)
            else far(arg)
            for spec, arg in zip(in_specs, args)
        ]
        return call(
            functools.partial(body, length=length, **sizes), grid, in_specs, out_specs, out_shape,
            args, name=name,
        )

    def updates(left, right, where, reverse, after=None):
        return run(
            update_kernel, (2,), [SMEM, SMEM, head_cols, head_cols], [pair_tiles, pair_tiles],
            [pair_kept, pair_sent], (where, exps, left, right), after,
            reverse=reverse, name="updates",
        )

    def chip(mine, other, reverse, after=None):
        return run(
            chip_kernel, (2,), [SMEM, SMEM, pair_tiles, pair_tiles], [line_tile, line_tile],
            [line_kept, line_sent], (here, exps, mine, other), after,
            reverse=reverse, span=float(span), name="chip",
        )

    def core_state(edges, mine, other, where, reverse, after=None):
        specs = [pair_tiles] if len(edges) == 1 else [line_tile, line_tile]
        return run(
            core_state_kernel, (2,), [SMEM, SMEM, pair_tiles, pair_tiles] + specs,
            [pair_tiles, pair_tiles], [pair_kept, pair_sent],
            (where, exps, mine, other, *edges), after,
            reverse=reverse, count=len(edges), span=float(span), name="core_state",
        )

    inner_shape = pltpu.HBM((span, features), f32)
    even = here * jnp.array([1, 0, 1], jnp.int32)
    r_mine, sent = updates(query, grad, even, True)
    r_other = noted(swap(sent, "core"))
    r_pair = run(
        pair_kernel, (2,), [SMEM, SMEM, pair_tiles, pair_tiles], pair_tiles, pair_sent,
        (here, exps, r_mine, r_other), span=float(span), name="pair",
    )
    f_mine, sent = updates(key, value, here, False, r_mine)
    f_other = noted(swap(sent, "core"))
    r_parts = exchange(r_pair.reshape((2 * groups,) + tile), CHIPS)
    r_parts = noted(r_parts.reshape((groups, 2) + tile))
    f_chip, sent = chip(f_mine, f_other, False, r_pair)
    f_next = noted(swap(sent, "xl"))
    all_pairs = pl.BlockSpec((groups, 2) + tile, lambda i: (0, 0, 0, 0))
    r_edges, state_grad = run(
        scan_kernel, (1,), [SMEM, all_pairs], [all_pairs, single], [pair_sent, tile_shape],
        (decay_exp, r_parts), f_chip, span=2.0 * span, name="scan",
    )
    quarter = pl.BlockSpec((4,) + tile, lambda i: (0, 0, 0))
    quarter_shape = pltpu.HBM((4,) + tile, f32)
    f_line, sent = run(
        line_kernel, (1,), [SMEM, SMEM, line, line], [quarter, quarter],
        [quarter_shape, quarter_shape], (here, exps, f_chip, f_next), r_edges,
        span=2.0 * span, name="line",
    )
    f_beside = noted(swap(sent, "zl"))
    inner_gk, inner_gv = run(
        inner_kernel, (2,), [SMEM] + 4 * [head_cols] + [FREE], 2 * [head_cols],
        2 * [inner_shape],
        (exps, query, key, value, grad, f_next), r_edges, name="inner",
    )
    r_edges = exchange(r_edges.reshape((2 * groups,) + tile), CHIPS)
    r_edges = noted(r_edges.reshape((groups, 2) + tile))
    mine, sent = core_state([r_edges], r_mine, r_other, even, True, inner_gk)
    other = noted(swap(sent, "core"))
    grad_key, grad_value, send = run(
        key_value_kernel, (2,), [SMEM, SMEM] + 4 * [head_cols] + 2 * [pair_tiles],
        [head_cols, head_cols, pl.BlockSpec((8, 4, span, WIDTH), lambda i: (0, 0, 0, i))],
        [token_shape, token_shape, pltpu.HBM((8, 4, span, 2 * WIDTH), bf16)],
        (even, exps, key, value, inner_gk, inner_gv, mine, other), f_line, name="key_value",
    )
    cols = exchange(send.reshape(32, span, 2 * WIDTH), PLANE)
    cols = cols.reshape(32 * span, 2 * WIDTH)

    f_lines = run(
        line_pair_kernel, (1,), [SMEM, SMEM, quarter, quarter, single],
        pl.BlockSpec((5,) + tile, lambda i: (0, 0, 0)), pltpu.HBM((5,) + tile, f32),
        (here, exps, f_line, f_beside, state_in[0, 0]), send, span=4.0 * span,
        name="line_pair",
    )
    f_parts = lax.all_gather(f_lines, "zh")
    tokens, width = rows.shape
    block = width // 4
    partial = call(
        weight_kernel, (4,),
        [
            pl.BlockSpec((tokens, 2 * WIDTH), lambda i: (0, 0)),
            pl.BlockSpec((tokens, block), lambda i: (0, i)),
        ],
        pl.BlockSpec((8, 2, block // 8, WIDTH), lambda i: (0, i, 0, 0)),
        pltpu.HBM((8, 8, block // 8, WIDTH), bf16), (cols, far(rows)), scratch=[pltpu.VMEM((2 * WIDTH, tokens), bf16)], name="weight", vmem=40,
    )
    f_edge, f_sent = run(
        edge_kernel, (1,),
        [SMEM, SMEM, pl.BlockSpec((4, 5) + tile, lambda i: (0, 0, 0, 0)), quarter, quarter],
        [quarter, quarter], [quarter_shape, quarter_shape],
        (here, exps, f_parts, f_line, f_beside), partial, span=4.0 * span, name="edge",
    )
    f_side = noted(swap(f_sent, "zl"))
    f_edge, sent = run(
        chip_state_kernel, (1,), [SMEM, SMEM, quarter, quarter, line, line], [line, line],
        [line_kept, line_sent], (here, exps, f_edge, f_side, f_chip, f_next),
        span=2.0 * span, name="chip_state",
    )
    partial, sent = lax.optimization_barrier((partial, sent))
    f_far = noted(swap(sent, "xl"))
    mine, sent = core_state([f_edge, f_far], f_mine, f_other, here, False)
    other = noted(swap(sent, "core"))
    grad_query = run(
        query_kernel, (2,), [SMEM, SMEM] + 3 * [head_cols] + 2 * [pair_tiles], head_cols,
        token_shape, (here, exps, key, value, grad, mine, other), name="query",
    )
    share = block // 8
    pieces = exchange(partial.reshape(64, share, WIDTH), OWNERS).reshape(8, 8, share, WIDTH)
    weight_grads = call(
        total_kernel, (2,), [pl.BlockSpec((4, 8, share, WIDTH), lambda i: (i, 0, 0, 0))],
        pl.BlockSpec((1, 1, share, 4 * WIDTH), lambda i: (i, 0, 0, 0)),
        pltpu.HBM((2, 1, share, 4 * WIDTH), f32), (pieces,), name="total",
    )
    return (
        grad_query[None], grad_key[None], grad_value[None], weight_grads, state_grad[None, None]
    )


def solution(mesh):
    fine = Mesh(mesh.devices.reshape(4, 2, 4, 2, 2, 2), ("y", "xh", "zh", "zl", "xl", "core"))
    dp, seq = ("y", "xh"), CHAIN
    tokens = P(dp, seq, None)
    in_specs = (tokens, tokens, tokens, tokens, tokens, P(seq), P(dp, seq, None, None))
    out_specs = (tokens, tokens, tokens, P(None, seq, dp, None), P(dp, seq, None, None))
    return jax.shard_map(
        per_device, mesh=fine, in_specs=in_specs, out_specs=out_specs, check_vma=False
    )
```
